32 devices in a mesh: dp: 16 (over z, y, core), tensor: 2 (over x).
Axes of the slice: x: 2, y: 2, z: 4, core: 2. Of those that a mesh axis runs over, the one named last changes fastest.
Arguments:
- block_input: bfloat16 [32768, 768], P(('dp', 'tensor')), may hold values from -15 to 15
- cotangent: bfloat16 [32768, 768], P(('dp', 'tensor')), may hold values from -6 to 6
- w_qkv: bfloat16 [768, 3, 768], P('dp', None, 'tensor'), may hold values from -0.21875 to 0.21875
- w_out: bfloat16 [768, 768], P('tensor', 'dp'), may hold values from -0.875 to 0.875
- w_up: bfloat16 [768, 3072], P('dp', 'tensor'), may hold values from -0.21875 to 0.21875
- w_down: bfloat16 [3072, 768], P('tensor', 'dp'), may hold values from -0.109375 to 0.109375
- w_mod: bfloat16 [768, 4608], P(None, ('dp', 'tensor')), may hold values from -0.21875 to 0.21875
- time_table: bfloat16 [256, 768], P(('dp', 'tensor')), may hold values from -5 to 5
- prompt_len: int32 [16], P('dp'), may hold values from 512 to 1024, as said below
- cont_len: int32 [16, 8], P('dp'), may hold values from 64 to 128, as said below
- timestep: int32 [16, 9], P('dp'), may hold values from 0 to 255
Outputs:
- block_output: bfloat16 [32768, 768], P(('dp', 'tensor'))
- input_grad: float32 [32768, 768], P(('dp', 'tensor'))
- qkv_grad: float32 [768, 3, 768], P('dp', None, 'tensor')
- out_grad: float32 [768, 768], P('tensor', 'dp')
- up_grad: float32 [768, 3072], P('dp', 'tensor')
- down_grad: float32 [3072, 768], P('tensor', 'dp')
- mod_grad: float32 [768, 4608], P(None, ('dp', 'tensor'))
- table_grad: float32 [256, 768], P(('dp', 'tensor'))
- stats: float32 [3], replicated
The draws below stay inside these ranges and needn't reach their ends.
Inputs may be any that keep to these rules, and one draw needn't show every extreme that they name: `prompt_len`: some group has exactly 1024 valid prompt tokens and some 1024 // 2. `cont_len`: some continuation has exactly 128 valid tokens and some 128 // 2.
All inputs are finite; a program needn't handle non-finite values.
Results may differ from the reference program's by a relative error of at most 0.01575.
The reference program's roundings to bfloat16 on the way count: a program that leaves them out, or rounds other values in their place, can miss the bound.
Values may be sent and summed in bfloat16 or wider, within the bound.
No kernel may reach another device: no remote copies, remote signals or barrier semaphores. Data moves between devices by JAX's collectives and lax.ppermute only.
A program may use at most 320 MiB of HBM per device.

```python
import jax
import jax.numpy as jnp
from jax import lax

D = 768
HEADS = 12
HEAD_DIM = 64
FF = 3072
PROMPT = 1024
CONT = 128
NCONT = 8
STEPS = 256
QBLOCK = 512
GRP_TOK = 2048
GROUPS = 16
TOKENS = 32768


def draw_block_input(key, part):
    first_key = jax.random.fold_in(key, 0)
    member = jnp.arange(TOKENS) // GRP_TOK
    rising = 1.0 + 2.0 * member.astype(jnp.float32) / max(GROUPS - 1, 1)
    base = jnp.clip(jax.random.normal(first_key, (TOKENS, D), jnp.float32), -5.0, 5.0)
    return (base * rising[:, None]).astype(jnp.bfloat16)


def forced_counts(key, count, lowest, highest):
    first_key, second_key = jax.random.split(key)
    values = jax.random.randint(first_key, (count,), lowest, highest + 1)
    order = jax.random.permutation(second_key, count)
    values = values.at[order[0]].set(highest)
    values = values.at[order[1]].set(lowest)
    return values.astype(jnp.int32)


def draw_prompt_len(key, part):
    return forced_counts(jax.random.fold_in(key, 11), GROUPS, PROMPT // 2, PROMPT)


def draw_cont_len(key, part):
    return forced_counts(jax.random.fold_in(key, 12), GROUPS * NCONT, CONT // 2, CONT).reshape(GROUPS, NCONT)


def draw_timestep(key, part):
    return forced_counts(jax.random.fold_in(key, 13), GROUPS * (NCONT + 1), 0, STEPS - 1).reshape(GROUPS, NCONT + 1)


def block_scale(rng, dims, cuts, smallest, high):
    loudness = 1.0
    for dim, blocks in cuts:
        steps = jax.random.uniform(jax.random.fold_in(jax.random.fold_in(rng, 6), dim), (blocks,), jnp.float32, smallest / len(cuts), high / len(cuts))
        loudness = loudness * jnp.repeat(jnp.exp(steps), dims[dim] // blocks).reshape((-1,) + (1,) * (len(dims) - 1 - dim))
    return loudness


def scatter_about(stream_key, extent, scale, reach, cuts=(), kind=jnp.bfloat16):
    values = scale * jax.random.normal(stream_key, extent, jnp.float32)
    if cuts:
        values = values * block_scale(stream_key, extent, cuts, -0.22, 0.18)
    return jnp.clip(values, -reach, reach).astype(kind)


def setup_inputs(seed: int = 0) -> dict:
    arg_keys = jax.random.split(jax.random.key(seed), 12)
    block_input = draw_block_input(jax.random.fold_in(arg_keys[11], 71), 0)
    cotangent = scatter_about(arg_keys[1], (TOKENS, D), 1.0, 6.0, ((0, 32),))
    w_qkv = scatter_about(arg_keys[2], (D, 3, D), D ** -0.5, 0.21875, ((0, 16), (2, 2)))
    w_out = scatter_about(arg_keys[3], (D, D), (D // 16) ** -0.5, 0.875, ((0, 2), (1, 16)))
    w_up = scatter_about(arg_keys[4], (D, FF), D ** -0.5, 0.21875, ((0, 16), (1, 2)))
    w_down = scatter_about(arg_keys[5], (FF, D), FF ** -0.5, 0.109375, ((0, 2), (1, 16)))
    w_mod = scatter_about(arg_keys[6], (D, 6 * D), D ** -0.5, 0.21875, ((1, 32),))
    time_table = scatter_about(arg_keys[7], (STEPS, D), 1.0, 5.0, ((0, 32),))
    prompt_len = draw_prompt_len(jax.random.fold_in(arg_keys[11], 71), 0)
    cont_len = draw_cont_len(jax.random.fold_in(arg_keys[11], 71), 0)
    timestep = draw_timestep(jax.random.fold_in(arg_keys[11], 71), 0)
    return dict(block_input=block_input, cotangent=cotangent, w_qkv=w_qkv, w_out=w_out, w_up=w_up, w_down=w_down, w_mod=w_mod, time_table=time_table, prompt_len=prompt_len, cont_len=cont_len, timestep=timestep)


precise = lax.Precision.HIGHEST
masked_score = -1e+30

@jax.custom_vjp
def low(v):
    return lax.optimization_barrier(v.astype(jnp.bfloat16)).astype(jnp.float32)

@jax.custom_vjp
def low_back(v):
    return v

def low_keep(v):
    return (low(v), None)

def low_pass(kept, grad):
    return (grad,)

def back_keep(v):
    return (v, None)

def back_low(kept, grad):
    return (low(grad),)
low.defvjp(low_keep, low_pass)
low_back.defvjp(back_keep, back_low)

def norm_modulate(inputs, shifts, scales):
    average = lax.optimization_barrier(jnp.mean(inputs, -1, keepdims=True))
    centred = inputs - average
    spread = lax.optimization_barrier(jnp.mean(centred * centred, -1, keepdims=True))
    return centred * lax.rsqrt(spread + 1e-05) * (1.0 + scales) + shifts

def rotate(heads, places):
    half_dim = heads.shape[-1] // 2
    freqs = 10000.0 ** (-jnp.arange(half_dim, dtype=heads.dtype) / half_dim)
    angles = places[:, None] * freqs[None, :]
    cosine = jnp.cos(angles)[:, None, :]
    sine = jnp.sin(angles)[:, None, :]
    first = heads[..., :half_dim]
    second = heads[..., half_dim:]
    return jnp.concatenate([first * cosine - second * sine, second * cosine + first * sine], -1)

def allowed_pairs(query_pos, key_pos, key_valid):
    query_cont = query_pos >= PROMPT
    key_cont = key_pos >= PROMPT
    query_id = jnp.maximum(query_pos - PROMPT, 0) // CONT
    key_id = jnp.maximum(key_pos - PROMPT, 0) // CONT
    earlier = key_pos[None, :] <= query_pos[:, None]
    to_prompt = jnp.logical_not(key_cont)[None, :] & (query_cont[:, None] | earlier)
    to_self = key_cont[None, :] & query_cont[:, None] & (key_id[None, :] == query_id[:, None]) & earlier
    return key_valid[None, :] & (to_prompt | to_self)

def group_layer(w_qkv, w_out, w_up, w_down, inputs, modulate, prompt_count, cont_count):
    inside = jnp.arange(GRP_TOK, dtype=jnp.int32)
    in_cont = inside >= PROMPT
    offset = jnp.maximum(inside - PROMPT, 0)
    cont_id = offset // CONT
    within = offset % CONT
    places = jnp.where(in_cont, prompt_count + within, inside).astype(inputs.dtype)
    valid = jnp.where(in_cont, within < cont_count[cont_id], inside < prompt_count)
    segment = jnp.where(in_cont, 1 + cont_id, 0)
    row_mod = modulate[segment].reshape(GRP_TOK, 6, D)
    normed = low(norm_modulate(inputs, row_mod[:, 0], row_mod[:, 1]))
    joined = low_back(jnp.dot(normed, w_qkv.reshape(D, 3 * D), precision=precise)).reshape(GRP_TOK, 3, HEADS, HEAD_DIM)
    queries = low(rotate(joined[:, 0], places))
    keys_rot = low(rotate(joined[:, 1], places))
    values = low(joined[:, 2])
    scaling = HEAD_DIM ** (-0.5)

    def attend(block_index):
        start = block_index * QBLOCK
        query_blk = lax.dynamic_slice_in_dim(queries, start, QBLOCK, 0)
        query_pos = start + jnp.arange(QBLOCK, dtype=jnp.int32)
        allowed = allowed_pairs(query_pos, inside, valid)
        scores = jnp.einsum('qhd,khd->hqk', query_blk, keys_rot, precision=precise) * scaling
        scores = low_back(jnp.where(allowed[None], scores, masked_score))
        highest = lax.optimization_barrier(jnp.max(scores, -1, keepdims=True))
        exponent = jnp.exp(scores - highest)
        probability = low(exponent / lax.optimization_barrier(jnp.sum(exponent, -1, keepdims=True)))
        return jnp.einsum('hqk,khd->qhd', probability, values, precision=precise)
    blocks = lax.map(jax.checkpoint(attend), jnp.arange(GRP_TOK // QBLOCK, dtype=jnp.int32))
    attended = low_back(low(blocks.reshape(GRP_TOK, D)))
    attn_branch = low_back(jnp.dot(attended, w_out, precision=precise))
    middle = inputs + row_mod[:, 2] * attn_branch
    normed_two = low(norm_modulate(middle, row_mod[:, 3], row_mod[:, 4]))
    pre_act = low_back(jnp.dot(normed_two, w_up, precision=precise))
    hidden = low(jax.nn.gelu(pre_act, approximate=False))
    mlp_branch = low_back(jnp.dot(hidden, w_down, precision=precise))
    result = middle + row_mod[:, 5] * mlp_branch
    weight_valid = valid.astype(inputs.dtype)[:, None]
    attn_part = row_mod[:, 2] * attn_branch
    mlp_part = row_mod[:, 5] * mlp_branch
    sums = jnp.stack([jnp.sum(weight_valid * result * result), jnp.sum(weight_valid * attn_part * attn_part), jnp.sum(weight_valid * mlp_part * mlp_part), jnp.sum(weight_valid) * D])
    return (result, sums)

def reference(block_input, cotangent, w_qkv, w_out, w_up, w_down, w_mod, time_table, prompt_len, cont_len, timestep):
    primals = tuple((source.astype(jnp.float32) for source in (block_input, w_qkv, w_out, w_up, w_down, w_mod, time_table)))
    layer_step = jax.checkpoint(group_layer)

    def forward(inputs, qkv_weight, out_weight, up_weight, down_weight, mod_weight, table):
        condition = table[timestep.reshape(-1)]
        modulate = low_back(jnp.dot(condition, mod_weight, precision=precise)).reshape(GROUPS, NCONT + 1, 6 * D)
        grouped = inputs.reshape(GROUPS, GRP_TOK, D)

        def scan_step(running, item):
            result, sums = layer_step(qkv_weight, out_weight, up_weight, down_weight, item[0], item[1], item[2], item[3])
            return (running + sums, result)
        totals, results = lax.scan(scan_step, jnp.zeros((4,), inputs.dtype), (grouped, modulate, prompt_len, cont_len))
        return (results.reshape(TOKENS, D), totals)
    output, back_fn, totals = jax.vjp(forward, *primals, has_aux=True)
    grads = back_fn(cotangent.astype(jnp.float32))
    stats = jnp.sqrt(totals[:3] / totals[3])
    return (output.astype(jnp.bfloat16), grads[0], grads[1], grads[2], grads[3], grads[4], grads[5], grads[6], stats)
```

```python
import math

import jax
import jax.numpy as jnp
from jax import lax
from jax.experimental import pallas as pl
from jax.experimental.pallas import tpu as pltpu
from jax.sharding import PartitionSpec as P

HEAD_DIM = 64
PROMPT = 1024
CONT = 128
NCONT = 8
STEPS = 256
SEGS = 1 + NCONT

bf16 = jnp.bfloat16
f32 = jnp.float32
NN = (((1,), (0,)), ((), ()))
NT = (((1,), (1,)), ((), ()))
TN = (((0,), (0,)), ((), ()))
SCALE = HEAD_DIM ** (-0.5)
SCALE2 = SCALE * math.log2(math.e)
NEG = -1e30


def dot(left, right, dims=NN):
    return lax.dot_general(left, right, dims, preferred_element_type=f32)


def lanes(shape):
    return lax.broadcasted_iota(jnp.int32, shape, 1)


def rows(shape):
    return lax.broadcasted_iota(jnp.int32, shape, 0)


def swap(x, axis, bit):
    count = lax.axis_size(axis)
    return lax.ppermute(x, axis, [(i, i ^ bit) for i in range(count)])


def dp_bits():
    count = lax.axis_size("dp")
    return [1 << k for k in reversed(range(count.bit_length() - 1))]


def bit_of(index, bit):
    return (index // bit) % 2


def join_halves(own, other, mine, axis):
    low = jnp.where(mine == 0, own, other)
    high = jnp.where(mine == 0, other, own)
    return jnp.stack([low, high], axis)


def gather_weights(piece, swap_first):
    me = lax.axis_index("dp")
    bits = dp_bits()
    cur, other, axis = piece, None, 0
    for bit in bits[:-2]:
        cur = join_halves(cur, swap(cur, "dp", bit), bit_of(me, bit), axis)
        axis += 1
    if swap_first:
        cur = jnp.stack([cur, swap(cur, "tensor", 1)], 0)
        for bit in bits[-2:]:
            cur = join_halves(cur, swap(cur, "dp", bit), bit_of(me, bit), axis + 1)
            axis += 1
    else:
        bit = bits[-2]
        cur = join_halves(cur, swap(cur, "dp", bit), bit_of(me, bit), axis)
        axis += 1
        cur = jnp.stack([cur, swap(cur, "tensor", 1)], 0)
        bit = bits[-1]
        cur = join_halves(cur, swap(cur, "dp", bit), bit_of(me, bit), axis + 1)
    cur = cur.reshape(2, -1, piece.shape[-1])
    return cur[0], cur[1]


def scatter_grads(mine, other, swap_first):
    me = lax.axis_index("dp")
    bits = dp_bits()
    columns = mine.shape[-1]
    cur = jnp.stack([mine, other], 0).astype(bf16)
    cur = cur.reshape((2,) + (2,) * len(bits) + (-1, columns))

    def halve(cur, bit, axis):
        b = bit_of(me, bit)
        keep = lax.dynamic_index_in_dim(cur, b, axis, keepdims=False)
        send = lax.dynamic_index_in_dim(cur, 1 - b, axis, keepdims=False)
        return keep.astype(f32) + swap(send, "dp", bit).astype(f32)

    order = list(reversed(bits))
    cur = halve(cur, order[0], len(bits)).astype(bf16)
    if swap_first:
        cur = (cur[0].astype(f32) + swap(cur[1], "tensor", 1).astype(f32)).astype(bf16)
        cur = halve(cur, order[1], len(bits) - 2).astype(bf16)
    else:
        cur = halve(cur, order[1], len(bits) - 1).astype(bf16)
        cur = (cur[0].astype(f32) + swap(cur[1], "tensor", 1).astype(f32)).astype(bf16)
    axis = len(bits) - 3
    for bit in order[2:]:
        total = halve(cur, bit, axis)
        cur = total.astype(bf16)
        axis -= 1
    return total


def turn(x, cosine, sine):
    lane = lanes(x.shape) % 64
    swapped = jnp.where(lane < 32, -pltpu.roll(x, 96, 1), pltpu.roll(x, 32, 1))
    return x * cosine + swapped * sine


def turn_back(x, cosine, sine):
    lane = lanes(x.shape) % 64
    swapped = jnp.where(lane < 32, pltpu.roll(x, 96, 1), -pltpu.roll(x, 32, 1))
    return x * cosine + swapped * sine


def project_kernel(turned, x_ref, w_ref, cos_ref, sin_ref, out_ref):
    joined = dot(x_ref[...], w_ref[...])
    part = pl.program_id(0)

    @pl.when(part < turned)
    def _():
        for c in range(joined.shape[1] // 128):
            cut = slice(c * 128, (c + 1) * 128)
            out_ref[:, cut] = turn(joined[:, cut], cos_ref[...], sin_ref[...]).astype(bf16)

    @pl.when(part >= turned)
    def _():
        out_ref[...] = joined.astype(bf16)


def project(x, w, cosine, sine, first, turned):
    count, width = x.shape
    head_width = w.shape[1] // 3
    parts = 3 - first
    whole = pl.BlockSpec((count, 128), lambda p: (0, 0))
    return pl.pallas_call(
        lambda *refs: project_kernel(turned, *refs),
        grid=(parts,),
        in_specs=[
            pl.BlockSpec((count, width), lambda p: (0, 0)),
            pl.BlockSpec((width, head_width), lambda p: (0, p + first)),
            whole,
            whole,
        ],
        out_specs=pl.BlockSpec((count, head_width), lambda p: (0, p)),
        out_shape=jax.ShapeDtypeStruct((count, parts * head_width), bf16),
        compiler_params=pltpu.CompilerParams(vmem_limit_bytes=32 * 2**20),
        cost_estimate=pl.CostEstimate(
            flops=2 * count * width * parts * head_width,
            bytes_accessed=2 * (count * width + parts * head_width * (count + width)),
            transcendentals=0,
        ),
        name="project",
    )(x, w, cosine, sine)


def forward_kernel(info, q_ref, kp_ref, vp_ref, ko_ref, vo_ref, o_ref, lse_ref):
    role = info[0]
    prompt_count = info[1]
    count = q_ref.shape[0]
    lane = lanes((count, 128))
    row = rows((count, 128))
    tile = 256
    blocks = count // tile

    def prepare(h):
        sel = (lane // 64) == h
        extra = 64 * (1 - h)
        q = jnp.where(sel, q_ref[...], jnp.where(lane == extra, 1.0, 0.0).astype(bf16))
        bias = jnp.where((lane == extra) & (row >= prompt_count), NEG, 0.0).astype(bf16)
        k = jnp.where(sel, kp_ref[...], bias)
        v = jnp.where(sel, vp_ref[...], jnp.ones((), bf16))
        return sel, q, k, v

    def finish(h, i, o, top):
        extra = 64 * (1 - h)
        weight = o[:, extra : extra + 1]
        lse = top * SCALE2 + jnp.log2(weight)
        turned = jnp.transpose(jnp.broadcast_to(lse, (tile, 128)))
        lse_ref[0, h : h + 1, i * tile : (i + 1) * tile] = turned[0:1, :]
        return o * (1.0 / weight)

    def store(outs):
        for i in range(blocks):
            merged = jnp.where(lanes((tile, 128)) < 64, outs[0][i], outs[1][i])
            o_ref[i * tile : (i + 1) * tile, :] = merged.astype(bf16)

    @pl.when(role == 0)
    def _():
        outs = []
        for h in range(2):
            sel, q, k, v = prepare(h)
            heads = []
            for i in range(blocks):
                start, stop = i * tile, (i + 1) * tile
                s = dot(q[start:stop], k[:stop], NT)
                near = jnp.where(lanes((tile, tile)) <= rows((tile, tile)), s[:, start:], NEG)
                top = jnp.max(near, 1, keepdims=True)
                if i:
                    top = jnp.maximum(top, jnp.max(s[:, :start], 1, keepdims=True))
                o = dot(jnp.exp2(near * SCALE2 - top * SCALE2).astype(bf16), v[start:stop])
                if i:
                    o = o + dot(
                        jnp.exp2(s[:, :start] * SCALE2 - top * SCALE2).astype(bf16), v[:start]
                    )
                heads.append(finish(h, i, o, top))
            outs.append(heads)
        store(outs)

    @pl.when(role != 0)
    def _():
        outs = []
        for h in range(2):
            sel, q, k, v = prepare(h)
            own_k = jnp.where(sel, ko_ref[...], jnp.zeros((), bf16))
            own_v = jnp.where(sel, vo_ref[...], jnp.ones((), bf16))
            heads = []
            for i in range(blocks):
                start, stop = i * tile, (i + 1) * tile
                s = dot(q[start:stop], k, NT)
                cuts = [slice(r, r + CONT) for r in range(start, stop, CONT)]
                near = []
                for cut in cuts:
                    piece = dot(q[cut], own_k[cut], NT)
                    col, line = lanes((CONT, CONT)), rows((CONT, CONT))
                    fine = (col <= line) & (col < info[2 + cut.start // CONT])
                    near.append(jnp.where(fine, piece, NEG))
                near = jnp.concatenate(near, 0)
                top = jnp.maximum(
                    jnp.max(s, 1, keepdims=True), jnp.max(near, 1, keepdims=True)
                )
                far_weight = jnp.exp2(s * SCALE2 - top * SCALE2).astype(bf16)
                near_weight = jnp.exp2(near * SCALE2 - top * SCALE2).astype(bf16)
                own = [
                    dot(near_weight[n * CONT : (n + 1) * CONT], own_v[cut])
                    for n, cut in enumerate(cuts)
                ]
                heads.append(finish(h, i, dot(far_weight, v) + jnp.concatenate(own, 0), top))
            outs.append(heads)
        store(outs)


def attend(info, joined, prompt):
    count = joined.shape[0]
    head_width = joined.shape[1] // 3
    pairs = head_width // 128

    def spec(offset):
        return pl.BlockSpec((count, 128), lambda h, s: (0, offset + h))

    return pl.pallas_call(
        forward_kernel,
        grid_spec=pltpu.PrefetchScalarGridSpec(
            num_scalar_prefetch=1,
            grid=(pairs,),
            in_specs=[spec(0), spec(0), spec(pairs), spec(pairs), spec(2 * pairs)],
            out_specs=[spec(0), pl.BlockSpec((1, 2, count), lambda h, s: (h, 0, 0))],
        ),
        out_shape=[
            jax.ShapeDtypeStruct((count, head_width), bf16),
            jax.ShapeDtypeStruct((pairs, 2, count), f32),
        ],
        compiler_params=pltpu.CompilerParams(vmem_limit_bytes=40 * 2**20),
        cost_estimate=pl.CostEstimate(
            flops=18 * count * count * 128 * pairs * 2,
            bytes_accessed=8 * count * head_width * 2,
            transcendentals=2 * pairs * count * count,
        ),
        name="attend",
    )(info, joined, prompt, prompt, joined, joined)


def backward_kernel(
    info,
    q_ref,
    do_ref,
    o_ref,
    lse_ref,
    kp_ref,
    vp_ref,
    ko_ref,
    vo_ref,
    co_ref,
    so_ref,
    cp_ref,
    sp_ref,
    dq_ref,
    dko_ref,
    dvo_ref,
    dkp_ref,
    dvp_ref,
    dq_acc,
):
    role = info[0]
    prompt_count = info[1]
    count = q_ref.shape[0]
    tile = 256
    lane = lanes((count, 128))
    none = jnp.zeros((), bf16)
    products = jnp.transpose(do_ref[...].astype(f32) * o_ref[...].astype(f32))
    deltas = [jnp.sum(products[64 * h : 64 * h + 64], 0, keepdims=True) for h in range(2)]

    def far_block(j, first):
        start, stop = j * tile, (j + 1) * tile
        cut = slice(start, stop)
        q_from = start if first else 0
        lane_k = lanes((tile, 128))
        row_k = rows((tile, 128)) + start
        key_parts, value_parts = [], []
        for h in range(2):
            extra = 64 * (1 - h)
            sel = (lane_k // 64) == h
            bias = jnp.where((lane_k == extra) & (row_k >= prompt_count), NEG, 0.0).astype(bf16)
            k = jnp.where(sel, kp_ref[cut, :], bias)
            k_plain = jnp.where(sel, kp_ref[cut, :], none)
            v = jnp.where(sel, vp_ref[cut, :], none)
            lane_q = lane[q_from:]
            ones = jnp.where(lane_q == extra, 1.0, 0.0).astype(bf16)
            q = jnp.where((lane_q // 64) == h, q_ref[q_from:, :], ones)
            s = dot(k, q, NT)
            if first:
                near = jnp.where(rows((tile, tile)) <= lanes((tile, tile)), s[:, :tile], NEG)
                s = jnp.concatenate([near, s[:, tile:]], 1) if stop < count else near
            weight = jnp.exp2(s * SCALE2 - lse_ref[0, h : h + 1, q_from:])
            grad = dot(v, do_ref[q_from:, :], NT)
            score = (weight * (grad - deltas[h][:, q_from:])).astype(bf16)
            value_parts.append(dot(weight.astype(bf16), do_ref[q_from:, :]))
            key_parts.append(dot(score, q_ref[q_from:, :]))
            query_part = dot(score, k_plain, TN)
            if j == 0 and h == 0:
                dq_acc[...] = query_part
            else:
                dq_acc[q_from:, :] += query_part
        key_grad = jnp.where(lane_k < 64, key_parts[0], key_parts[1]) * SCALE
        value_grad = jnp.where(lane_k < 64, value_parts[0], value_parts[1])
        dkp_ref[cut, :] = turn_back(key_grad, cp_ref[cut, :], sp_ref[cut, :]).astype(bf16)
        dvp_ref[cut, :] = value_grad.astype(bf16)

    @pl.when(role == 0)
    def _():
        for j in range(count // tile):
            far_block(j, True)
        dko_ref[...] = jnp.zeros_like(dko_ref)
        dvo_ref[...] = jnp.zeros_like(dvo_ref)

    @pl.when(role != 0)
    def _():
        for j in range(count // tile):
            far_block(j, False)
        lane_k = lanes((CONT, CONT))
        row_k = rows((CONT, CONT))
        for i in range(count // CONT):
            cut = slice(i * CONT, (i + 1) * CONT)
            key_parts, value_parts, query_part = [], [], None
            for h in range(2):
                sel = (lane_k // 64) == h
                k = jnp.where(sel, ko_ref[cut, :], none)
                v = jnp.where(sel, vo_ref[cut, :], none)
                fine = (row_k <= lane_k) & (row_k < info[2 + i])
                s = jnp.where(fine, dot(k, q_ref[cut, :], NT), NEG)
                weight = jnp.exp2(s * SCALE2 - lse_ref[0, h : h + 1, cut])
                grad = dot(v, do_ref[cut, :], NT)
                score = (weight * (grad - deltas[h][:, cut])).astype(bf16)
                value_parts.append(dot(weight.astype(bf16), do_ref[cut, :]))
                key_parts.append(dot(score, q_ref[cut, :]))
                part = dot(score, k, TN)
                query_part = part if query_part is None else query_part + part
            dq_acc[cut, :] += query_part
            key_grad = jnp.where(lane_k < 64, key_parts[0], key_parts[1]) * SCALE
            value_grad = jnp.where(lane_k < 64, value_parts[0], value_parts[1])
            dko_ref[cut, :] = turn_back(key_grad, co_ref[cut, :], so_ref[cut, :]).astype(bf16)
            dvo_ref[cut, :] = value_grad.astype(bf16)

    dq_ref[...] = turn_back(dq_acc[...] * SCALE, co_ref[...], so_ref[...]).astype(bf16)


def attend_back(info, joined, prompt, grad, out, lse, tables):
    count = joined.shape[0]
    head_width = joined.shape[1] // 3
    pairs = head_width // 128

    def spec(offset):
        return pl.BlockSpec((count, 128), lambda h, s: (0, offset + h))

    table = pl.BlockSpec((count, 128), lambda h, s: (0, 0))
    return pl.pallas_call(
        backward_kernel,
        grid_spec=pltpu.PrefetchScalarGridSpec(
            num_scalar_prefetch=1,
            grid=(pairs,),
            in_specs=[
                spec(0),
                spec(0),
                spec(0),
                pl.BlockSpec((1, 2, count), lambda h, s: (h, 0, 0)),
                spec(0),
                spec(pairs),
                spec(pairs),
                spec(2 * pairs),
                table,
                table,
                table,
                table,
            ],
            out_specs=[spec(0)] * 5,
            scratch_shapes=[pltpu.VMEM((count, 128), f32)],
        ),
        out_shape=[jax.ShapeDtypeStruct((count, head_width), bf16)] * 5,
        compiler_params=pltpu.CompilerParams(vmem_limit_bytes=48 * 2**20),
        cost_estimate=pl.CostEstimate(
            flops=40 * count * count * 128 * pairs * 2,
            bytes_accessed=14 * count * head_width * 2,
            transcendentals=2 * pairs * count * count,
        ),
        name="attend_back",
    )(info, joined, grad, out, lse, prompt, prompt, joined, joined, *tables)


def norm_parts(inputs):
    average = jnp.mean(inputs, -1, keepdims=True)
    centred = inputs - average
    spread = jnp.mean(centred * centred, -1, keepdims=True)
    inverse = lax.rsqrt(spread + 1e-05)
    return centred * inverse, inverse


def norm_back(unit, inverse, grad, scales):
    inner = grad * (1.0 + scales)
    first = jnp.mean(inner, -1, keepdims=True)
    second = jnp.mean(inner * unit, -1, keepdims=True)
    return inverse * (inner - first - unit * second)


def split_three(values):
    high = lax.reduce_precision(values, 8, 7)
    rest = values - high
    mid = lax.reduce_precision(rest, 8, 7)
    return high, mid, rest - mid


def body(
    block_input,
    cotangent,
    w_qkv,
    w_out,
    w_up,
    w_down,
    w_mod,
    time_table,
    prompt_len,
    cont_len,
    timestep,
):
    count, width = block_input.shape
    tiles = count // CONT
    dp_count = lax.axis_size("dp")
    tensor_count = lax.axis_size("tensor")
    devices = dp_count * tensor_count
    both = ("dp", "tensor")
    role = lax.axis_index("tensor")
    is_prompt = role == 0

    qkv_piece = w_qkv.reshape(w_qkv.shape[0], -1)
    head_width = w_qkv.shape[2]
    hidden_width = w_up.shape[1]
    cut_qkv = 640
    rest_a = jnp.concatenate([w_out.T, w_up], 1)
    rest_b = w_down.T
    qkv_a = gather_weights(qkv_piece[:, :cut_qkv], True)
    qkv_b = gather_weights(qkv_piece[:, cut_qkv:], False)
    qkv = [jnp.concatenate([qkv_a[t], qkv_b[t]], 1) for t in range(2)]

    steps = jnp.pad(timestep.reshape(1, -1), ((0, 0), (0, width - SEGS))).astype(bf16)
    packet = jnp.concatenate([time_table, steps], 0)
    table_rows = time_table.shape[0]
    packet = jnp.pad(packet, ((0, 16 - packet.shape[0]), (0, 0)))
    packets = lax.all_to_all(
        jnp.broadcast_to(packet[None], (devices,) + packet.shape), both, 0, 0, tiled=True
    )
    table_full = packets[:, :table_rows].reshape(STEPS, width)
    step_rows = packets[::tensor_count, table_rows, :SEGS].astype(jnp.int32)
    step_pad = jnp.pad(step_rows, ((0, 0), (0, 16 - SEGS))).reshape(-1)
    pick = (step_pad[:, None] == jnp.arange(STEPS, dtype=jnp.int32)[None, :]).astype(bf16)
    cond = dot(pick, table_full).astype(bf16)
    col_width = w_mod.shape[1]
    col_part = dot(cond, w_mod).reshape(dp_count, 1, 16, col_width)
    col_part = jnp.broadcast_to(col_part, (dp_count, tensor_count, 16, col_width))
    arrived = lax.all_to_all(
        col_part.reshape(devices, 16, col_width), both, 0, 0, tiled=True
    )
    modulate = jnp.transpose(arrived, (1, 0, 2)).reshape(16, 6, width)
    prompt_mod = modulate[0]
    mods = jnp.where(
        is_prompt, jnp.broadcast_to(modulate[0:1], (tiles, 6, width)), modulate[1 : 1 + tiles]
    )
    mods = [mods[:, n][:, None, :] for n in range(6)]

    prompt_rows = jnp.where(is_prompt, block_input, swap(block_input, "tensor", 1))

    half = HEAD_DIM // 2
    freqs = 10000.0 ** (-(jnp.arange(128, dtype=jnp.int32) % half).astype(f32) / half)
    inside = jnp.arange(count, dtype=jnp.int32)
    prompt_count = prompt_len[0]
    own_places = jnp.where(is_prompt, inside, prompt_count + inside % CONT).astype(f32)
    own_angles = own_places[:, None] * freqs[None, :]
    prompt_angles = inside.astype(f32)[:, None] * freqs[None, :]
    own_cos, own_sin = jnp.cos(own_angles), jnp.sin(own_angles)
    prompt_cos, prompt_sin = jnp.cos(prompt_angles), jnp.sin(prompt_angles)
    own_len = jnp.where(
        is_prompt,
        jnp.clip(prompt_count - CONT * jnp.arange(NCONT, dtype=jnp.int32), 0, CONT),
        cont_len[0],
    )
    info = jnp.concatenate([jnp.stack([role, prompt_count]), own_len]).astype(jnp.int32)
    valid = (inside % CONT < own_len[inside // CONT]).astype(f32).reshape(tiles, CONT, 1)

    inputs = block_input.astype(f32).reshape(tiles, CONT, width)
    unit_one, inverse_one = norm_parts(inputs)
    normed = (unit_one * (1.0 + mods[1]) + mods[0]).astype(bf16).reshape(count, width)
    prompt_unit, _ = norm_parts(prompt_rows.astype(f32))
    prompt_normed = (prompt_unit * (1.0 + prompt_mod[1]) + prompt_mod[0]).astype(bf16)
    joined, prompts, attended, lses = [], [], [], []
    for t in range(2):
        joined.append(project(normed, qkv[t], own_cos, own_sin, 0, 2))
        prompts.append(project(prompt_normed, qkv[t], prompt_cos, prompt_sin, 1, 1))
        out, lse = attend(info, joined[t], prompts[t])
        attended.append(out)
        lses.append(lse)

    part_a = gather_weights(rest_a, True)
    down_t = gather_weights(rest_b, False)
    out_t = [part[:, :head_width] for part in part_a]
    up = [part[:, head_width:] for part in part_a]

    attn_branch = dot(attended[0], out_t[0], NT) + dot(attended[1], out_t[1], NT)
    attn_branch = attn_branch.reshape(tiles, CONT, width)
    attn_part = mods[2] * attn_branch
    middle = inputs + attn_part
    unit_two, inverse_two = norm_parts(middle)
    normed_two = (unit_two * (1.0 + mods[4]) + mods[3]).astype(bf16).reshape(count, width)

    hidden, slope = [], []
    for t in range(2):
        pre_act = dot(normed_two, up[t])
        cdf = 0.5 * (1.0 + lax.erf(pre_act * (2.0**-0.5)))
        pdf = jnp.exp(-0.5 * pre_act * pre_act) * ((2.0 * math.pi) ** -0.5)
        hidden.append((pre_act * cdf).astype(bf16))
        slope.append((cdf + pre_act * pdf).astype(bf16))
    mlp_branch = dot(hidden[0], down_t[0], NT) + dot(hidden[1], down_t[1], NT)
    mlp_branch = mlp_branch.reshape(tiles, CONT, width)
    mlp_part = mods[5] * mlp_branch
    result = middle + mlp_part

    upstream = cotangent.astype(f32).reshape(tiles, CONT, width)
    mlp_grad = (upstream * mods[5]).astype(bf16).reshape(count, width)
    gate_two_grad = jnp.sum(upstream * mlp_branch, 1)
    down_grads = [dot(mlp_grad, hidden[t], TN).astype(bf16) for t in range(2)]
    pre_grad = [(dot(mlp_grad, down_t[t]) * slope[t].astype(f32)).astype(bf16) for t in range(2)]
    up_grads = [dot(normed_two, pre_grad[t], TN).astype(bf16) for t in range(2)]
    normed_two_grad = dot(pre_grad[0], up[0], NT) + dot(pre_grad[1], up[1], NT)
    normed_two_grad = normed_two_grad.reshape(tiles, CONT, width)
    shift_two_grad = jnp.sum(normed_two_grad, 1)
    scale_two_grad = jnp.sum(normed_two_grad * unit_two, 1)
    middle_grad = upstream + norm_back(unit_two, inverse_two, normed_two_grad, mods[4])
    attn_grad = (middle_grad * mods[2]).astype(bf16).reshape(count, width)
    gate_one_grad = jnp.sum(middle_grad * attn_branch, 1)
    out_grads = [dot(attn_grad, attended[t], TN).astype(bf16) for t in range(2)]

    down_grad = scatter_grads(down_grads[0], down_grads[1], False)
    part_grad = scatter_grads(
        jnp.concatenate([out_grads[0], up_grads[0]], 1),
        jnp.concatenate([out_grads[1], up_grads[1]], 1),
        True,
    )
    out_grad = part_grad[:, :head_width]
    up_grad = part_grad[:, head_width:]

    tables = (own_cos, own_sin, prompt_cos, prompt_sin)
    prompt_sum, own_sum, qkv_grads = None, None, []
    for t in range(2):
        attended_grad = dot(attn_grad, out_t[t]).astype(bf16)
        dq, dk, dv, dk_prompt, dv_prompt = attend_back(
            info, joined[t], prompts[t], attended_grad, attended[t], lses[t], tables
        )
        wq, wk, wv = (qkv[t][:, n * head_width : (n + 1) * head_width] for n in range(3))
        prompt_part = dot(dk_prompt, wk, NT) + dot(dv_prompt, wv, NT)
        own_part = dot(dq, wq, NT) + dot(dk, wk, NT) + dot(dv, wv, NT)
        prompt_sum = prompt_part if t == 0 else prompt_sum + prompt_part
        own_sum = own_part if t == 0 else own_sum + own_part
        qkv_grads.append(
            jnp.concatenate(
                [
                    dot(normed, dq, TN),
                    dot(normed, dk, TN) + dot(prompt_normed, dk_prompt, TN),
                    dot(normed, dv, TN) + dot(prompt_normed, dv_prompt, TN),
                ],
                1,
            ).astype(bf16)
        )
    arrived_prompt = swap(prompt_sum.astype(bf16), "tensor", 1)
    normed_grad = own_sum + jnp.where(is_prompt, prompt_sum + arrived_prompt.astype(f32), 0.0)
    normed_grad = normed_grad.reshape(tiles, CONT, width)
    qkv_grad = jnp.concatenate(
        [
            scatter_grads(qkv_grads[0][:, :cut_qkv], qkv_grads[1][:, :cut_qkv], True),
            scatter_grads(qkv_grads[0][:, cut_qkv:], qkv_grads[1][:, cut_qkv:], False),
        ],
        1,
    )

    shift_one_grad = jnp.sum(normed_grad, 1)
    scale_one_grad = jnp.sum(normed_grad * unit_one, 1)
    input_grad = middle_grad + norm_back(unit_one, inverse_one, normed_grad, mods[1])

    sums = jnp.stack(
        [
            shift_one_grad,
            scale_one_grad,
            gate_one_grad,
            shift_two_grad,
            scale_two_grad,
            gate_two_grad,
        ],
        1,
    ).reshape(tiles, 6 * width)
    first_row = (jnp.arange(tiles) == 0)[:, None]
    prompt_sums = jnp.where(first_row, jnp.sum(sums, 0, keepdims=True), 0.0)
    segment_sums = jnp.where(is_prompt, prompt_sums, sums).astype(bf16)

    local = jnp.stack(
        [
            jnp.sum(valid * result * result),
            jnp.sum(valid * attn_part * attn_part),
            jnp.sum(valid * mlp_part * mlp_part),
            jnp.sum(valid) * width,
        ]
    )
    local = jnp.concatenate(split_three(local))
    local = jnp.pad(local, (0, col_width - 12)).astype(bf16)
    packet = segment_sums.reshape(tiles, devices, col_width).transpose(1, 0, 2)
    packet = jnp.concatenate(
        [packet, jnp.broadcast_to(local[None, None], (devices, 1, col_width))], 1
    )
    packet = jnp.pad(packet, ((0, 0), (0, 16 - packet.shape[1]), (0, 0)))
    packets = lax.all_to_all(packet, both, 0, 0, tiled=True)
    totals = jnp.sum(packets[:, tiles, :12].astype(f32), 0)
    totals = totals[:4] + totals[4:8] + totals[8:12]
    stats = jnp.sqrt(totals[:3] / totals[3])

    grads = packets[:, :tiles].reshape(devices * tiles, col_width)
    cond_groups = cond.reshape(dp_count, 16, width)
    own_steps = step_pad.reshape(dp_count, 16)
    cond_rows = jnp.stack([cond_groups[:, :tiles], cond_groups[:, 1 : 1 + tiles]], 1)
    step_slots = jnp.stack([own_steps[:, :tiles], own_steps[:, 1 : 1 + tiles]], 1).reshape(-1)
    mod_grad = dot(cond_rows.reshape(devices * tiles, width), grads, TN)
    condition_grad = dot(grads, w_mod, NT)
    slot_pick = (step_slots[:, None] == jnp.arange(STEPS, dtype=jnp.int32)[None, :]).astype(f32)
    table_part = lax.dot_general(
        slot_pick,
        condition_grad,
        TN,
        precision=lax.Precision.HIGHEST,
        preferred_element_type=f32,
    )
    table_pieces = lax.all_to_all(
        table_part.reshape(devices, table_rows, width), both, 0, 0, tiled=True
    )
    table_grad = jnp.sum(table_pieces, 0)
    return (
        result.reshape(count, width).astype(bf16),
        input_grad.reshape(count, width),
        qkv_grad.reshape(w_qkv.shape),
        out_grad.T,
        up_grad,
        down_grad.T,
        mod_grad,
        table_grad,
        stats,
    )


def solution(mesh):
    return jax.shard_map(
        body,
        mesh=mesh,
        in_specs=(
            P(("dp", "tensor"), None),
            P(("dp", "tensor"), None),
            P("dp", None, "tensor"),
            P("tensor", "dp"),
            P("dp", "tensor"),
            P("tensor", "dp"),
            P(None, ("dp", "tensor")),
            P(("dp", "tensor"), None),
            P("dp"),
            P("dp", None),
            P("dp", None),
        ),
        out_specs=(
            P(("dp", "tensor"), None),
            P(("dp", "tensor"), None),
            P("dp", None, "tensor"),
            P("tensor", "dp"),
            P("dp", "tensor"),
            P("tensor", "dp"),
            P(None, ("dp", "tensor")),
            P(("dp", "tensor"), None),
            P(),
        ),
        check_vma=False,
    )
```

```python
import math

import jax
import jax.numpy as jnp
from jax import lax
from jax.experimental import pallas as pl
from jax.experimental.pallas import tpu as pltpu
from jax.sharding import PartitionSpec as P

HEAD_DIM = 64
PROMPT = 1024
CONT = 128
NCONT = 8
STEPS = 256
SEGS = 1 + NCONT

bf16 = jnp.bfloat16
f32 = jnp.float32
NN = (((1,), (0,)), ((), ()))
NT = (((1,), (1,)), ((), ()))
TN = (((0,), (0,)), ((), ()))
SCALE = HEAD_DIM ** (-0.5)
SCALE2 = SCALE * math.log2(math.e)
NEG = -1e30


def dot(left, right, dims=NN):
    return lax.dot_general(left, right, dims, preferred_element_type=f32)


def lanes(shape):
    return lax.broadcasted_iota(jnp.int32, shape, 1)


def rows(shape):
    return lax.broadcasted_iota(jnp.int32, shape, 0)


BOTH = ("dp", "tensor")
TENSOR, CORE, NEAR = 1, 2, 4
LONG = pl.CostEstimate(flops=10**11, bytes_accessed=1, transcendentals=0)


def swap(x, bits):
    count = lax.axis_size(BOTH)
    return lax.ppermute(x, BOTH, [(i, i ^ bits) for i in range(count)])


def tie(*arrays):
    return lax.optimization_barrier(arrays)


def after(array, *others):
    return lax.optimization_barrier((array,) + others)[0]


def far_count():
    return lax.axis_size("dp") // 4


def far_bits():
    return [1 << k for k in range(far_count().bit_length() - 1)]


def plus(left, right):
    return (left.astype(f32) + right.astype(f32)).astype(bf16)


def send_far(cur):
    cur = cur.reshape((-1, 2) + cur.shape[1:])
    return cur[:, 0], cur[:, 1]


def join_kernel(cuts, bit_ref, own_ref, came_ref, *out_refs):
    bit = bit_ref[0]
    start = 0
    for out_ref, cut in zip(out_refs, cuts):
        for n in range(own_ref.shape[0]):
            out_ref[n, bit] = own_ref[n, :, start : start + cut]
            out_ref[n, 1 - bit] = came_ref[n, :, start : start + cut]
        start += cut


def join(own, came, bit, cuts=None):
    count, rows_each, columns = own.shape
    sizes = cuts or (columns,)
    group = min(count, 2)
    spec = pl.BlockSpec((group, rows_each, columns), lambda n, s: (n, 0, 0))
    outs = pl.pallas_call(
        lambda *refs: join_kernel(sizes, *refs),
        grid_spec=pltpu.PrefetchScalarGridSpec(
            num_scalar_prefetch=1,
            grid=(count // group,),
            in_specs=[spec, spec],
            out_specs=[
                pl.BlockSpec((group, 2, rows_each, cut), lambda n, s: (n, 0, 0, 0)) for cut in sizes
            ],
        ),
        out_shape=[jax.ShapeDtypeStruct((count, 2, rows_each, cut), bf16) for cut in sizes],
        cost_estimate=pl.CostEstimate(flops=1, bytes_accessed=10**6, transcendentals=0),
        compiler_params=pltpu.CompilerParams(vmem_limit_bytes=16 * 2**20),
        name="join",
    )(bit.astype(jnp.int32).reshape(1), own, came)
    outs = [out.reshape(2 * count, rows_each, -1) for out in outs]
    return outs if cuts else outs[0]


def turn(x, cosine, sine):
    lane = lanes(x.shape) % 64
    swapped = jnp.where(lane < 32, -pltpu.roll(x, 96, 1), pltpu.roll(x, 32, 1))
    return x * cosine + swapped * sine


def turn_back(x, cosine, sine):
    lane = lanes(x.shape) % 64
    swapped = jnp.where(lane < 32, pltpu.roll(x, 96, 1), -pltpu.roll(x, 32, 1))
    return x * cosine + swapped * sine


def norm_parts(inputs):
    average = jnp.mean(inputs, -1, keepdims=True)
    centred = inputs - average
    spread = jnp.mean(centred * centred, -1, keepdims=True)
    inverse = lax.rsqrt(spread + 1e-05)
    return centred * inverse, inverse


def norm_back(unit, inverse, grad, scales):
    inner = grad * (1.0 + scales)
    first = jnp.mean(inner, -1, keepdims=True)
    second = jnp.mean(inner * unit, -1, keepdims=True)
    return inverse * (inner - first - unit * second)


def modulation(mods_ref, info, tile, part):
    segment = jnp.where(info[0] == 0, 0, 1 + tile)
    width = mods_ref.shape[1] // 6
    return mods_ref[pl.ds(segment, 1), part * width : (part + 1) * width]


def store_pieces(total, info, keep_ref, send_ref, lead):
    half, rows_each = keep_ref.shape[-3], keep_ref.shape[-2]
    fars = half // 2
    for k in range(half):
        low = total[2 * k * rows_each : (2 * k + 1) * rows_each]
        high = total[(2 * k + 1) * rows_each : (2 * k + 2) * rows_each]
        place = ((k % 2) ^ info[11]) * fars + ((k // 2) ^ info[12])
        keep_ref[lead + (place,)] = jnp.where(info[10] == 0, low, high).astype(bf16)
        send_ref[lead + (place,)] = jnp.where(info[10] == 0, high, low).astype(bf16)


def fill(source_ref, w_refs, out_ref, tables):
    for half, w_ref in enumerate(w_refs):
        pl.when(pl.program_id(0) == half)(lambda w_ref=w_ref: fill_half(source_ref, w_ref, out_ref, tables))


def fill_half(source_ref, w_ref, out_ref, tables):
    joined = dot(source_ref[...], w_ref[...])
    for c in range(joined.shape[1] // 128):
        cut = slice(c * 128, (c + 1) * 128)
        piece = joined[:, cut]
        if tables:
            piece = turn(piece, tables[0][...], tables[1][...])
        out_ref[0, :, cut] = piece.astype(bf16)


def project_own_kernel(info, x_ref, mods_ref, *refs):
    w_ref, (cos_ref, sin_ref, joined_ref, normed_ref) = refs[:2], refs[2:]
    half, part = pl.program_id(0), pl.program_id(1)

    @pl.when((half == 0) & (part == 0))
    def _():
        for i in range(x_ref.shape[0] // CONT):
            cut = slice(i * CONT, (i + 1) * CONT)
            unit, _ = norm_parts(x_ref[cut, :].astype(f32))
            shift, scale = (modulation(mods_ref, info, i, n) for n in range(2))
            normed_ref[cut, :] = (unit * (1.0 + scale) + shift).astype(bf16)

    pl.when(part < 2)(lambda: fill(normed_ref, w_ref, joined_ref, (cos_ref, sin_ref)))
    pl.when(part == 2)(lambda: fill(normed_ref, w_ref, joined_ref, None))


def project_prompt_kernel(info, x_ref, *refs):
    came_refs, (mods_ref, *w_ref, cos_ref, sin_ref, joined_ref, normed_ref) = refs[:-7], refs[-7:]
    half, part = pl.program_id(0), pl.program_id(1)
    width = x_ref.shape[1]

    @pl.when((half == 0) & (part == 0))
    def _():
        shift, scale = mods_ref[0:1, :width], mods_ref[0:1, width : 2 * width]
        for i in range(x_ref.shape[0] // CONT):
            cut = slice(i * CONT, (i + 1) * CONT)
            place = i * CONT
            for came_ref in came_refs:
                if 0 <= place < came_ref.shape[0]:
                    came = came_ref[place : place + CONT, :].astype(f32)
                place -= came_ref.shape[0]
            x = jnp.where(info[0] == 0, x_ref[cut, :].astype(f32), came)
            unit, _ = norm_parts(x)
            normed_ref[cut, :] = (unit * (1.0 + scale) + shift).astype(bf16)

    pl.when(part == 0)(lambda: fill(normed_ref, w_ref, joined_ref, (cos_ref, sin_ref)))
    pl.when(part == 1)(lambda: fill(normed_ref, w_ref, joined_ref, None))


def project(kernel, parts, estimate, info, inputs, mods, qkv, tables):
    count, width = inputs[0].shape
    head_width = qkv[0].shape[1] // 3

    def whole(array):
        return pl.BlockSpec(array.shape, lambda t, p, s: (0,) * array.ndim)

    def weight(half):
        def place(t, p, s):
            now = p + 3 - parts
            return (0, jnp.where(t == half, now, 2 if half == 0 else 3 - parts))

        return pl.BlockSpec((width, head_width), place)

    return pl.pallas_call(
        kernel,
        grid_spec=pltpu.PrefetchScalarGridSpec(
            num_scalar_prefetch=1,
            grid=(2, parts),
            in_specs=[whole(array) for array in inputs]
            + [whole(mods), weight(0), weight(1)]
            + [whole(table) for table in tables],
            out_specs=[
                pl.BlockSpec((1, count, head_width), lambda t, p, s: (t, 0, p)),
                whole(inputs[0]),
            ],
        ),
        out_shape=[
            jax.ShapeDtypeStruct((2, count, parts * head_width), bf16),
            jax.ShapeDtypeStruct((count, width), bf16),
        ],
        compiler_params=pltpu.CompilerParams(vmem_limit_bytes=32 * 2**20),
        cost_estimate=estimate,
        name="project",
    )(info, *inputs, mods, *qkv, *tables)


def middle_kernel(
    info, x_ref, a0_ref, a1_ref, mods_ref, o0_ref, o1_ref, branch_ref, middle_ref, n2_ref
):
    branch = dot(a0_ref[...], o0_ref[...], NT) + dot(a1_ref[...], o1_ref[...], NT)
    branch_ref[...] = branch
    per = x_ref.shape[0] // CONT
    for u in range(per):
        cut = slice(u * CONT, (u + 1) * CONT)
        gate, shift, scale = (
            modulation(mods_ref, info, pl.program_id(0) * per + u, n) for n in (2, 3, 4)
        )
        middle = x_ref[cut, :].astype(f32) + gate * branch[cut]
        middle_ref[cut, :] = middle
        unit, _ = norm_parts(middle)
        n2_ref[cut, :] = (unit * (1.0 + scale) + shift).astype(bf16)


def middle_norm(info, x, attended, mods, out_t):
    count, width = x.shape
    head_width = attended[0].shape[1]
    tile = 256
    by_row = pl.BlockSpec((tile, width), lambda i, s: (i, 0))
    by_head = pl.BlockSpec((tile, head_width), lambda i, s: (i, 0))
    return pl.pallas_call(
        middle_kernel,
        grid_spec=pltpu.PrefetchScalarGridSpec(
            num_scalar_prefetch=1,
            grid=(count // tile,),
            in_specs=[
                by_row,
                by_head,
                by_head,
                pl.BlockSpec(mods.shape, lambda i, s: (0, 0)),
                pl.BlockSpec((width, head_width), lambda i, s: (0, 0)),
                pl.BlockSpec((width, head_width), lambda i, s: (0, 0)),
            ],
            out_specs=[by_row] * 3,
        ),
        out_shape=[
            jax.ShapeDtypeStruct((count, width), f32),
            jax.ShapeDtypeStruct((count, width), f32),
            jax.ShapeDtypeStruct((count, width), bf16),
        ],
        compiler_params=pltpu.CompilerParams(vmem_limit_bytes=32 * 2**20),
        cost_estimate=LONG,
        name="middle_norm",
    )(info, x, *attended, mods, *out_t)


def mlp_kernel(first, info, n2_ref, *refs):
    if first:
        cot_ref, mods_ref = refs[:2]
        refs = refs[2:]
    else:
        n2_turned, out_grad, out_turned, branch_before, grad_before = refs[:5]
        refs = refs[5:]
    up_ref, down_ref, branch_ref, grad_ref = refs[:4]
    down_keep_ref, down_send_ref, up_keep_ref, up_send_ref = refs[4:8]
    if first:
        n2_turned, out_grad, out_turned = refs[8:11]
    hidden, pre_grad = refs[-2:]
    count = n2_ref.shape[0]

    @pl.when(pl.program_id(0) == 0)
    def _():
        if first:
            for i in range(count // CONT):
                cut = slice(i * CONT, (i + 1) * CONT)
                gate = modulation(mods_ref, info, i, 5)
                out_grad[cut, :] = (cot_ref[cut, :].astype(f32) * gate).astype(bf16)
            n2_turned[...] = jnp.transpose(n2_ref[...])
            out_turned[...] = jnp.transpose(out_grad[...])
            branch_ref[...] = jnp.zeros_like(branch_ref)
            grad_ref[...] = jnp.zeros_like(grad_ref)
        else:
            branch_ref[...] = branch_before[...]
            grad_ref[...] = grad_before[...]

    up, down = up_ref[...], down_ref[...]
    tile = 256
    for i in range(count // tile):
        cut = slice(i * tile, (i + 1) * tile)
        pre = dot(n2_ref[cut, :], up)
        cdf = 0.5 * (1.0 + lax.erf(pre * (2.0**-0.5)))
        pdf = jnp.exp(-0.5 * pre * pre) * ((2.0 * math.pi) ** -0.5)
        value = (pre * cdf).astype(bf16)
        hidden[cut, :] = value
        grad = (dot(out_grad[cut, :], down) * (cdf + pre * pdf)).astype(bf16)
        pre_grad[cut, :] = grad
        branch_ref[cut, :] += dot(value, down, NT)
        grad_ref[cut, :] += dot(grad, up, NT)
    store_pieces(dot(out_turned[...], hidden[...]), info, down_keep_ref, down_send_ref, ())
    store_pieces(dot(n2_turned[...], pre_grad[...]), info, up_keep_ref, up_send_ref, ())


def feed_forward(info, n2, sources, up, down):
    count, width = n2.shape
    hidden_width = up.shape[1]
    first = len(sources) == 2
    cols = 384
    dp_count = lax.axis_size("dp")
    pieces = (dp_count // 2, width // dp_count, hidden_width)

    def whole(array):
        return pl.BlockSpec(array.shape, lambda b, s: (0,) * array.ndim)

    piece_spec = pl.BlockSpec(pieces[:2] + (cols,), lambda b, s: (0, 0, b))
    weight_spec = pl.BlockSpec((width, cols), lambda b, s: (0, b))
    outs = [jax.ShapeDtypeStruct((count, width), f32)] * 2 + [
        jax.ShapeDtypeStruct(pieces, bf16)
    ] * 4
    out_specs = [whole(n2)] * 2 + [piece_spec] * 4
    if first:
        shapes = [(width, count), (count, width), (width, count)]
        outs += [jax.ShapeDtypeStruct(shape, bf16) for shape in shapes]
        out_specs += [pl.BlockSpec(shape, lambda b, s: (0, 0)) for shape in shapes]
    return pl.pallas_call(
        lambda *refs: mlp_kernel(first, *refs),
        grid_spec=pltpu.PrefetchScalarGridSpec(
            num_scalar_prefetch=1,
            grid=(hidden_width // cols,),
            in_specs=[whole(n2)] + [whole(array) for array in sources] + [weight_spec] * 2,
            out_specs=out_specs,
            scratch_shapes=[pltpu.VMEM((count, cols), bf16), pltpu.VMEM((count, cols), bf16)],
        ),
        out_shape=outs,
        compiler_params=pltpu.CompilerParams(vmem_limit_bytes=52 * 2**20),
        cost_estimate=LONG,
        name="feed_forward",
    )(info, n2, *sources, up, down)


def post_kernel(
    info,
    middle_ref,
    branch_ref,
    mlp_ref,
    n2_grad_ref,
    cot_ref,
    a0_ref,
    a1_ref,
    mods_ref,
    o0_ref,
    o1_ref,
    out_ref,
    middle_grad_ref,
    g0_ref,
    g1_ref,
    sums_ref,
    keep_ref,
    send_ref,
    total,
    attn_grad,
):
    step = pl.program_id(0)
    per = middle_ref.shape[0] // CONT
    for u in range(per):
        cut = slice(u * CONT, (u + 1) * CONT)
        tile = step * per + u
        gate1, scale2, gate2 = (modulation(mods_ref, info, tile, n) for n in (2, 4, 5))
        middle, branch, mlp = middle_ref[cut, :], branch_ref[cut, :], mlp_ref[cut, :]
        n2_grad, upstream = n2_grad_ref[cut, :], cot_ref[cut, :].astype(f32)
        mlp_part, attn_part = gate2 * mlp, gate1 * branch
        result = middle + mlp_part
        out_ref[cut, :] = result.astype(bf16)
        unit, inverse = norm_parts(middle)
        middle_grad = upstream + norm_back(unit, inverse, n2_grad, scale2)
        middle_grad_ref[cut, :] = middle_grad
        attn_grad[cut, :] = (middle_grad * gate1).astype(bf16)
        valid = (rows((CONT, 1)) < info[2 + tile]).astype(f32)
        for n, value in enumerate(
            (
                middle_grad * branch,
                n2_grad,
                n2_grad * unit,
                upstream * mlp,
                valid * result * result,
                valid * attn_part * attn_part,
                valid * mlp_part * mlp_part,
            )
        ):
            sums_ref[u, n : n + 1, :] = jnp.sum(value, 0, keepdims=True)
        sums_ref[u, 7:8, :] = jnp.zeros_like(gate1)
    halves = ((a0_ref, g0_ref, o0_ref), (a1_ref, g1_ref, o1_ref))
    for t, (a_ref, g_ref, o_ref) in enumerate(halves):
        g_ref[...] = dot(attn_grad[...], o_ref[...]).astype(bf16)
        part = dot(attn_grad[...], a_ref[...], TN)
        total[t] = jnp.where(step == 0, part, total[t] + part)

    @pl.when(step == pl.num_programs(0) - 1)
    def _():
        for t in range(2):
            store_pieces(total[t], info, keep_ref, send_ref, (t,))


def post(info, middle, branch, mlp, n2_grad, cotangent, attended, mods, out_t):
    count, width = middle.shape
    head_width = attended[0].shape[1]
    tile = 256
    tiles = count // CONT
    dp_count = lax.axis_size("dp")
    pieces = (2, dp_count // 2, width // dp_count, head_width)
    by_row = pl.BlockSpec((tile, width), lambda i, s: (i, 0))
    by_head = pl.BlockSpec((tile, head_width), lambda i, s: (i, 0))
    return pl.pallas_call(
        post_kernel,
        grid_spec=pltpu.PrefetchScalarGridSpec(
            num_scalar_prefetch=1,
            grid=(count // tile,),
            in_specs=[by_row] * 5
            + [
                by_head,
                by_head,
                pl.BlockSpec(mods.shape, lambda i, s: (0, 0)),
                pl.BlockSpec((width, head_width), lambda i, s: (0, 0)),
                pl.BlockSpec((width, head_width), lambda i, s: (0, 0)),
            ],
            out_specs=[
                by_row,
                by_row,
                by_head,
                by_head,
                pl.BlockSpec((tile // CONT, 8, width), lambda i, s: (i, 0, 0)),
                pl.BlockSpec(pieces, lambda i, s: (0, 0, 0, 0)),
                pl.BlockSpec(pieces, lambda i, s: (0, 0, 0, 0)),
            ],
            scratch_shapes=[
                pltpu.VMEM((2, width, head_width), f32),
                pltpu.VMEM((tile, width), bf16),
            ],
        ),
        out_shape=[
            jax.ShapeDtypeStruct((count, width), bf16),
            jax.ShapeDtypeStruct((count, width), f32),
            jax.ShapeDtypeStruct((count, head_width), bf16),
            jax.ShapeDtypeStruct((count, head_width), bf16),
            jax.ShapeDtypeStruct((tiles, 8, width), f32),
            jax.ShapeDtypeStruct(pieces, bf16),
            jax.ShapeDtypeStruct(pieces, bf16),
        ],
        compiler_params=pltpu.CompilerParams(vmem_limit_bytes=48 * 2**20),
        cost_estimate=LONG,
        name="post",
    )(info, middle, branch, mlp, n2_grad, cotangent, *attended, mods, *out_t)


def last_kernel(
    info, x_ref, own_ref, prompt_ref, came_ref, middle_grad_ref, mods_ref, out_ref, sums_ref
):
    step = pl.program_id(0)
    per = x_ref.shape[0] // CONT
    for u in range(per):
        cut = slice(u * CONT, (u + 1) * CONT)
        scale = modulation(mods_ref, info, step * per + u, 1)
        prompt = prompt_ref[cut, :] + came_ref[cut, :].astype(f32)
        grad = own_ref[cut, :] + jnp.where(info[0] == 0, prompt, 0.0)
        unit, inverse = norm_parts(x_ref[cut, :].astype(f32))
        sums_ref[u, 0:1, :] = jnp.sum(grad, 0, keepdims=True)
        sums_ref[u, 1:2, :] = jnp.sum(grad * unit, 0, keepdims=True)
        sums_ref[u, 2:, :] = jnp.zeros((6, x_ref.shape[1]), f32)
        out_ref[cut, :] = middle_grad_ref[cut, :] + norm_back(unit, inverse, grad, scale)


def last(info, x, own_sum, prompt_sum, came, middle_grad, mods):
    count, width = x.shape
    tile = 256
    by_row = pl.BlockSpec((tile, width), lambda i, s: (i, 0))
    return pl.pallas_call(
        last_kernel,
        grid_spec=pltpu.PrefetchScalarGridSpec(
            num_scalar_prefetch=1,
            grid=(count // tile,),
            in_specs=[by_row] * 5 + [pl.BlockSpec(mods.shape, lambda i, s: (0, 0))],
            out_specs=[by_row, pl.BlockSpec((tile // CONT, 8, width), lambda i, s: (i, 0, 0))],
        ),
        out_shape=[
            jax.ShapeDtypeStruct((count, width), f32),
            jax.ShapeDtypeStruct((count // CONT, 8, width), f32),
        ],
        compiler_params=pltpu.CompilerParams(vmem_limit_bytes=32 * 2**20),
        cost_estimate=LONG,
        name="last",
    )(info, x, own_sum, prompt_sum, came, middle_grad, mods)


def forward_kernel(info, *refs):
    q_ref, kp_ref, vp_ref, ko_ref, vo_ref = (ref.at[0] for ref in refs[:5])
    o_ref, lse_ref = refs[5:]
    role = info[0]
    prompt_count = info[1]
    count = q_ref.shape[0]
    lane = lanes((count, 128))
    row = rows((count, 128))
    tile = 256
    blocks = count // tile

    def prepare(h):
        sel = (lane // 64) == h
        extra = 64 * (1 - h)
        q = jnp.where(sel, q_ref[...], jnp.where(lane == extra, 1.0, 0.0).astype(bf16))
        bias = jnp.where((lane == extra) & (row >= prompt_count), NEG, 0.0).astype(bf16)
        k = jnp.where(sel, kp_ref[...], bias)
        v = jnp.where(sel, vp_ref[...], jnp.ones((), bf16))
        return sel, q, k, v

    def finish(h, i, o, top):
        extra = 64 * (1 - h)
        weight = o[:, extra : extra + 1]
        lse = top * SCALE2 + jnp.log2(weight)
        turned = jnp.transpose(jnp.broadcast_to(lse, (tile, 128)))
        lse_ref[0, h : h + 1, i * tile : (i + 1) * tile] = turned[0:1, :]
        return o * (1.0 / weight)

    def store(outs):
        for i in range(blocks):
            merged = jnp.where(lanes((tile, 128)) < 64, outs[0][i], outs[1][i])
            o_ref[i * tile : (i + 1) * tile, :] = merged.astype(bf16)

    @pl.when(role == 0)
    def _():
        outs = []
        for h in range(2):
            sel, q, k, v = prepare(h)
            heads = []
            for i in range(blocks):
                start, stop = i * tile, (i + 1) * tile
                s = dot(q[start:stop], k[:stop], NT)
                near = jnp.where(lanes((tile, tile)) <= rows((tile, tile)), s[:, start:], NEG)
                top = jnp.max(near, 1, keepdims=True)
                if i:
                    top = jnp.maximum(top, jnp.max(s[:, :start], 1, keepdims=True))
                o = dot(jnp.exp2(near * SCALE2 - top * SCALE2).astype(bf16), v[start:stop])
                if i:
                    o = o + dot(
                        jnp.exp2(s[:, :start] * SCALE2 - top * SCALE2).astype(bf16), v[:start]
                    )
                heads.append(finish(h, i, o, top))
            outs.append(heads)
        store(outs)

    @pl.when(role != 0)
    def _():
        outs = []
        for h in range(2):
            sel, q, k, v = prepare(h)
            own_k = jnp.where(sel, ko_ref[...], jnp.zeros((), bf16))
            own_v = jnp.where(sel, vo_ref[...], jnp.ones((), bf16))
            heads = []
            for i in range(blocks):
                start, stop = i * tile, (i + 1) * tile
                s = dot(q[start:stop], k, NT)
                cuts = [slice(r, r + CONT) for r in range(start, stop, CONT)]
                near = []
                for cut in cuts:
                    piece = dot(q[cut], own_k[cut], NT)
                    col, line = lanes((CONT, CONT)), rows((CONT, CONT))
                    fine = (col <= line) & (col < info[2 + cut.start // CONT])
                    near.append(jnp.where(fine, piece, NEG))
                near = jnp.concatenate(near, 0)
                top = jnp.maximum(
                    jnp.max(s, 1, keepdims=True), jnp.max(near, 1, keepdims=True)
                )
                far_weight = jnp.exp2(s * SCALE2 - top * SCALE2).astype(bf16)
                near_weight = jnp.exp2(near * SCALE2 - top * SCALE2).astype(bf16)
                own = [
                    dot(near_weight[n * CONT : (n + 1) * CONT], own_v[cut])
                    for n, cut in enumerate(cuts)
                ]
                heads.append(finish(h, i, dot(far_weight, v) + jnp.concatenate(own, 0), top))
            outs.append(heads)
        store(outs)


def attend(info, joined, prompts, t):
    count = joined.shape[1]
    head_width = joined.shape[2] // 3
    pairs = head_width // 128

    def spec(offset):
        return pl.BlockSpec((1, count, 128), lambda h, s: (t, 0, offset + h))

    return pl.pallas_call(
        forward_kernel,
        grid_spec=pltpu.PrefetchScalarGridSpec(
            num_scalar_prefetch=1,
            grid=(pairs,),
            in_specs=[spec(0), spec(0), spec(pairs), spec(pairs), spec(2 * pairs)],
            out_specs=[
                pl.BlockSpec((count, 128), lambda h, s: (0, h)),
                pl.BlockSpec((1, 2, count), lambda h, s: (h, 0, 0)),
            ],
        ),
        out_shape=[
            jax.ShapeDtypeStruct((count, head_width), bf16),
            jax.ShapeDtypeStruct((pairs, 2, count), f32),
        ],
        compiler_params=pltpu.CompilerParams(vmem_limit_bytes=40 * 2**20),
        cost_estimate=LONG,
        name="attend",
    )(info, joined, prompts, prompts, joined, joined)


def backward_kernel(first, last, tiles, own, info, *refs):
    refs = list(refs)
    q_ref, do_ref, o_ref, lse_ref = refs[0].at[0], *refs[1:4]
    del refs[:4]
    if tiles:
        kp_ref, vp_ref, cp_ref, sp_ref = refs[0].at[0], refs[1].at[0], *refs[2:4]
        del refs[:4]
    if own:
        ko_ref, vo_ref = refs[0].at[0], refs[1].at[0]
        del refs[:2]
    if own or last:
        co_ref, so_ref = refs[:2]
        del refs[:2]
    before_ref = None if first else refs.pop(0)
    dq_ref = refs.pop(0)
    if tiles:
        dkp_ref, dvp_ref = refs[:2]
        del refs[:2]
    if own:
        dko_ref, dvo_ref = refs[:2]
        del refs[:2]
    (dq_acc,) = refs
    role = info[0]
    prompt_count = info[1]
    count = q_ref.shape[0]
    tile = 256
    lane = lanes((count, 128))
    none = jnp.zeros((), bf16)
    products = jnp.transpose(do_ref[...].astype(f32) * o_ref[...].astype(f32))
    deltas = [jnp.sum(products[64 * h : 64 * h + 64], 0, keepdims=True) for h in range(2)]
    dq_acc[...] = jnp.zeros_like(dq_acc) if first else before_ref[...]

    def far_block(j, prompt):
        start, stop = j * tile, (j + 1) * tile
        cut = slice(start - tiles[0] * tile, stop - tiles[0] * tile)
        q_from = start if prompt else 0
        lane_k = lanes((tile, 128))
        row_k = rows((tile, 128)) + start
        key_parts, value_parts = [], []
        for h in range(2):
            extra = 64 * (1 - h)
            sel = (lane_k // 64) == h
            bias = jnp.where((lane_k == extra) & (row_k >= prompt_count), NEG, 0.0).astype(bf16)
            k = jnp.where(sel, kp_ref[cut, :], bias)
            k_plain = jnp.where(sel, kp_ref[cut, :], none)
            v = jnp.where(sel, vp_ref[cut, :], none)
            lane_q = lane[q_from:]
            ones = jnp.where(lane_q == extra, 1.0, 0.0).astype(bf16)
            q = jnp.where((lane_q // 64) == h, q_ref[q_from:, :], ones)
            s = dot(k, q, NT)
            if prompt:
                near = jnp.where(rows((tile, tile)) <= lanes((tile, tile)), s[:, :tile], NEG)
                s = jnp.concatenate([near, s[:, tile:]], 1) if stop < count else near
            weight = jnp.exp2(s * SCALE2 - lse_ref[0, h : h + 1, q_from:])
            grad = dot(v, do_ref[q_from:, :], NT)
            score = (weight * (grad - deltas[h][:, q_from:])).astype(bf16)
            value_parts.append(dot(weight.astype(bf16), do_ref[q_from:, :]))
            key_parts.append(dot(score, q_ref[q_from:, :]))
            dq_acc[q_from:, :] += dot(score, k_plain, TN)
        key_grad = jnp.where(lane_k < 64, key_parts[0], key_parts[1]) * SCALE
        value_grad = jnp.where(lane_k < 64, value_parts[0], value_parts[1])
        dkp_ref[cut, :] = turn_back(key_grad, cp_ref[cut, :], sp_ref[cut, :]).astype(bf16)
        dvp_ref[cut, :] = value_grad.astype(bf16)

    @pl.when(role == 0)
    def _():
        for j in tiles:
            far_block(j, True)
        if own:
            dko_ref[...] = jnp.zeros_like(dko_ref)
            dvo_ref[...] = jnp.zeros_like(dvo_ref)

    @pl.when(role != 0)
    def _():
        for j in tiles:
            far_block(j, False)
        lane_k = lanes((CONT, CONT))
        row_k = rows((CONT, CONT))
        for i in range(count // CONT if own else 0):
            cut = slice(i * CONT, (i + 1) * CONT)
            key_parts, value_parts, query_part = [], [], None
            for h in range(2):
                sel = (lane_k // 64) == h
                k = jnp.where(sel, ko_ref[cut, :], none)
                v = jnp.where(sel, vo_ref[cut, :], none)
                fine = (row_k <= lane_k) & (row_k < info[2 + i])
                s = jnp.where(fine, dot(k, q_ref[cut, :], NT), NEG)
                weight = jnp.exp2(s * SCALE2 - lse_ref[0, h : h + 1, cut])
                grad = dot(v, do_ref[cut, :], NT)
                score = (weight * (grad - deltas[h][:, cut])).astype(bf16)
                value_parts.append(dot(weight.astype(bf16), do_ref[cut, :]))
                key_parts.append(dot(score, q_ref[cut, :]))
                part = dot(score, k, TN)
                query_part = part if query_part is None else query_part + part
            dq_acc[cut, :] += query_part
            key_grad = jnp.where(lane_k < 64, key_parts[0], key_parts[1]) * SCALE
            value_grad = jnp.where(lane_k < 64, value_parts[0], value_parts[1])
            dko_ref[cut, :] = turn_back(key_grad, co_ref[cut, :], so_ref[cut, :]).astype(bf16)
            dvo_ref[cut, :] = value_grad.astype(bf16)

    if last:
        dq_ref[...] = turn_back(dq_acc[...] * SCALE, co_ref[...], so_ref[...]).astype(bf16)
    else:
        dq_ref[...] = dq_acc[...]


def attend_back(info, joined, prompts, t, grad, out, lse, tables, tiles, own, before=None, last=True):
    count = joined.shape[1]
    head_width = joined.shape[2] // 3
    pairs = head_width // 128
    first = before is None
    part = 256 * len(tiles)

    def half_spec(offset):
        return pl.BlockSpec((1, count, 128), lambda h, s: (t, 0, offset + h))

    def part_spec(offset):
        return pl.BlockSpec((1, part, 128), lambda h, s: (t, tiles[0] * 256 // part, offset + h))

    rows_spec = pl.BlockSpec((count, 128), lambda h, s: (0, h))
    whole = pl.BlockSpec((count, 128), lambda h, s: (0, 0))
    args = [joined, grad, out, lse]
    specs = [
        half_spec(0),
        rows_spec,
        rows_spec,
        pl.BlockSpec((1, 2, count), lambda h, s: (h, 0, 0)),
    ]
    outs = [jax.ShapeDtypeStruct((count, head_width), bf16 if last else f32)]
    out_specs = [rows_spec]
    if tiles:
        args += [prompts, prompts, tables[2], tables[3]]
        part_table = pl.BlockSpec((part, 128), lambda h, s: (tiles[0] * 256 // part, 0))
        specs += [part_spec(0), part_spec(pairs), part_table, part_table]
        outs += [jax.ShapeDtypeStruct((part, head_width), bf16)] * 2
        out_specs += [pl.BlockSpec((part, 128), lambda h, s: (0, h))] * 2
    if own:
        args += [joined, joined]
        specs += [half_spec(pairs), half_spec(2 * pairs)]
        outs += [jax.ShapeDtypeStruct((count, head_width), bf16)] * 2
        out_specs += [rows_spec] * 2
    if own or last:
        args += [tables[0], tables[1]]
        specs += [whole, whole]
    if not first:
        args += [before]
        specs += [rows_spec]
    return pl.pallas_call(
        lambda *refs: backward_kernel(first, last, tiles, own, *refs),
        grid_spec=pltpu.PrefetchScalarGridSpec(
            num_scalar_prefetch=1,
            grid=(pairs,),
            in_specs=specs,
            out_specs=out_specs,
            scratch_shapes=[pltpu.VMEM((count, 128), f32)],
        ),
        out_shape=outs,
        compiler_params=pltpu.CompilerParams(vmem_limit_bytes=48 * 2**20),
        cost_estimate=LONG,
        name="attend_back",
    )(info, *args)


def split_three(values):
    high = lax.reduce_precision(values, 8, 7)
    rest = values - high
    mid = lax.reduce_precision(rest, 8, 7)
    return high, mid, rest - mid


def pick(x, index, axis):
    return lax.dynamic_index_in_dim(x, index, axis, keepdims=False)


def body(
    block_input,
    cotangent,
    w_qkv,
    w_out,
    w_up,
    w_down,
    w_mod,
    time_table,
    prompt_len,
    cont_len,
    timestep,
):
    count, width = block_input.shape
    tiles = count // CONT
    dp_count = lax.axis_size("dp")
    tensor_count = lax.axis_size("tensor")
    devices = dp_count * tensor_count
    role = lax.axis_index("tensor")
    is_prompt = role == 0
    me = lax.axis_index("dp")
    core, near, far = me % 2, (me // 2) % 2, me // 4
    fars = far_count()
    low_bits = far_bits()
    high_bits = list(reversed(low_bits))
    head_width = w_qkv.shape[2]
    half = count // 2

    def far_bit(bit):
        return (far // bit) % 2

    far_top, far_rest = high_bits[0], high_bits[1:]
    cuts = (head_width, w_up.shape[1], w_down.shape[0])
    table_rows, rows_each = time_table.shape[0], w_qkv.shape[0]
    steps = jnp.pad(timestep.reshape(1, -1), ((0, rows_each - 1), (0, 128 - SEGS))).astype(bf16)
    table_width = table_rows * width // rows_each
    table_width += -table_width % 128
    table_part = time_table.reshape(-1)
    table_part = jnp.pad(table_part, (0, rows_each * table_width - table_part.shape[0]))
    table_part = table_part.reshape(rows_each, table_width)
    first = [w_qkv.reshape(rows_each, -1), table_part, steps]
    first_cuts = (first[0].shape[1], table_width + 128)
    first = jnp.concatenate(first, 1)[None]
    bounds = [0, count // 4, count * 5 // 8, count]
    x_parts = [block_input[bounds[n] : bounds[n + 1]] for n in range(3)]
    rest = jnp.concatenate([w_out.T, w_up, w_down.T], 1)[None]
    came_first = swap(first, 8 * far_top)
    first, came_first, x_parts, rest = tie(first, came_first, x_parts, rest)
    came = [swap(x_parts[0], TENSOR)]
    for bit in far_rest:
        first = join(first, came_first, far_bit(2 * bit))
        came_first = swap(first, 8 * bit)
    came_first, first, came, rest = tie(came_first, first, came, rest)
    qkv_far, table_far = join(first, came_first, far_bit(1), first_cuts)

    table_near = [swap(table_far, bits) for bits in (NEAR, TENSOR, NEAR + TENSOR)]
    qkv_near = [swap(qkv_far, bits) for bits in (NEAR, TENSOR)]
    table_own = join(table_far, table_near[0], near)
    table_other = join(table_near[1], table_near[2], near)
    table_came = [swap(table_own, CORE), swap(table_other, CORE)]
    table_cuts = (table_width, 128)
    packets = [
        join(table_own, table_came[0], core, table_cuts),
        join(table_other, table_came[1], core, table_cuts),
    ]
    rest_came = swap(rest, 8 * far_top)

    turns = HEAD_DIM // 2
    freqs = 10000.0 ** (-(jnp.arange(128, dtype=jnp.int32) % turns).astype(f32) / turns)
    inside = jnp.arange(count, dtype=jnp.int32)
    prompt_count = prompt_len[0]
    own_places = jnp.where(is_prompt, inside, prompt_count + inside % CONT).astype(f32)
    own_angles = own_places[:, None] * freqs[None, :]
    prompt_angles = inside.astype(f32)[:, None] * freqs[None, :]
    tables = (jnp.cos(own_angles), jnp.sin(own_angles), jnp.cos(prompt_angles), jnp.sin(prompt_angles))
    own_len = jnp.where(
        is_prompt,
        jnp.clip(prompt_count - CONT * jnp.arange(NCONT, dtype=jnp.int32), 0, CONT),
        cont_len[0],
    )
    info = jnp.concatenate(
        [jnp.stack([role, prompt_count]), own_len, jnp.stack([core, near, far])]
    ).astype(jnp.int32)

    table_full = jnp.concatenate([packets[0][0], packets[1][0]], 0)
    table_full = table_full.reshape(2 * dp_count, -1)[:, : table_rows * width]
    table_full = table_full.reshape(STEPS, width)
    step_rows = packets[0][1][:, 0, :SEGS].astype(jnp.int32)
    row_ids = (jnp.arange(2)[:, None, None] + role) % 2 * table_rows + (
        jnp.arange(dp_count)[None, :, None] * 2 * table_rows + jnp.arange(table_rows)
    )
    row_ids = row_ids.reshape(-1).astype(jnp.int32)
    step_pad = jnp.pad(step_rows, ((0, 0), (0, 16 - SEGS))).reshape(-1)
    chosen = (step_pad[:, None] == row_ids[None, :]).astype(bf16)
    cond = dot(chosen, table_full).astype(bf16)
    col_width = w_mod.shape[1]
    col_part = dot(cond, w_mod).reshape(dp_count, 1, 16, col_width)
    col_part = jnp.broadcast_to(col_part, (dp_count, tensor_count, 16, col_width))
    col_part = col_part.reshape(devices, 16, col_width).astype(f32)
    arrived = lax.all_to_all(col_part, BOTH, 0, 0, tiled=True)
    qkv_far, qkv_near, rest, rest_came, tables, info, _ = tie(
        qkv_far, qkv_near, rest, rest_came, tables, info, col_part
    )
    qkv_near.append(swap(qkv_far, NEAR + TENSOR))
    rest = join(rest, rest_came, far_bit(far_top), None if far_rest else cuts)
    if far_rest:
        rest_came = swap(rest, 8 * far_rest[0])

    qkv_far, qkv_near, arrived, came, x_parts = tie(qkv_far, qkv_near, arrived, came, x_parts)
    came.append(swap(x_parts[1], TENSOR))
    mods = jnp.transpose(arrived, (1, 0, 2)).reshape(16, 6 * width).astype(f32)
    qkv_own = join(qkv_far, qkv_near[0], near)
    qkv_other = join(qkv_near[1], qkv_near[2], near)
    qkv_came = [swap(qkv_own, CORE), swap(qkv_other, CORE)]
    for bit in far_rest[1:]:
        rest = join(rest, rest_came, far_bit(bit * 2))
        rest_came = swap(rest, 8 * bit)
    qkv = [
        join(own, other, core).reshape(width, -1)
        for own, other in zip((qkv_own, qkv_other), qkv_came)
    ]
    rest, rest_came, mods, qkv, came, x_parts = tie(rest, rest_came, mods, qkv, came, x_parts)

    came.append(swap(x_parts[2], TENSOR))
    o_own, u_own, d_own = join(rest, rest_came, far_bit(1), cuts) if far_rest else rest
    u_near, o_near, o_other = swap(u_own, NEAR), swap(o_own, NEAR), swap(o_own, TENSOR)
    joined, normed = project(
        project_own_kernel, 3, LONG, info, [block_input], mods, qkv, tables[:2]
    )
    came, joined, u_near = tie(came, joined, u_near)
    prompts, prompt_normed = project(
        project_prompt_kernel, 2, LONG, info, [block_input, *came], mods, qkv, tables[2:]
    )
    u_near, o_near, o_other, u_own, o_own, d_own, prompts = tie(
        u_near, o_near, o_other, u_own, o_own, d_own, prompts
    )
    d_near, u_other, oo_near = swap(d_own, NEAR), swap(u_own, TENSOR), swap(o_other, NEAR)
    u_own, o_own = join(u_own, u_near, near), join(o_own, o_near, near)
    u_core = swap(u_own, CORE)
    out_0, lse_0 = attend(info, *tie(joined, prompts, u_own, o_own)[:2], 0)
    d_near, u_other, oo_near, u_core, d_own, u_own, o_own, o_other, out_0, joined = tie(
        d_near, u_other, oo_near, u_core, d_own, u_own, o_own, o_other, out_0, joined
    )
    d_other, uu_near = swap(d_own, TENSOR), swap(u_other, NEAR)
    d_own, o_other = join(d_own, d_near, near), join(o_other, oo_near, near)
    d_core, o_core, oo_core = swap(d_own, CORE), swap(o_own, CORE), swap(o_other, CORE)
    up_0 = join(u_own, u_core, core).reshape(width, -1)
    out_1, lse_1 = attend(info, *tie(joined, prompts, d_own, o_other, up_0)[:2], 1)
    d_other, uu_near, d_core, o_core, oo_core, d_own, o_own, o_other, u_other, out_1 = tie(
        d_other, uu_near, d_core, o_core, oo_core, d_own, o_own, o_other, u_other, out_1
    )
    attended, lses = [out_0, out_1], [lse_0, lse_1]
    out_t = [
        join(o_own, o_core, core).reshape(width, -1),
        join(o_other, oo_core, core).reshape(width, -1),
    ]
    branch, middle, normed_two = middle_norm(info, block_input, attended, mods, out_t)

    dd_near = swap(d_other, NEAR)
    u_other = join(u_other, uu_near, near)
    uu_core = swap(u_other, CORE)
    down_0 = join(d_own, d_core, core).reshape(width, -1)
    d_other, u_other, normed_two, down_0 = tie(d_other, u_other, normed_two, down_0)
    mlp, n2_grad, d_keep_0, d_send_0, u_keep_0, u_send_0, *shared = feed_forward(
        info, normed_two, (cotangent, mods), up_0, down_0
    )
    dd_near, uu_core, d_other, u_other, mlp, d_send_0, u_send_0 = tie(
        dd_near, uu_core, d_other, u_other, mlp, d_send_0, u_send_0
    )
    d_other = join(d_other, dd_near, near)
    dd_core = swap(d_other, CORE)
    up_1 = join(u_other, uu_core, core).reshape(width, -1)
    down_1 = join(d_other, dd_core, core).reshape(width, -1)
    up_1, down_1, mlp, d_send_0, u_send_0 = tie(up_1, down_1, mlp, d_send_0, u_send_0)
    d_came_0, u_came_0 = swap(d_send_0, CORE), swap(u_send_0, CORE)
    mlp, n2_grad, d_keep_1, d_send_1, u_keep_1, u_send_1 = feed_forward(
        info, normed_two, (*shared, mlp, n2_grad), up_1, down_1
    )
    d_came_0, u_came_0, mlp, d_send_1, u_send_1 = tie(d_came_0, u_came_0, mlp, d_send_1, u_send_1)
    d_came_1, u_came_1 = swap(d_send_1, CORE), swap(u_send_1, CORE)
    block_output, middle_grad, grad_0, grad_1, post_sums, o_keep, o_send = post(
        info, middle, branch, mlp, n2_grad, cotangent, attended, mods, out_t
    )
    d_came_1, u_came_1, o_keep, o_send, grad_0, grad_1 = tie(
        d_came_1, u_came_1, o_keep, o_send, grad_0, grad_1
    )

    def by_near(x):
        return x.reshape((2, 2, fars) + x.shape[2:])

    def near_part(keep, came, part):
        half_of = slice(part * fars, (part + 1) * fars)
        return plus(keep[half_of], came[half_of])

    o_came = swap(o_send, CORE)
    d_send = [near_part(d_keep_0, d_came_0, 1), near_part(d_keep_1, d_came_1, 1)]
    d_keep = [near_part(d_keep_0, d_came_0, 0), near_part(d_keep_1, d_came_1, 0)]
    u_send, u_keep = plus(u_keep_1, u_came_1), plus(u_keep_0, u_came_0)
    d_came, u_came = swap(jnp.stack(d_send), NEAR), swap(u_send, TENSOR)
    d_keep, u_keep, grad_1 = tie(d_keep, u_keep, grad_1)

    def back(t, grad, blocks, own, before=None, last=True):
        return attend_back(
            info, joined, prompts, t, grad, attended[t], lses[t], tables, blocks, own, before, last
        )

    wq, wk, wv = (
        [qkv[t][:, n * head_width : (n + 1) * head_width] for t in range(2)] for n in range(3)
    )

    def prompt_part(t, dk, dv):
        return dot(dk, wk[t], NT) + dot(dv, wv[t], NT)

    def own_part(t, dq, dk, dv):
        return dot(dq, wq[t], NT) + dot(dk, wk[t], NT) + dot(dv, wv[t], NT)

    def weight_part(dq, dk, dv, dk_prompt, dv_prompt):
        parts = [
            dot(normed, dq, TN),
            dot(normed, dk, TN) + dot(prompt_normed, dk_prompt, TN),
            dot(normed, dv, TN) + dot(prompt_normed, dv_prompt, TN),
        ]
        whole = jnp.concatenate(parts, 1).astype(bf16)
        return whole.reshape(fars, 2, 2, -1, whole.shape[1])

    dq_1, dkp_1, dvp_1, dk_1, dv_1 = back(1, grad_1, (0, 1, 2, 3), True)
    d_came, u_came, o_came, d_keep, u_keep, o_keep, grad_0, dq_1, dkp_1, dvp_1, dk_1, dv_1 = tie(
        d_came, u_came, o_came, d_keep, u_keep, o_keep, grad_0, dq_1, dkp_1, dvp_1, dk_1, dv_1
    )
    o_cur = by_near(plus(o_keep, o_came))
    d_keep, d_send = plus(d_keep[0], d_came[0]), plus(d_keep[1], d_came[1])
    u_keep, u_send = near_part(u_keep, u_came, 0), near_part(u_keep, u_came, 1)
    d_came, u_came = swap(d_send, TENSOR), swap(u_send, NEAR)
    o_came = swap(o_cur[:, 1], NEAR)
    o_keep = o_cur[:, 0]
    q_cur = weight_part(dq_1, dk_1, dv_1, dkp_1, dvp_1)
    q_came = swap(pick(q_cur, 1 - core, 2), CORE)
    q_keep = pick(q_cur, core, 2)
    own_sum = own_part(1, dq_1, dk_1, dv_1)
    prompt_sum = prompt_part(1, dkp_1, dvp_1)
    q_keep, own_sum, prompt_sum, grad_0, d_keep, u_keep, o_keep = tie(
        q_keep, own_sum, prompt_sum, grad_0, d_keep, u_keep, o_keep
    )

    dq_0, dkp_a, dvp_a = back(0, grad_0, (0, 1), False, None, False)
    q_came, d_came, u_came, o_came, q_keep, d_keep, u_keep, o_keep, dq_0, dkp_a, dvp_a = tie(
        q_came, d_came, u_came, o_came, q_keep, d_keep, u_keep, o_keep, dq_0, dkp_a, dvp_a
    )
    sum_a = prompt_sum[:half] + prompt_part(0, dkp_a, dvp_a)
    came_a = swap(sum_a.astype(bf16), TENSOR)
    d_keep, d_send = send_far(plus(d_keep, d_came))
    u_keep, u_send = send_far(plus(u_keep, u_came))
    o_cur = plus(o_keep, o_came)
    q_cur = plus(q_keep, q_came)
    d_came, u_came = swap(d_send, 8), swap(u_send, 8)
    o_came, o_keep = swap(o_cur[1], TENSOR), o_cur[0]
    q_came, q_keep = swap(pick(q_cur, 1 - near, 1), NEAR), pick(q_cur, near, 1)
    sum_a, d_keep, u_keep, o_keep, q_keep, dq_0 = tie(sum_a, d_keep, u_keep, o_keep, q_keep, dq_0)

    dq_0, dkp_b, dvp_b, dk_0, dv_0 = back(0, grad_0, (2, 3), True, dq_0, True)
    came, keep, grads = tie(
        (came_a, d_came, u_came, o_came, q_came),
        (d_keep, u_keep, o_keep, q_keep),
        (dkp_b, dvp_b, dk_0, dv_0, dq_0),
    )
    came_a, d_came, u_came, o_came, q_came = came
    d_keep, u_keep, o_keep, q_keep = keep
    dkp_b, dvp_b, dk_0, dv_0, dq_0 = grads
    sum_b = prompt_sum[half:] + prompt_part(0, dkp_b, dvp_b)
    came_b = swap(sum_b.astype(bf16), TENSOR)
    sum_b, dq_0, dk_0, dv_0 = tie(sum_b, dq_0, dk_0, dv_0)

    def far_end(keep, came):
        for bit in low_bits[1:]:
            keep, send = send_far(plus(keep, came))
            came = swap(send, 8 * bit)
        return keep, came

    d_keep, d_came = far_end(d_keep, d_came)
    u_keep, u_came = far_end(u_keep, u_came)
    o_keep, o_send = send_far(plus(o_keep, o_came))
    o_came = swap(o_send, 8)
    q_other = swap(plus(q_keep, q_came), TENSOR)
    dkp_0, dvp_0 = jnp.concatenate([dkp_a, dkp_b], 0), jnp.concatenate([dvp_a, dvp_b], 0)
    q_cur = weight_part(dq_0, dk_0, dv_0, dkp_0, dvp_0)
    q_came, q_keep = swap(pick(q_cur, 1 - core, 2), CORE), pick(q_cur, core, 2)
    own_sum = own_sum + own_part(0, dq_0, dk_0, dv_0)
    q_came, q_keep, own_sum = tie(q_came, q_keep, own_sum)
    q_cur = plus(q_keep, q_came)
    q_came, q_keep = swap(pick(q_cur, 1 - near, 1), NEAR), pick(q_cur, near, 1)
    d_came, u_came, o_came, q_other, own_sum, o_keep, d_keep, u_keep, came_b = tie(
        d_came, u_came, o_came, q_other, own_sum, o_keep, d_keep, u_keep, came_b
    )
    input_grad, last_sums = last(
        info,
        block_input,
        own_sum,
        jnp.concatenate([sum_a, sum_b], 0),
        jnp.concatenate([came_a, came_b], 0),
        middle_grad,
        mods,
    )
    q_came, q_keep, last_sums, d_keep, u_keep = tie(q_came, q_keep, last_sums, d_keep, u_keep)
    down_grad = (d_keep.astype(f32) + d_came.astype(f32))[0]
    up_grad = (u_keep.astype(f32) + u_came.astype(f32))[0]
    o_keep, o_came = far_end(o_keep, o_came)
    out_grad = (o_keep.astype(f32) + o_came.astype(f32))[0]
    q_cur = q_keep.astype(f32) + q_came.astype(f32) + q_other.astype(f32)
    q_cur = q_cur.reshape((2,) * len(low_bits) + q_cur.shape[1:])
    for bit in low_bits:
        axis = q_cur.ndim - 3
        mine = (far // bit) % 2
        q_cur = q_cur.astype(bf16)
        came = swap(pick(q_cur, 1 - mine, axis), 8 * bit)
        q_cur = pick(q_cur, mine, axis).astype(f32) + came.astype(f32)

    order = [last_sums[:, 0], last_sums[:, 1]] + [post_sums[:, n] for n in range(4)]
    sums = jnp.stack(order, 1).reshape(tiles, 6 * width)
    first_row = (jnp.arange(tiles) == 0)[:, None]
    prompt_sums = jnp.where(first_row, jnp.sum(sums, 0, keepdims=True), 0.0)
    segment_sums = jnp.where(is_prompt, prompt_sums, sums).astype(bf16)

    local = jnp.concatenate(
        [
            jnp.sum(post_sums[:, 4:7], (0, 2)),
            (jnp.sum(own_len) * width).astype(f32).reshape(1),
        ]
    )
    local = jnp.concatenate(split_three(local))
    local = jnp.pad(local, (0, col_width - 12)).astype(bf16)
    packet = segment_sums.reshape(tiles, devices, col_width).transpose(1, 0, 2)
    packet = jnp.concatenate(
        [packet, jnp.broadcast_to(local[None, None], (devices, 1, col_width))], 1
    )
    packet = jnp.pad(packet, ((0, 0), (0, 16 - packet.shape[1]), (0, 0)))
    packets = lax.all_to_all(packet, BOTH, 0, 0, tiled=True)
    totals = jnp.sum(packets[:, tiles, :12].astype(f32), 0)
    totals = totals[:4] + totals[4:8] + totals[8:12]
    stats = jnp.sqrt(totals[:3] / totals[3])

    grads = packets[:, :tiles].reshape(devices * tiles, col_width)
    cond_groups = cond.reshape(dp_count, 16, width)
    own_steps = step_pad.reshape(dp_count, 16)
    cond_rows = jnp.stack([cond_groups[:, :tiles], cond_groups[:, 1 : 1 + tiles]], 1)
    step_slots = jnp.stack([own_steps[:, :tiles], own_steps[:, 1 : 1 + tiles]], 1).reshape(-1)
    mod_grad = dot(cond_rows.reshape(devices * tiles, width), grads, TN)
    condition_grad = dot(grads, w_mod, NT)
    slot_pick = (step_slots[:, None] == jnp.arange(STEPS, dtype=jnp.int32)[None, :]).astype(f32)
    table_part = lax.dot_general(
        slot_pick,
        condition_grad,
        TN,
        precision=lax.Precision.HIGHEST,
        preferred_element_type=f32,
    )
    table_pieces = lax.all_to_all(
        table_part.astype(bf16).reshape(devices, table_rows, width), BOTH, 0, 0, tiled=True
    )
    table_grad = jnp.sum(table_pieces.astype(f32), 0)
    return (
        block_output,
        input_grad,
        q_cur.reshape(w_qkv.shape),
        out_grad.T,
        up_grad,
        down_grad.T,
        mod_grad,
        table_grad,
        stats,
    )


def solution(mesh):
    return jax.shard_map(
        body,
        mesh=mesh,
        in_specs=(
            P(("dp", "tensor"), None),
            P(("dp", "tensor"), None),
            P("dp", None, "tensor"),
            P("tensor", "dp"),
            P("dp", "tensor"),
            P("tensor", "dp"),
            P(None, ("dp", "tensor")),
            P(("dp", "tensor"), None),
            P("dp"),
            P("dp", None),
            P("dp", None),
        ),
        out_specs=(
            P(("dp", "tensor"), None),
            P(("dp", "tensor"), None),
            P("dp", None, "tensor"),
            P("tensor", "dp"),
            P("dp", "tensor"),
            P("tensor", "dp"),
            P(None, ("dp", "tensor")),
            P(("dp", "tensor"), None),
            P(),
        ),
        check_vma=False,
    )
```

```python
import math

import jax
import jax.numpy as jnp
from jax import lax
from jax.experimental import pallas as pl
from jax.experimental.pallas import tpu as pltpu
from jax.sharding import PartitionSpec as P

HEAD_DIM = 64
PROMPT = 1024
CONT = 128
NCONT = 8
STEPS = 256
SEGS = 1 + NCONT

bf16 = jnp.bfloat16
f32 = jnp.float32
NN = (((1,), (0,)), ((), ()))
NT = (((1,), (1,)), ((), ()))
TN = (((0,), (0,)), ((), ()))
SCALE = HEAD_DIM ** (-0.5)
SCALE2 = SCALE * math.log2(math.e)
NEG = -1e30


def dot(left, right, dims=NN):
    return lax.dot_general(left, right, dims, preferred_element_type=f32)


def lanes(shape):
    return lax.broadcasted_iota(jnp.int32, shape, 1)


def rows(shape):
    return lax.broadcasted_iota(jnp.int32, shape, 0)


BOTH = ("dp", "tensor")
TENSOR, CORE, NEAR = 1, 2, 4
LONG = pl.CostEstimate(flops=10**11, bytes_accessed=1, transcendentals=0)


def swap(x, bits):
    count = lax.axis_size(BOTH)
    return lax.ppermute(x, BOTH, [(i, i ^ bits) for i in range(count)])


def tie(*arrays):
    return lax.optimization_barrier(arrays)


def after(array, *others):
    return lax.optimization_barrier((array,) + others)[0]


def far_count():
    return lax.axis_size("dp") // 4


def far_bits():
    return [1 << k for k in range(far_count().bit_length() - 1)]


def plus(left, right):
    return (left.astype(f32) + right.astype(f32)).astype(bf16)


def send_far(cur):
    cur = cur.reshape((-1, 2) + cur.shape[1:])
    return cur[:, 0], cur[:, 1]


def join_kernel(cuts, bit_ref, own_ref, came_ref, *out_refs):
    bit = bit_ref[0]
    start = 0
    for out_ref, cut in zip(out_refs, cuts):
        for n in range(own_ref.shape[0]):
            out_ref[n, bit] = own_ref[n, :, start : start + cut]
            out_ref[n, 1 - bit] = came_ref[n, :, start : start + cut]
        start += cut


def join(own, came, bit, cuts=None):
    count, rows_each, columns = own.shape
    sizes = cuts or (columns,)
    group = min(count, 2)
    spec = pl.BlockSpec((group, rows_each, columns), lambda n, s: (n, 0, 0))
    outs = pl.pallas_call(
        lambda *refs: join_kernel(sizes, *refs),
        grid_spec=pltpu.PrefetchScalarGridSpec(
            num_scalar_prefetch=1,
            grid=(count // group,),
            in_specs=[spec, spec],
            out_specs=[
                pl.BlockSpec((group, 2, rows_each, cut), lambda n, s: (n, 0, 0, 0)) for cut in sizes
            ],
        ),
        out_shape=[jax.ShapeDtypeStruct((count, 2, rows_each, cut), bf16) for cut in sizes],
        cost_estimate=pl.CostEstimate(flops=1, bytes_accessed=10**6, transcendentals=0),
        compiler_params=pltpu.CompilerParams(vmem_limit_bytes=16 * 2**20),
        name="join",
    )(bit.astype(jnp.int32).reshape(1), own, came)
    outs = [out.reshape(2 * count, rows_each, -1) for out in outs]
    return outs if cuts else outs[0]


def turn(x, cosine, sine):
    lane = lanes(x.shape) % 64
    swapped = jnp.where(lane < 32, -pltpu.roll(x, 96, 1), pltpu.roll(x, 32, 1))
    return x * cosine + swapped * sine


def turn_back(x, cosine, sine):
    lane = lanes(x.shape) % 64
    swapped = jnp.where(lane < 32, pltpu.roll(x, 96, 1), -pltpu.roll(x, 32, 1))
    return x * cosine + swapped * sine


def norm_parts(inputs):
    average = jnp.mean(inputs, -1, keepdims=True)
    centred = inputs - average
    spread = jnp.mean(centred * centred, -1, keepdims=True)
    inverse = lax.rsqrt(spread + 1e-05)
    return centred * inverse, inverse


def norm_back(unit, inverse, grad, scales):
    inner = grad * (1.0 + scales)
    first = jnp.mean(inner, -1, keepdims=True)
    second = jnp.mean(inner * unit, -1, keepdims=True)
    return inverse * (inner - first - unit * second)


def modulation(mods_ref, info, tile, part):
    segment = jnp.where(info[0] == 0, 0, 1 + tile)
    width = mods_ref.shape[1] // 6
    return mods_ref[pl.ds(segment, 1), part * width : (part + 1) * width]


def store_pieces(total, info, keep_ref, send_ref, lead):
    half, rows_each = keep_ref.shape[-3], keep_ref.shape[-2]
    fars = half // 2
    for k in range(half):
        low = total[2 * k * rows_each : (2 * k + 1) * rows_each]
        high = total[(2 * k + 1) * rows_each : (2 * k + 2) * rows_each]
        place = ((k % 2) ^ info[11]) * fars + ((k // 2) ^ info[12])
        keep_ref[lead + (place,)] = jnp.where(info[10] == 0, low, high).astype(bf16)
        send_ref[lead + (place,)] = jnp.where(info[10] == 0, high, low).astype(bf16)


def fill(source_ref, w_refs, out_ref, tables):
    for half, w_ref in enumerate(w_refs):
        pl.when(pl.program_id(0) == half)(lambda w_ref=w_ref: fill_half(source_ref, w_ref, out_ref, tables))


def fill_half(source_ref, w_ref, out_ref, tables):
    joined = dot(source_ref[...], w_ref[...])
    for c in range(joined.shape[1] // 128):
        cut = slice(c * 128, (c + 1) * 128)
        piece = joined[:, cut]
        if tables:
            piece = turn(piece, tables[0][...], tables[1][...])
        out_ref[0, :, cut] = piece.astype(bf16)


def project_own_kernel(info, x_ref, mods_ref, *refs):
    w_ref, (cos_ref, sin_ref, joined_ref, normed_ref) = refs[:2], refs[2:]
    half, part = pl.program_id(0), pl.program_id(1)

    @pl.when((half == 0) & (part == 0))
    def _():
        for i in range(x_ref.shape[0] // CONT):
            cut = slice(i * CONT, (i + 1) * CONT)
            unit, _ = norm_parts(x_ref[cut, :].astype(f32))
            shift, scale = (modulation(mods_ref, info, i, n) for n in range(2))
            normed_ref[cut, :] = (unit * (1.0 + scale) + shift).astype(bf16)

    pl.when(part < 2)(lambda: fill(normed_ref, w_ref, joined_ref, (cos_ref, sin_ref)))
    pl.when(part == 2)(lambda: fill(normed_ref, w_ref, joined_ref, None))


def project_prompt_kernel(info, x_ref, *refs):
    came_refs, (mods_ref, *w_ref, cos_ref, sin_ref, joined_ref, normed_ref) = refs[:-7], refs[-7:]
    half, part = pl.program_id(0), pl.program_id(1)
    width = x_ref.shape[1]

    @pl.when((half == 0) & (part == 0))
    def _():
        shift, scale = mods_ref[0:1, :width], mods_ref[0:1, width : 2 * width]
        for i in range(x_ref.shape[0] // CONT):
            cut = slice(i * CONT, (i + 1) * CONT)
            place = i * CONT
            for came_ref in came_refs:
                if 0 <= place < came_ref.shape[0]:
                    came = came_ref[place : place + CONT, :].astype(f32)
                place -= came_ref.shape[0]
            x = jnp.where(info[0] == 0, x_ref[cut, :].astype(f32), came)
            unit, _ = norm_parts(x)
            normed_ref[cut, :] = (unit * (1.0 + scale) + shift).astype(bf16)

    pl.when(part == 0)(lambda: fill(normed_ref, w_ref, joined_ref, (cos_ref, sin_ref)))
    pl.when(part == 1)(lambda: fill(normed_ref, w_ref, joined_ref, None))


def project(kernel, parts, estimate, info, inputs, mods, qkv, tables):
    count, width = inputs[0].shape
    head_width = qkv[0].shape[1] // 3

    def whole(array):
        return pl.BlockSpec(array.shape, lambda t, p, s: (0,) * array.ndim)

    def weight(half):
        def place(t, p, s):
            now = p + 3 - parts
            return (0, jnp.where(t == half, now, 2 if half == 0 else 3 - parts))

        return pl.BlockSpec((width, head_width), place)

    return pl.pallas_call(
        kernel,
        grid_spec=pltpu.PrefetchScalarGridSpec(
            num_scalar_prefetch=1,
            grid=(2, parts),
            in_specs=[whole(array) for array in inputs]
            + [whole(mods), weight(0), weight(1)]
            + [whole(table) for table in tables],
            out_specs=[
                pl.BlockSpec((1, count, head_width), lambda t, p, s: (t, 0, p)),
                whole(inputs[0]),
            ],
        ),
        out_shape=[
            jax.ShapeDtypeStruct((2, count, parts * head_width), bf16),
            jax.ShapeDtypeStruct((count, width), bf16),
        ],
        compiler_params=pltpu.CompilerParams(vmem_limit_bytes=20 * 2**20),
        cost_estimate=estimate,
        name="project",
    )(info, *inputs, mods, *qkv, *tables)


def middle_kernel(
    info, x_ref, a0_ref, a1_ref, mods_ref, o0_ref, o1_ref, branch_ref, middle_ref, n2_ref
):
    branch = dot(a0_ref[...], o0_ref[...], NT) + dot(a1_ref[...], o1_ref[...], NT)
    branch_ref[...] = branch
    per = x_ref.shape[0] // CONT
    for u in range(per):
        cut = slice(u * CONT, (u + 1) * CONT)
        gate, shift, scale = (
            modulation(mods_ref, info, pl.program_id(0) * per + u, n) for n in (2, 3, 4)
        )
        middle = x_ref[cut, :].astype(f32) + gate * branch[cut]
        middle_ref[cut, :] = middle
        unit, _ = norm_parts(middle)
        n2_ref[cut, :] = (unit * (1.0 + scale) + shift).astype(bf16)


def middle_norm(info, x, attended, mods, out_t):
    count, width = x.shape
    head_width = attended[0].shape[1]
    tile = 256
    by_row = pl.BlockSpec((tile, width), lambda i, s: (i, 0))
    by_head = pl.BlockSpec((tile, head_width), lambda i, s: (i, 0))
    return pl.pallas_call(
        middle_kernel,
        grid_spec=pltpu.PrefetchScalarGridSpec(
            num_scalar_prefetch=1,
            grid=(count // tile,),
            in_specs=[
                by_row,
                by_head,
                by_head,
                pl.BlockSpec(mods.shape, lambda i, s: (0, 0)),
                pl.BlockSpec((width, head_width), lambda i, s: (0, 0)),
                pl.BlockSpec((width, head_width), lambda i, s: (0, 0)),
            ],
            out_specs=[by_row] * 3,
        ),
        out_shape=[
            jax.ShapeDtypeStruct((count, width), f32),
            jax.ShapeDtypeStruct((count, width), f32),
            jax.ShapeDtypeStruct((count, width), bf16),
        ],
        compiler_params=pltpu.CompilerParams(vmem_limit_bytes=16 * 2**20),
        cost_estimate=LONG,
        name="middle_norm",
    )(info, x, *attended, mods, *out_t)


def mlp_kernel(first, info, n2_ref, *refs):
    if first:
        cot_ref, mods_ref = refs[:2]
        refs = refs[2:]
    else:
        n2_turned, out_grad, out_turned, branch_before, grad_before = refs[:5]
        refs = refs[5:]
    up_ref, down_ref, branch_ref, grad_ref = refs[:4]
    down_keep_ref, down_send_ref, up_keep_ref, up_send_ref = refs[4:8]
    if first:
        n2_turned, out_grad, out_turned = refs[8:11]
    hidden, pre_grad = refs[-2:]
    count = n2_ref.shape[0]

    @pl.when(pl.program_id(0) == 0)
    def _():
        if first:
            for i in range(count // CONT):
                cut = slice(i * CONT, (i + 1) * CONT)
                gate = modulation(mods_ref, info, i, 5)
                out_grad[cut, :] = (cot_ref[cut, :].astype(f32) * gate).astype(bf16)
            n2_turned[...] = jnp.transpose(n2_ref[...])
            out_turned[...] = jnp.transpose(out_grad[...])
            branch_ref[...] = jnp.zeros_like(branch_ref)
            grad_ref[...] = jnp.zeros_like(grad_ref)
        else:
            branch_ref[...] = branch_before[...]
            grad_ref[...] = grad_before[...]

    up, down = up_ref[...], down_ref[...]
    tile = 256
    for i in range(count // tile):
        cut = slice(i * tile, (i + 1) * tile)
        pre = dot(n2_ref[cut, :], up)
        cdf = 0.5 * (1.0 + lax.erf(pre * (2.0**-0.5)))
        pdf = jnp.exp(-0.5 * pre * pre) * ((2.0 * math.pi) ** -0.5)
        value = (pre * cdf).astype(bf16)
        hidden[cut, :] = value
        grad = (dot(out_grad[cut, :], down) * (cdf + pre * pdf)).astype(bf16)
        pre_grad[cut, :] = grad
        branch_ref[cut, :] += dot(value, down, NT)
        grad_ref[cut, :] += dot(grad, up, NT)
    store_pieces(dot(out_turned[...], hidden[...]), info, down_keep_ref, down_send_ref, ())
    store_pieces(dot(n2_turned[...], pre_grad[...]), info, up_keep_ref, up_send_ref, ())


def feed_forward(info, n2, sources, up, down):
    count, width = n2.shape
    hidden_width = up.shape[1]
    first = len(sources) == 2
    cols = 384
    dp_count = lax.axis_size("dp")
    pieces = (dp_count // 2, width // dp_count, hidden_width)

    def whole(array):
        return pl.BlockSpec(
            array.shape, lambda b, s: (0,) * array.ndim, pipeline_mode=pl.Buffered(1)
        )

    piece_spec = pl.BlockSpec(pieces[:2] + (cols,), lambda b, s: (0, 0, b))
    weight_spec = pl.BlockSpec((width, cols), lambda b, s: (0, b))
    outs = [jax.ShapeDtypeStruct((count, width), f32)] * 2 + [
        jax.ShapeDtypeStruct(pieces, bf16)
    ] * 4
    out_specs = [whole(n2)] * 2 + [piece_spec] * 4
    if first:
        shapes = [(width, count), (count, width), (width, count)]
        outs += [jax.ShapeDtypeStruct(shape, bf16) for shape in shapes]
        out_specs += [pl.BlockSpec(shape, lambda b, s: (0, 0)) for shape in shapes]
    return pl.pallas_call(
        lambda *refs: mlp_kernel(first, *refs),
        grid_spec=pltpu.PrefetchScalarGridSpec(
            num_scalar_prefetch=1,
            grid=(hidden_width // cols,),
            in_specs=[whole(n2)] + [whole(array) for array in sources] + [weight_spec] * 2,
            out_specs=out_specs,
            scratch_shapes=[pltpu.VMEM((count, cols), bf16), pltpu.VMEM((count, cols), bf16)],
        ),
        out_shape=outs,
        compiler_params=pltpu.CompilerParams(vmem_limit_bytes=32 * 2**20),
        cost_estimate=LONG,
        name="feed_forward",
    )(info, n2, *sources, up, down)


def post_kernel(
    info,
    middle_ref,
    branch_ref,
    mlp_ref,
    n2_grad_ref,
    cot_ref,
    a0_ref,
    a1_ref,
    mods_ref,
    o0_ref,
    o1_ref,
    out_ref,
    middle_grad_ref,
    g0_ref,
    g1_ref,
    sums_ref,
    keep_ref,
    send_ref,
    total,
    attn_grad,
):
    step = pl.program_id(0)
    per = middle_ref.shape[0] // CONT
    for u in range(per):
        cut = slice(u * CONT, (u + 1) * CONT)
        tile = step * per + u
        gate1, scale2, gate2 = (modulation(mods_ref, info, tile, n) for n in (2, 4, 5))
        middle, branch, mlp = middle_ref[cut, :], branch_ref[cut, :], mlp_ref[cut, :]
        n2_grad, upstream = n2_grad_ref[cut, :], cot_ref[cut, :].astype(f32)
        mlp_part, attn_part = gate2 * mlp, gate1 * branch
        result = middle + mlp_part
        out_ref[cut, :] = result.astype(bf16)
        unit, inverse = norm_parts(middle)
        middle_grad = upstream + norm_back(unit, inverse, n2_grad, scale2)
        middle_grad_ref[cut, :] = middle_grad
        attn_grad[cut, :] = (middle_grad * gate1).astype(bf16)
        valid = (rows((CONT, 1)) < info[2 + tile]).astype(f32)
        for n, value in enumerate(
            (
                middle_grad * branch,
                n2_grad,
                n2_grad * unit,
                upstream * mlp,
                valid * result * result,
                valid * attn_part * attn_part,
                valid * mlp_part * mlp_part,
            )
        ):
            sums_ref[u, n : n + 1, :] = jnp.sum(value, 0, keepdims=True)
        sums_ref[u, 7:8, :] = jnp.zeros_like(gate1)
    halves = ((a0_ref, g0_ref, o0_ref), (a1_ref, g1_ref, o1_ref))
    for t, (a_ref, g_ref, o_ref) in enumerate(halves):
        g_ref[...] = dot(attn_grad[...], o_ref[...]).astype(bf16)
        part = dot(attn_grad[...], a_ref[...], TN)
        total[t] = jnp.where(step == 0, part, total[t] + part)

    @pl.when(step == pl.num_programs(0) - 1)
    def _():
        for t in range(2):
            store_pieces(total[t], info, keep_ref, send_ref, (t,))


def post(info, middle, branch, mlp, n2_grad, cotangent, attended, mods, out_t):
    count, width = middle.shape
    head_width = attended[0].shape[1]
    tile = 256
    tiles = count // CONT
    dp_count = lax.axis_size("dp")
    pieces = (2, dp_count // 2, width // dp_count, head_width)
    by_row = pl.BlockSpec((tile, width), lambda i, s: (i, 0))
    by_head = pl.BlockSpec((tile, head_width), lambda i, s: (i, 0))
    return pl.pallas_call(
        post_kernel,
        grid_spec=pltpu.PrefetchScalarGridSpec(
            num_scalar_prefetch=1,
            grid=(count // tile,),
            in_specs=[by_row] * 5
            + [
                by_head,
                by_head,
                pl.BlockSpec(mods.shape, lambda i, s: (0, 0)),
                pl.BlockSpec((width, head_width), lambda i, s: (0, 0)),
                pl.BlockSpec((width, head_width), lambda i, s: (0, 0)),
            ],
            out_specs=[
                by_row,
                by_row,
                by_head,
                by_head,
                pl.BlockSpec((tile // CONT, 8, width), lambda i, s: (i, 0, 0)),
                pl.BlockSpec(pieces, lambda i, s: (0, 0, 0, 0)),
                pl.BlockSpec(pieces, lambda i, s: (0, 0, 0, 0)),
            ],
            scratch_shapes=[
                pltpu.VMEM((2, width, head_width), f32),
                pltpu.VMEM((tile, width), bf16),
            ],
        ),
        out_shape=[
            jax.ShapeDtypeStruct((count, width), bf16),
            jax.ShapeDtypeStruct((count, width), f32),
            jax.ShapeDtypeStruct((count, head_width), bf16),
            jax.ShapeDtypeStruct((count, head_width), bf16),
            jax.ShapeDtypeStruct((tiles, 8, width), f32),
            jax.ShapeDtypeStruct(pieces, bf16),
            jax.ShapeDtypeStruct(pieces, bf16),
        ],
        compiler_params=pltpu.CompilerParams(vmem_limit_bytes=32 * 2**20),
        cost_estimate=LONG,
        name="post",
    )(info, middle, branch, mlp, n2_grad, cotangent, *attended, mods, *out_t)


def last_kernel(
    info, x_ref, own_ref, prompt_ref, came_ref, middle_grad_ref, mods_ref, out_ref, sums_ref
):
    step = pl.program_id(0)
    per = x_ref.shape[0] // CONT
    for u in range(per):
        cut = slice(u * CONT, (u + 1) * CONT)
        scale = modulation(mods_ref, info, step * per + u, 1)
        prompt = prompt_ref[cut, :] + came_ref[cut, :].astype(f32)
        grad = own_ref[cut, :] + jnp.where(info[0] == 0, prompt, 0.0)
        unit, inverse = norm_parts(x_ref[cut, :].astype(f32))
        sums_ref[u, 0:1, :] = jnp.sum(grad, 0, keepdims=True)
        sums_ref[u, 1:2, :] = jnp.sum(grad * unit, 0, keepdims=True)
        sums_ref[u, 2:, :] = jnp.zeros((6, x_ref.shape[1]), f32)
        out_ref[cut, :] = middle_grad_ref[cut, :] + norm_back(unit, inverse, grad, scale)


def last(info, x, own_sum, prompt_sum, came, middle_grad, mods):
    count, width = x.shape
    tile = 256
    by_row = pl.BlockSpec((tile, width), lambda i, s: (i, 0))
    return pl.pallas_call(
        last_kernel,
        grid_spec=pltpu.PrefetchScalarGridSpec(
            num_scalar_prefetch=1,
            grid=(count // tile,),
            in_specs=[by_row] * 5 + [pl.BlockSpec(mods.shape, lambda i, s: (0, 0))],
            out_specs=[by_row, pl.BlockSpec((tile // CONT, 8, width), lambda i, s: (i, 0, 0))],
        ),
        out_shape=[
            jax.ShapeDtypeStruct((count, width), f32),
            jax.ShapeDtypeStruct((count // CONT, 8, width), f32),
        ],
        compiler_params=pltpu.CompilerParams(vmem_limit_bytes=16 * 2**20),
        cost_estimate=LONG,
        name="last",
    )(info, x, own_sum, prompt_sum, came, middle_grad, mods)


def forward_kernel(info, *refs):
    q_ref, kp_ref, vp_ref, ko_ref, vo_ref = (ref.at[0] for ref in refs[:5])
    o_ref, lse_ref = refs[5:]
    role = info[0]
    prompt_count = info[1]
    count = q_ref.shape[0]
    lane = lanes((count, 128))
    row = rows((count, 128))
    tile = 256
    blocks = count // tile

    def prepare(h):
        sel = (lane // 64) == h
        extra = 64 * (1 - h)
        q = jnp.where(sel, q_ref[...], jnp.where(lane == extra, 1.0, 0.0).astype(bf16))
        bias = jnp.where((lane == extra) & (row >= prompt_count), NEG, 0.0).astype(bf16)
        k = jnp.where(sel, kp_ref[...], bias)
        v = jnp.where(sel, vp_ref[...], jnp.ones((), bf16))
        return sel, q, k, v

    def finish(h, i, o, top):
        extra = 64 * (1 - h)
        weight = o[:, extra : extra + 1]
        lse = top * SCALE2 + jnp.log2(weight)
        turned = jnp.transpose(jnp.broadcast_to(lse, (tile, 128)))
        lse_ref[0, h : h + 1, i * tile : (i + 1) * tile] = turned[0:1, :]
        return o * (1.0 / weight)

    def store(outs):
        for i in range(blocks):
            merged = jnp.where(lanes((tile, 128)) < 64, outs[0][i], outs[1][i])
            o_ref[i * tile : (i + 1) * tile, :] = merged.astype(bf16)

    @pl.when(role == 0)
    def _():
        outs = []
        for h in range(2):
            sel, q, k, v = prepare(h)
            heads = []
            for i in range(blocks):
                start, stop = i * tile, (i + 1) * tile
                s = dot(q[start:stop], k[:stop], NT)
                near = jnp.where(lanes((tile, tile)) <= rows((tile, tile)), s[:, start:], NEG)
                top = jnp.max(near, 1, keepdims=True)
                if i:
                    top = jnp.maximum(top, jnp.max(s[:, :start], 1, keepdims=True))
                o = dot(jnp.exp2(near * SCALE2 - top * SCALE2).astype(bf16), v[start:stop])
                if i:
                    o = o + dot(
                        jnp.exp2(s[:, :start] * SCALE2 - top * SCALE2).astype(bf16), v[:start]
                    )
                heads.append(finish(h, i, o, top))
            outs.append(heads)
        store(outs)

    @pl.when(role != 0)
    def _():
        outs = []
        for h in range(2):
            sel, q, k, v = prepare(h)
            own_k = jnp.where(sel, ko_ref[...], jnp.zeros((), bf16))
            own_v = jnp.where(sel, vo_ref[...], jnp.ones((), bf16))
            heads, far, near, tops = [], [], [], []
            col, line = lanes((CONT, CONT)), rows((CONT, CONT))
            cuts = [slice(r, r + CONT) for r in range(0, count, CONT)]
            for n, cut in enumerate(cuts):
                fine = (col <= line) & (col < info[2 + n])
                near.append(jnp.where(fine, dot(q[cut], own_k[cut], NT), NEG))
            near = jnp.concatenate(near, 0)
            near_tops = jnp.max(near, 1, keepdims=True)
            for i in range(blocks):
                cut = slice(i * tile, (i + 1) * tile)
                s = dot(q[cut], k, NT)
                tops.append(jnp.maximum(jnp.max(s, 1, keepdims=True), near_tops[cut]))
                far.append(dot(jnp.exp2(s * SCALE2 - tops[i] * SCALE2).astype(bf16), v))
            weight = jnp.exp2(near * SCALE2 - jnp.concatenate(tops, 0) * SCALE2).astype(bf16)
            own = jnp.concatenate([dot(weight[cut], own_v[cut]) for cut in cuts], 0)
            for i in range(blocks):
                heads.append(finish(h, i, far[i] + own[i * tile : (i + 1) * tile], tops[i]))
            outs.append(heads)
        store(outs)


def attend(info, joined, prompts, t):
    count = joined.shape[1]
    head_width = joined.shape[2] // 3
    pairs = head_width // 128

    def spec(offset):
        return pl.BlockSpec((1, count, 128), lambda h, s: (t, 0, offset + h))

    return pl.pallas_call(
        forward_kernel,
        grid_spec=pltpu.PrefetchScalarGridSpec(
            num_scalar_prefetch=1,
            grid=(pairs,),
            in_specs=[spec(0), spec(0), spec(pairs), spec(pairs), spec(2 * pairs)],
            out_specs=[
                pl.BlockSpec((count, 128), lambda h, s: (0, h)),
                pl.BlockSpec((1, 2, count), lambda h, s: (h, 0, 0)),
            ],
        ),
        out_shape=[
            jax.ShapeDtypeStruct((count, head_width), bf16),
            jax.ShapeDtypeStruct((pairs, 2, count), f32),
        ],
        compiler_params=pltpu.CompilerParams(vmem_limit_bytes=20 * 2**20),
        cost_estimate=LONG,
        name="attend",
    )(info, joined, prompts, prompts, joined, joined)


def backward_kernel(first, last, tiles, own, info, *refs):
    refs = list(refs)
    q_ref, do_ref, o_ref, lse_ref = refs[0].at[0], *refs[1:4]
    del refs[:4]
    if tiles:
        kp_ref, vp_ref, cp_ref, sp_ref = refs[0].at[0], refs[1].at[0], *refs[2:4]
        del refs[:4]
    if own:
        ko_ref, vo_ref = refs[0].at[0], refs[1].at[0]
        del refs[:2]
    if own or last:
        co_ref, so_ref = refs[:2]
        del refs[:2]
    before_ref = None if first else refs.pop(0)
    dq_ref = refs.pop(0)
    if tiles:
        dkp_ref, dvp_ref = refs[:2]
        del refs[:2]
    if own:
        dko_ref, dvo_ref = refs[:2]
        del refs[:2]
    (dq_acc,) = refs
    role = info[0]
    prompt_count = info[1]
    count = q_ref.shape[0]
    tile = 256
    lane = lanes((count, 128))
    none = jnp.zeros((), bf16)
    products = jnp.transpose(do_ref[...].astype(f32) * o_ref[...].astype(f32))
    deltas = [jnp.sum(products[64 * h : 64 * h + 64], 0, keepdims=True) for h in range(2)]
    dq_acc[...] = jnp.zeros_like(dq_acc) if first else before_ref[...]

    def far_block(j, prompt):
        start, stop = j * tile, (j + 1) * tile
        cut = slice(start - tiles[0] * tile, stop - tiles[0] * tile)
        q_from = start if prompt else 0
        lane_k = lanes((tile, 128))
        row_k = rows((tile, 128)) + start
        key_parts, value_parts = [], []
        for h in range(2):
            extra = 64 * (1 - h)
            sel = (lane_k // 64) == h
            bias = jnp.where((lane_k == extra) & (row_k >= prompt_count), NEG, 0.0).astype(bf16)
            k = jnp.where(sel, kp_ref[cut, :], bias)
            k_plain = jnp.where(sel, kp_ref[cut, :], none)
            v = jnp.where(sel, vp_ref[cut, :], none)
            lane_q = lane[q_from:]
            ones = jnp.where(lane_q == extra, 1.0, 0.0).astype(bf16)
            q = jnp.where((lane_q // 64) == h, q_ref[q_from:, :], ones)
            s = dot(k, q, NT)
            if prompt:
                near = jnp.where(rows((tile, tile)) <= lanes((tile, tile)), s[:, :tile], NEG)
                s = jnp.concatenate([near, s[:, tile:]], 1) if stop < count else near
            weight = jnp.exp2(s * SCALE2 - lse_ref[0, h : h + 1, q_from:])
            grad = dot(v, do_ref[q_from:, :], NT)
            score = (weight * (grad - deltas[h][:, q_from:])).astype(bf16)
            value_parts.append(dot(weight.astype(bf16), do_ref[q_from:, :]))
            key_parts.append(dot(score, q_ref[q_from:, :]))
            dq_acc[q_from:, :] += dot(score, k_plain, TN)
        key_grad = jnp.where(lane_k < 64, key_parts[0], key_parts[1]) * SCALE
        value_grad = jnp.where(lane_k < 64, value_parts[0], value_parts[1])
        dkp_ref[cut, :] = turn_back(key_grad, cp_ref[cut, :], sp_ref[cut, :]).astype(bf16)
        dvp_ref[cut, :] = value_grad.astype(bf16)

    @pl.when(role == 0)
    def _():
        for j in tiles:
            far_block(j, True)
        if own:
            dko_ref[...] = jnp.zeros_like(dko_ref)
            dvo_ref[...] = jnp.zeros_like(dvo_ref)

    @pl.when(role != 0)
    def _():
        for j in tiles:
            far_block(j, False)
        lane_k = lanes((CONT, CONT))
        row_k = rows((CONT, CONT))
        every = range(count // CONT if own else 0)
        cuts = [slice(i * CONT, (i + 1) * CONT) for i in every]
        key_parts, value_parts = [], []
        for h in range(2 if own else 0):
            sel = (lane // 64) == h
            k = jnp.where(sel, ko_ref[...], none)
            v = jnp.where(sel, vo_ref[...], none)
            scores, weights = [], []
            for i, cut in enumerate(cuts):
                fine = (row_k <= lane_k) & (row_k < info[2 + i])
                scores.append(jnp.where(fine, dot(k[cut], q_ref[cut, :], NT), NEG) * SCALE2 - lse_ref[0, h : h + 1, cut])
            weight = jnp.exp2(jnp.concatenate(scores, 0))
            grad = jnp.concatenate([dot(v[cut], do_ref[cut, :], NT) - deltas[h][:, cut] for cut in cuts], 0)
            score = (weight * grad).astype(bf16)
            weight = weight.astype(bf16)
            value_parts.append([dot(weight[cut], do_ref[cut, :]) for cut in cuts])
            key_parts.append([dot(score[cut], q_ref[cut, :]) for cut in cuts])
            for cut in cuts:
                dq_acc[cut, :] += dot(score[cut], k[cut], TN)
        for i, cut in enumerate(cuts):
            key_grad = jnp.where(lane_k < 64, key_parts[0][i], key_parts[1][i]) * SCALE
            value_grad = jnp.where(lane_k < 64, value_parts[0][i], value_parts[1][i])
            dko_ref[cut, :] = turn_back(key_grad, co_ref[cut, :], so_ref[cut, :]).astype(bf16)
            dvo_ref[cut, :] = value_grad.astype(bf16)

    if last:
        dq_ref[...] = turn_back(dq_acc[...] * SCALE, co_ref[...], so_ref[...]).astype(bf16)
    else:
        dq_ref[...] = dq_acc[...]


def attend_back(info, joined, prompts, t, grad, out, lse, tables, tiles, own, before=None, last=True):
    count = joined.shape[1]
    head_width = joined.shape[2] // 3
    pairs = head_width // 128
    first = before is None
    part = 256 * len(tiles)

    def half_spec(offset):
        return pl.BlockSpec((1, count, 128), lambda h, s: (t, 0, offset + h))

    def part_spec(offset):
        return pl.BlockSpec((1, part, 128), lambda h, s: (t, tiles[0] * 256 // part, offset + h))

    rows_spec = pl.BlockSpec((count, 128), lambda h, s: (0, h))
    whole = pl.BlockSpec((count, 128), lambda h, s: (0, 0))
    args = [joined, grad, out, lse]
    specs = [
        half_spec(0),
        rows_spec,
        rows_spec,
        pl.BlockSpec((1, 2, count), lambda h, s: (h, 0, 0)),
    ]
    outs = [jax.ShapeDtypeStruct((count, head_width), bf16 if last else f32)]
    out_specs = [rows_spec]
    if tiles:
        args += [prompts, prompts, tables[2], tables[3]]
        part_table = pl.BlockSpec((part, 128), lambda h, s: (tiles[0] * 256 // part, 0))
        specs += [part_spec(0), part_spec(pairs), part_table, part_table]
        outs += [jax.ShapeDtypeStruct((part, head_width), bf16)] * 2
        out_specs += [pl.BlockSpec((part, 128), lambda h, s: (0, h))] * 2
    if own:
        args += [joined, joined]
        specs += [half_spec(pairs), half_spec(2 * pairs)]
        outs += [jax.ShapeDtypeStruct((count, head_width), bf16)] * 2
        out_specs += [rows_spec] * 2
    if own or last:
        args += [tables[0], tables[1]]
        specs += [whole, whole]
    if not first:
        args += [before]
        specs += [rows_spec]
    return pl.pallas_call(
        lambda *refs: backward_kernel(first, last, tiles, own, *refs),
        grid_spec=pltpu.PrefetchScalarGridSpec(
            num_scalar_prefetch=1,
            grid=(pairs,),
            in_specs=specs,
            out_specs=out_specs,
            scratch_shapes=[pltpu.VMEM((count, 128), f32)],
        ),
        out_shape=outs,
        compiler_params=pltpu.CompilerParams(vmem_limit_bytes=20 * 2**20),
        cost_estimate=LONG,
        name="attend_back",
    )(info, *args)


def split_three(values):
    high = lax.reduce_precision(values, 8, 7)
    rest = values - high
    mid = lax.reduce_precision(rest, 8, 7)
    return high, mid, rest - mid


def pick(x, index, axis):
    return lax.dynamic_index_in_dim(x, index, axis, keepdims=False)


def body(
    block_input,
    cotangent,
    w_qkv,
    w_out,
    w_up,
    w_down,
    w_mod,
    time_table,
    prompt_len,
    cont_len,
    timestep,
):
    count, width = block_input.shape
    tiles = count // CONT
    dp_count = lax.axis_size("dp")
    tensor_count = lax.axis_size("tensor")
    devices = dp_count * tensor_count
    role = lax.axis_index("tensor")
    is_prompt = role == 0
    me = lax.axis_index("dp")
    core, near, far = me % 2, (me // 2) % 2, me // 4
    fars = far_count()
    low_bits = far_bits()
    high_bits = list(reversed(low_bits))
    head_width = w_qkv.shape[2]
    half = count // 2

    def far_bit(bit):
        return (far // bit) % 2

    far_top, far_rest = high_bits[0], high_bits[1:]
    cuts = (head_width, w_up.shape[1], w_down.shape[0])
    table_rows, rows_each = time_table.shape[0], w_qkv.shape[0]
    steps = jnp.pad(timestep.reshape(1, -1), ((0, rows_each - 1), (0, 128 - SEGS))).astype(bf16)
    table_width = table_rows * width // rows_each
    table_width += -table_width % 128
    table_part = time_table.reshape(-1)
    table_part = jnp.pad(table_part, (0, rows_each * table_width - table_part.shape[0]))
    table_part = table_part.reshape(rows_each, table_width)
    first = [w_qkv.reshape(rows_each, -1), table_part, steps]
    first_cuts = (first[0].shape[1], table_width + 128)
    first = jnp.concatenate(first, 1)[None]
    bounds = [0, count // 4, count * 5 // 8, count]
    x_parts = [block_input[bounds[n] : bounds[n + 1]] for n in range(3)]
    rest = jnp.concatenate([w_out.T, w_up, w_down.T], 1)[None]
    came_first = swap(first, 8 * far_top)
    first, came_first, x_parts, rest = tie(first, came_first, x_parts, rest)
    came = [swap(x_parts[0], TENSOR)]
    for bit in far_rest:
        first = join(first, came_first, far_bit(2 * bit))
        came_first = swap(first, 8 * bit)
    came_first, first, came, rest = tie(came_first, first, came, rest)
    qkv_far, table_far = join(first, came_first, far_bit(1), first_cuts)

    table_near = [swap(table_far, bits) for bits in (NEAR, TENSOR, NEAR + TENSOR)]
    qkv_near = [swap(qkv_far, bits) for bits in (NEAR, TENSOR)]
    table_own = join(table_far, table_near[0], near)
    table_other = join(table_near[1], table_near[2], near)
    table_came = [swap(table_own, CORE), swap(table_other, CORE)]
    table_cuts = (table_width, 128)
    packets = [
        join(table_own, table_came[0], core, table_cuts),
        join(table_other, table_came[1], core, table_cuts),
    ]
    rest_came = swap(rest, 8 * far_top)

    turns = HEAD_DIM // 2
    freqs = 10000.0 ** (-(jnp.arange(128, dtype=jnp.int32) % turns).astype(f32) / turns)
    inside = jnp.arange(count, dtype=jnp.int32)
    prompt_count = prompt_len[0]
    own_places = jnp.where(is_prompt, inside, prompt_count + inside % CONT).astype(f32)
    own_angles = own_places[:, None] * freqs[None, :]
    prompt_angles = inside.astype(f32)[:, None] * freqs[None, :]
    tables = (jnp.cos(own_angles), jnp.sin(own_angles), jnp.cos(prompt_angles), jnp.sin(prompt_angles))
    own_len = jnp.where(
        is_prompt,
        jnp.clip(prompt_count - CONT * jnp.arange(NCONT, dtype=jnp.int32), 0, CONT),
        cont_len[0],
    )
    info = jnp.concatenate(
        [jnp.stack([role, prompt_count]), own_len, jnp.stack([core, near, far])]
    ).astype(jnp.int32)

    table_full = jnp.concatenate([packets[0][0], packets[1][0]], 0)
    table_full = table_full.reshape(2 * dp_count, -1)[:, : table_rows * width]
    table_full = table_full.reshape(STEPS, width)
    step_rows = packets[0][1][:, 0, :SEGS].astype(jnp.int32)
    row_ids = (jnp.arange(2)[:, None, None] + role) % 2 * table_rows + (
        jnp.arange(dp_count)[None, :, None] * 2 * table_rows + jnp.arange(table_rows)
    )
    row_ids = row_ids.reshape(-1).astype(jnp.int32)
    step_pad = jnp.pad(step_rows, ((0, 0), (0, 16 - SEGS))).reshape(-1)
    chosen = (step_pad[:, None] == row_ids[None, :]).astype(bf16)
    cond = dot(chosen, table_full).astype(bf16)
    col_width = w_mod.shape[1]
    col_part = dot(cond, w_mod).reshape(dp_count, 1, 16, col_width)
    col_part = jnp.broadcast_to(col_part, (dp_count, tensor_count, 16, col_width))
    col_part = col_part.reshape(devices, 16, col_width).astype(f32)
    arrived = lax.all_to_all(col_part, BOTH, 0, 0, tiled=True)
    qkv_far, qkv_near, rest, rest_came, tables, info, _ = tie(
        qkv_far, qkv_near, rest, rest_came, tables, info, col_part
    )
    qkv_near.append(swap(qkv_far, NEAR + TENSOR))
    rest = join(rest, rest_came, far_bit(far_top), None if far_rest else cuts)
    if far_rest:
        rest_came = swap(rest, 8 * far_rest[0])

    qkv_far, qkv_near, arrived, came, x_parts = tie(qkv_far, qkv_near, arrived, came, x_parts)
    came.append(swap(x_parts[1], TENSOR))
    mods = jnp.transpose(arrived, (1, 0, 2)).reshape(16, 6 * width).astype(f32)
    qkv_own = join(qkv_far, qkv_near[0], near)
    qkv_other = join(qkv_near[1], qkv_near[2], near)
    qkv_came = [swap(qkv_own, CORE), swap(qkv_other, CORE)]
    for bit in far_rest[1:]:
        rest = join(rest, rest_came, far_bit(bit * 2))
        rest_came = swap(rest, 8 * bit)
    qkv = [
        join(own, other, core).reshape(width, -1)
        for own, other in zip((qkv_own, qkv_other), qkv_came)
    ]
    rest, rest_came, mods, qkv, came, x_parts = tie(rest, rest_came, mods, qkv, came, x_parts)

    came.append(swap(x_parts[2], TENSOR))
    o_own, u_own, d_own = join(rest, rest_came, far_bit(1), cuts) if far_rest else rest
    u_near, o_near, o_other = swap(u_own, NEAR), swap(o_own, NEAR), swap(o_own, TENSOR)
    joined, normed = project(
        project_own_kernel, 3, LONG, info, [block_input], mods, qkv, tables[:2]
    )
    came, joined, u_near = tie(came, joined, u_near)
    prompts, prompt_normed = project(
        project_prompt_kernel, 2, LONG, info, [block_input, *came], mods, qkv, tables[2:]
    )
    u_near, o_near, o_other, u_own, o_own, d_own, prompts = tie(
        u_near, o_near, o_other, u_own, o_own, d_own, prompts
    )
    d_near, u_other, oo_near = swap(d_own, NEAR), swap(u_own, TENSOR), swap(o_other, NEAR)
    u_own, o_own = join(u_own, u_near, near), join(o_own, o_near, near)
    u_core = swap(u_own, CORE)
    out_0, lse_0 = attend(info, *tie(joined, prompts, u_own, o_own)[:2], 0)
    d_near, u_other, oo_near, u_core, d_own, u_own, o_own, o_other, out_0, joined = tie(
        d_near, u_other, oo_near, u_core, d_own, u_own, o_own, o_other, out_0, joined
    )
    d_other, uu_near = swap(d_own, TENSOR), swap(u_other, NEAR)
    d_own, o_other = join(d_own, d_near, near), join(o_other, oo_near, near)
    d_core, o_core, oo_core = swap(d_own, CORE), swap(o_own, CORE), swap(o_other, CORE)
    up_0 = join(u_own, u_core, core).reshape(width, -1)
    out_1, lse_1 = attend(info, *tie(joined, prompts, d_own, o_other, up_0)[:2], 1)
    d_other, uu_near, d_core, o_core, oo_core, d_own, o_own, o_other, u_other, out_1 = tie(
        d_other, uu_near, d_core, o_core, oo_core, d_own, o_own, o_other, u_other, out_1
    )
    attended, lses = [out_0, out_1], [lse_0, lse_1]
    out_t = [
        join(o_own, o_core, core).reshape(width, -1),
        join(o_other, oo_core, core).reshape(width, -1),
    ]
    branch, middle, normed_two = middle_norm(info, block_input, attended, mods, out_t)

    dd_near = swap(d_other, NEAR)
    u_other = join(u_other, uu_near, near)
    uu_core = swap(u_other, CORE)
    down_0 = join(d_own, d_core, core).reshape(width, -1)
    d_other, u_other, normed_two, down_0 = tie(d_other, u_other, normed_two, down_0)
    mlp, n2_grad, d_keep_0, d_send_0, u_keep_0, u_send_0, *shared = feed_forward(
        info, normed_two, (cotangent, mods), up_0, down_0
    )
    dd_near, uu_core, d_other, u_other, mlp, d_send_0, u_send_0 = tie(
        dd_near, uu_core, d_other, u_other, mlp, d_send_0, u_send_0
    )
    d_other = join(d_other, dd_near, near)
    dd_core = swap(d_other, CORE)
    up_1 = join(u_other, uu_core, core).reshape(width, -1)
    down_1 = join(d_other, dd_core, core).reshape(width, -1)
    up_1, down_1, mlp, d_send_0, u_send_0 = tie(up_1, down_1, mlp, d_send_0, u_send_0)
    d_came_0, u_came_0 = swap(d_send_0, CORE), swap(u_send_0, CORE)
    mlp, n2_grad, d_keep_1, d_send_1, u_keep_1, u_send_1 = feed_forward(
        info, normed_two, (*shared, mlp, n2_grad), up_1, down_1
    )
    d_came_0, u_came_0, mlp, d_send_1, u_send_1 = tie(d_came_0, u_came_0, mlp, d_send_1, u_send_1)
    d_came_1, u_came_1 = swap(d_send_1, CORE), swap(u_send_1, CORE)
    block_output, middle_grad, grad_0, grad_1, post_sums, o_keep, o_send = post(
        info, middle, branch, mlp, n2_grad, cotangent, attended, mods, out_t
    )
    d_came_1, u_came_1, o_keep, o_send, grad_0, grad_1 = tie(
        d_came_1, u_came_1, o_keep, o_send, grad_0, grad_1
    )

    def by_near(x):
        return x.reshape((2, 2, fars) + x.shape[2:])

    def near_part(keep, came, part):
        half_of = slice(part * fars, (part + 1) * fars)
        return plus(keep[half_of], came[half_of])

    o_came = swap(o_send, CORE)
    d_send = [near_part(d_keep_0, d_came_0, 1), near_part(d_keep_1, d_came_1, 1)]
    d_keep = [near_part(d_keep_0, d_came_0, 0), near_part(d_keep_1, d_came_1, 0)]
    u_send, u_keep = plus(u_keep_1, u_came_1), plus(u_keep_0, u_came_0)
    d_came, u_came = swap(jnp.stack(d_send), NEAR), swap(u_send, TENSOR)
    d_keep, u_keep, grad_1 = tie(d_keep, u_keep, grad_1)

    def back(t, grad, blocks, own, before=None, last=True):
        return attend_back(
            info, joined, prompts, t, grad, attended[t], lses[t], tables, blocks, own, before, last
        )

    wq, wk, wv = (
        [qkv[t][:, n * head_width : (n + 1) * head_width] for t in range(2)] for n in range(3)
    )

    def prompt_part(t, dk, dv):
        return dot(dk, wk[t], NT) + dot(dv, wv[t], NT)

    def own_part(t, dq, dk, dv):
        return dot(dq, wq[t], NT) + dot(dk, wk[t], NT) + dot(dv, wv[t], NT)

    def weight_part(dq, dk, dv, dk_prompt, dv_prompt):
        parts = [
            dot(normed, dq, TN),
            dot(normed, dk, TN) + dot(prompt_normed, dk_prompt, TN),
            dot(normed, dv, TN) + dot(prompt_normed, dv_prompt, TN),
        ]
        whole = jnp.concatenate(parts, 1).astype(bf16)
        return whole.reshape(fars, 2, 2, -1, whole.shape[1])

    dq_1, dkp_1, dvp_1, dk_1, dv_1 = back(1, grad_1, (0, 1, 2, 3), True)
    d_came, u_came, o_came, d_keep, u_keep, o_keep, grad_0, dq_1, dkp_1, dvp_1, dk_1, dv_1 = tie(
        d_came, u_came, o_came, d_keep, u_keep, o_keep, grad_0, dq_1, dkp_1, dvp_1, dk_1, dv_1
    )
    o_cur = by_near(plus(o_keep, o_came))
    d_keep, d_send = plus(d_keep[0], d_came[0]), plus(d_keep[1], d_came[1])
    u_keep, u_send = near_part(u_keep, u_came, 0), near_part(u_keep, u_came, 1)
    d_came, u_came = swap(d_send, TENSOR), swap(u_send, NEAR)
    o_came = swap(o_cur[:, 1], NEAR)
    o_keep = o_cur[:, 0]
    q_cur = weight_part(dq_1, dk_1, dv_1, dkp_1, dvp_1)
    q_came = swap(pick(q_cur, 1 - core, 2), CORE)
    q_keep = pick(q_cur, core, 2)
    own_sum = own_part(1, dq_1, dk_1, dv_1)
    prompt_sum = prompt_part(1, dkp_1, dvp_1)
    q_keep, own_sum, prompt_sum, grad_0, d_keep, u_keep, o_keep = tie(
        q_keep, own_sum, prompt_sum, grad_0, d_keep, u_keep, o_keep
    )

    dq_0, dkp_a, dvp_a = back(0, grad_0, (0, 1), False, None, False)
    q_came, d_came, u_came, o_came, q_keep, d_keep, u_keep, o_keep, dq_0, dkp_a, dvp_a = tie(
        q_came, d_came, u_came, o_came, q_keep, d_keep, u_keep, o_keep, dq_0, dkp_a, dvp_a
    )
    sum_a = prompt_sum[:half] + prompt_part(0, dkp_a, dvp_a)
    came_a = swap(sum_a.astype(bf16), TENSOR)
    d_keep, d_send = send_far(plus(d_keep, d_came))
    u_keep, u_send = send_far(plus(u_keep, u_came))
    o_cur = plus(o_keep, o_came)
    q_cur = plus(q_keep, q_came)
    d_came, u_came = swap(d_send, 8), swap(u_send, 8)
    o_came, o_keep = swap(o_cur[1], TENSOR), o_cur[0]
    q_came, q_keep = swap(pick(q_cur, 1 - near, 1), NEAR), pick(q_cur, near, 1)
    sum_a, d_keep, u_keep, o_keep, q_keep, dq_0 = tie(sum_a, d_keep, u_keep, o_keep, q_keep, dq_0)

    dq_0, dkp_b, dvp_b = back(0, grad_0, (2, 3), False, dq_0, False)
    came, keep, grads = tie(
        (came_a, d_came, u_came, o_came, q_came),
        (d_keep, u_keep, o_keep, q_keep),
        (dkp_b, dvp_b, dq_0),
    )
    came_a, d_came, u_came, o_came, q_came = came
    d_keep, u_keep, o_keep, q_keep = keep
    dkp_b, dvp_b, dq_0 = grads
    sum_b = prompt_sum[half:] + prompt_part(0, dkp_b, dvp_b)
    came_b = swap(sum_b.astype(bf16), TENSOR)

    def far_end(keep, came):
        for bit in low_bits[1:]:
            keep, send = send_far(plus(keep, came))
            came = swap(send, 8 * bit)
        return keep, came

    d_keep, d_came = far_end(d_keep, d_came)
    u_keep, u_came = far_end(u_keep, u_came)
    o_keep, o_send = send_far(plus(o_keep, o_came))
    o_came = swap(o_send, 8)
    q_send = plus(q_keep, q_came)
    q_send, sum_b, dq_0 = tie(q_send, sum_b, dq_0)
    dq_0, dk_0, dv_0 = back(0, grad_0, (), True, dq_0, True)
    came, keep, grads = tie(
        (d_came, u_came, o_came), (d_keep, u_keep, o_keep), (dq_0, dk_0, dv_0, q_send)
    )
    d_came, u_came, o_came = came
    d_keep, u_keep, o_keep = keep
    dq_0, dk_0, dv_0, q_send = grads
    dkp_0, dvp_0 = jnp.concatenate([dkp_a, dkp_b], 0), jnp.concatenate([dvp_a, dvp_b], 0)
    q_cur = weight_part(dq_0, dk_0, dv_0, dkp_0, dvp_0)
    q_came, q_keep = swap(pick(q_cur, 1 - core, 2), CORE), pick(q_cur, core, 2)
    own_sum = own_sum + own_part(0, dq_0, dk_0, dv_0)
    q_came, q_keep, own_sum, q_send = tie(q_came, q_keep, own_sum, q_send)
    q_cur = plus(q_keep, q_came)
    q_came, q_keep = swap(pick(q_cur, 1 - near, 1), NEAR), pick(q_cur, near, 1)
    q_keep, own_sum, came_b, q_send = tie(q_keep, own_sum, came_b, q_send)
    q_other = swap(q_send, TENSOR)
    input_grad, last_sums = last(
        info,
        block_input,
        own_sum,
        jnp.concatenate([sum_a, sum_b], 0),
        jnp.concatenate([came_a, came_b], 0),
        middle_grad,
        mods,
    )
    last_sums, d_keep, u_keep = tie(last_sums, d_keep, u_keep)
    down_grad = (d_keep.astype(f32) + d_came.astype(f32))[0]
    up_grad = (u_keep.astype(f32) + u_came.astype(f32))[0]
    o_keep, o_came = far_end(o_keep, o_came)
    out_grad = (o_keep.astype(f32) + o_came.astype(f32))[0]
    order = [last_sums[:, 0], last_sums[:, 1]] + [post_sums[:, n] for n in range(4)]
    sums = jnp.stack(order, 1).reshape(tiles, 6 * width)
    first_row = (jnp.arange(tiles) == 0)[:, None]
    prompt_sums = jnp.where(first_row, jnp.sum(sums, 0, keepdims=True), 0.0)
    segment_sums = jnp.where(is_prompt, prompt_sums, sums).astype(bf16)

    local = jnp.concatenate(
        [
            jnp.sum(post_sums[:, 4:7], (0, 2)),
            (jnp.sum(own_len) * width).astype(f32).reshape(1),
        ]
    )
    local = jnp.concatenate(split_three(local))
    local = jnp.pad(local, (0, col_width - 12)).astype(bf16)
    packet = segment_sums.reshape(tiles, devices, col_width).transpose(1, 0, 2)
    packet = jnp.concatenate(
        [packet, jnp.broadcast_to(local[None, None], (devices, 1, col_width))], 1
    )
    packet = jnp.pad(packet, ((0, 0), (0, 16 - packet.shape[1]), (0, 0)))
    packets = lax.all_to_all(packet, BOTH, 0, 0, tiled=True)
    q_keep = after(q_keep, packet)
    q_cur = q_keep.astype(f32) + q_came.astype(f32) + q_other.astype(f32)
    q_cur = q_cur.reshape((2,) * len(low_bits) + q_cur.shape[1:])

    def q_step(cur, bit):
        mine = (far // bit) % 2
        cur = cur.astype(bf16)
        return pick(cur, mine, cur.ndim - 3), swap(pick(cur, 1 - mine, cur.ndim - 3), 8 * bit)

    q_keep, q_came = q_step(q_cur, low_bits[0])
    totals = jnp.sum(packets[:, tiles, :12].astype(f32), 0)
    totals = totals[:4] + totals[4:8] + totals[8:12]
    stats = jnp.sqrt(totals[:3] / totals[3])

    grads = packets[:, :tiles].reshape(devices * tiles, col_width)
    cond_groups = cond.reshape(dp_count, 16, width)
    own_steps = step_pad.reshape(dp_count, 16)
    cond_rows = jnp.stack([cond_groups[:, :tiles], cond_groups[:, 1 : 1 + tiles]], 1)
    step_slots = jnp.stack([own_steps[:, :tiles], own_steps[:, 1 : 1 + tiles]], 1).reshape(-1)
    mod_grad = dot(cond_rows.reshape(devices * tiles, width), grads, TN)
    condition_grad = dot(grads, w_mod, NT)
    slot_pick = (step_slots[:, None] == jnp.arange(STEPS, dtype=jnp.int32)[None, :]).astype(f32)
    table_part = lax.dot_general(
        slot_pick,
        condition_grad,
        TN,
        precision=lax.Precision.HIGHEST,
        preferred_element_type=f32,
    )
    table_pieces = lax.all_to_all(
        table_part.astype(bf16).reshape(devices, table_rows, width), BOTH, 0, 0, tiled=True
    )
    table_grad = jnp.sum(table_pieces.astype(f32), 0)
    q_keep = after(q_keep, table_part)
    q_cur = q_keep.astype(f32) + q_came.astype(f32)
    for bit in low_bits[1:]:
        q_keep, q_came = q_step(q_cur, bit)
        q_cur = q_keep.astype(f32) + q_came.astype(f32)
    return (
        block_output,
        input_grad,
        q_cur.reshape(w_qkv.shape),
        out_grad.T,
        up_grad,
        down_grad.T,
        mod_grad,
        table_grad,
        stats,
    )


def solution(mesh):
    return jax.shard_map(
        body,
        mesh=mesh,
        in_specs=(
            P(("dp", "tensor"), None),
            P(("dp", "tensor"), None),
            P("dp", None, "tensor"),
            P("tensor", "dp"),
            P("dp", "tensor"),
            P("tensor", "dp"),
            P(None, ("dp", "tensor")),
            P(("dp", "tensor"), None),
            P("dp"),
            P("dp", None),
            P("dp", None),
        ),
        out_specs=(
            P(("dp", "tensor"), None),
            P(("dp", "tensor"), None),
            P("dp", None, "tensor"),
            P("tensor", "dp"),
            P("dp", "tensor"),
            P("tensor", "dp"),
            P(None, ("dp", "tensor")),
            P(("dp", "tensor"), None),
            P(),
        ),
        check_vma=False,
    )
```

```python
import math

import jax
import jax.numpy as jnp
from jax import lax
from jax.experimental import pallas as pl
from jax.experimental.pallas import tpu as pltpu
from jax.sharding import PartitionSpec as P

HEAD_DIM = 64
PROMPT = 1024
CONT = 128
NCONT = 8
STEPS = 256
SEGS = 1 + NCONT

bf16 = jnp.bfloat16
f32 = jnp.float32
NN = (((1,), (0,)), ((), ()))
NT = (((1,), (1,)), ((), ()))
TN = (((0,), (0,)), ((), ()))
SCALE = HEAD_DIM ** (-0.5)
SCALE2 = SCALE * math.log2(math.e)
NEG = -1e30


def dot(left, right, dims=NN):
    return lax.dot_general(left, right, dims, preferred_element_type=f32)


def lanes(shape):
    return lax.broadcasted_iota(jnp.int32, shape, 1)


def rows(shape):
    return lax.broadcasted_iota(jnp.int32, shape, 0)


BOTH = ("dp", "tensor")
TENSOR, CORE, NEAR = 1, 2, 4
LONG = pl.CostEstimate(flops=10**11, bytes_accessed=1, transcendentals=0)


def swap(x, bits):
    count = lax.axis_size(BOTH)
    return lax.ppermute(x, BOTH, [(i, i ^ bits) for i in range(count)])


def tie(*arrays):
    return lax.optimization_barrier(arrays)


def after(array, *others):
    return lax.optimization_barrier((array,) + others)[0]


def far_count():
    return lax.axis_size("dp") // 4


def far_bits():
    return [1 << k for k in range(far_count().bit_length() - 1)]


def plus(left, right):
    return (left.astype(f32) + right.astype(f32)).astype(bf16)


def send_far(cur):
    cur = cur.reshape((-1, 2) + cur.shape[1:])
    return cur[:, 0], cur[:, 1]


def join_kernel(cuts, bit_ref, own_ref, came_ref, *out_refs):
    bit = bit_ref[0]
    start = 0
    for out_ref, cut in zip(out_refs, cuts):
        for n in range(own_ref.shape[0]):
            out_ref[n, bit] = own_ref[n, :, start : start + cut]
            out_ref[n, 1 - bit] = came_ref[n, :, start : start + cut]
        start += cut


def join(own, came, bit, cuts=None):
    count, rows_each, columns = own.shape
    sizes = cuts or (columns,)
    group = min(count, 2)
    spec = pl.BlockSpec((group, rows_each, columns), lambda n, s: (n, 0, 0))
    outs = pl.pallas_call(
        lambda *refs: join_kernel(sizes, *refs),
        grid_spec=pltpu.PrefetchScalarGridSpec(
            num_scalar_prefetch=1,
            grid=(count // group,),
            in_specs=[spec, spec],
            out_specs=[
                pl.BlockSpec((group, 2, rows_each, cut), lambda n, s: (n, 0, 0, 0)) for cut in sizes
            ],
        ),
        out_shape=[jax.ShapeDtypeStruct((count, 2, rows_each, cut), bf16) for cut in sizes],
        cost_estimate=pl.CostEstimate(flops=1, bytes_accessed=10**6, transcendentals=0),
        compiler_params=pltpu.CompilerParams(vmem_limit_bytes=16 * 2**20),
        name="join",
    )(bit.astype(jnp.int32).reshape(1), own, came)
    outs = [out.reshape(2 * count, rows_each, -1) for out in outs]
    return outs if cuts else outs[0]


def turn(x, cosine, sine):
    lane = lanes(x.shape) % 64
    swapped = jnp.where(lane < 32, -pltpu.roll(x, 96, 1), pltpu.roll(x, 32, 1))
    return x * cosine + swapped * sine


def turn_back(x, cosine, sine):
    lane = lanes(x.shape) % 64
    swapped = jnp.where(lane < 32, pltpu.roll(x, 96, 1), -pltpu.roll(x, 32, 1))
    return x * cosine + swapped * sine


def norm_parts(inputs):
    average = jnp.mean(inputs, -1, keepdims=True)
    centred = inputs - average
    spread = jnp.mean(centred * centred, -1, keepdims=True)
    inverse = lax.rsqrt(spread + 1e-05)
    return centred * inverse, inverse


def norm_back(unit, inverse, grad, scales):
    inner = grad * (1.0 + scales)
    first = jnp.mean(inner, -1, keepdims=True)
    second = jnp.mean(inner * unit, -1, keepdims=True)
    return inverse * (inner - first - unit * second)


def modulation(mods_ref, info, tile, part):
    segment = jnp.where(info[0] == 0, 0, 1 + tile)
    width = mods_ref.shape[1] // 6
    return mods_ref[pl.ds(segment, 1), part * width : (part + 1) * width]


def store_pieces(total, info, keep_ref, send_ref, lead):
    half, rows_each = keep_ref.shape[-3], keep_ref.shape[-2]
    fars = half // 2
    for k in range(half):
        low = total[2 * k * rows_each : (2 * k + 1) * rows_each]
        high = total[(2 * k + 1) * rows_each : (2 * k + 2) * rows_each]
        place = ((k % 2) ^ info[11]) * fars + ((k // 2) ^ info[12])
        keep_ref[lead + (place,)] = jnp.where(info[10] == 0, low, high).astype(bf16)
        send_ref[lead + (place,)] = jnp.where(info[10] == 0, high, low).astype(bf16)


def fill(source_ref, w_refs, out_ref, tables):
    for half, w_ref in enumerate(w_refs):
        pl.when(pl.program_id(0) == half)(lambda w_ref=w_ref: fill_half(source_ref, w_ref, out_ref, tables))


def fill_half(source_ref, w_ref, out_ref, tables):
    joined = dot(source_ref[...], w_ref[...])
    for c in range(joined.shape[1] // 128):
        cut = slice(c * 128, (c + 1) * 128)
        piece = joined[:, cut]
        if tables:
            piece = turn(piece, tables[0][...], tables[1][...])
        out_ref[0, :, cut] = piece.astype(bf16)


def project_own_kernel(info, x_ref, mods_ref, *refs):
    w_ref, (cos_ref, sin_ref, joined_ref, normed_ref) = refs[:2], refs[2:]
    half, part = pl.program_id(0), pl.program_id(1)

    @pl.when((half == 0) & (part == 0))
    def _():
        for i in range(x_ref.shape[0] // CONT):
            cut = slice(i * CONT, (i + 1) * CONT)
            unit, _ = norm_parts(x_ref[cut, :].astype(f32))
            shift, scale = (modulation(mods_ref, info, i, n) for n in range(2))
            normed_ref[cut, :] = (unit * (1.0 + scale) + shift).astype(bf16)

    pl.when(part < 2)(lambda: fill(normed_ref, w_ref, joined_ref, (cos_ref, sin_ref)))
    pl.when(part == 2)(lambda: fill(normed_ref, w_ref, joined_ref, None))


def project_prompt_kernel(info, x_ref, *refs):
    came_refs, (mods_ref, *w_ref, cos_ref, sin_ref, joined_ref, normed_ref) = refs[:-7], refs[-7:]
    half, part = pl.program_id(0), pl.program_id(1)
    width = x_ref.shape[1]

    @pl.when((half == 0) & (part == 0))
    def _():
        shift, scale = mods_ref[0:1, :width], mods_ref[0:1, width : 2 * width]
        for i in range(x_ref.shape[0] // CONT):
            cut = slice(i * CONT, (i + 1) * CONT)
            place = i * CONT
            for came_ref in came_refs:
                if 0 <= place < came_ref.shape[0]:
                    came = came_ref[place : place + CONT, :].astype(f32)
                place -= came_ref.shape[0]
            x = jnp.where(info[0] == 0, x_ref[cut, :].astype(f32), came)
            unit, _ = norm_parts(x)
            normed_ref[cut, :] = (unit * (1.0 + scale) + shift).astype(bf16)

    pl.when(part == 0)(lambda: fill(normed_ref, w_ref, joined_ref, (cos_ref, sin_ref)))
    pl.when(part == 1)(lambda: fill(normed_ref, w_ref, joined_ref, None))


def project(kernel, parts, estimate, info, inputs, mods, qkv, tables):
    count, width = inputs[0].shape
    head_width = qkv[0].shape[1] // 3

    def whole(array):
        return pl.BlockSpec(array.shape, lambda t, p, s: (0,) * array.ndim)

    def weight(half):
        def place(t, p, s):
            now = p + 3 - parts
            return (0, jnp.where(t == half, now, 2 if half == 0 else 3 - parts))

        return pl.BlockSpec((width, head_width), place)

    return pl.pallas_call(
        kernel,
        grid_spec=pltpu.PrefetchScalarGridSpec(
            num_scalar_prefetch=1,
            grid=(2, parts),
            in_specs=[whole(array) for array in inputs]
            + [whole(mods), weight(0), weight(1)]
            + [whole(table) for table in tables],
            out_specs=[
                pl.BlockSpec((1, count, head_width), lambda t, p, s: (t, 0, p)),
                whole(inputs[0]),
            ],
        ),
        out_shape=[
            jax.ShapeDtypeStruct((2, count, parts * head_width), bf16),
            jax.ShapeDtypeStruct((count, width), bf16),
        ],
        compiler_params=pltpu.CompilerParams(vmem_limit_bytes=20 * 2**20),
        cost_estimate=estimate,
        name="project",
    )(info, *inputs, mods, *qkv, *tables)


def middle_kernel(
    info, x_ref, a0_ref, a1_ref, mods_ref, o0_ref, o1_ref, branch_ref, middle_ref, n2_ref
):
    branch = dot(a0_ref[...], o0_ref[...], NT) + dot(a1_ref[...], o1_ref[...], NT)
    branch_ref[...] = branch
    per = x_ref.shape[0] // CONT
    for u in range(per):
        cut = slice(u * CONT, (u + 1) * CONT)
        gate, shift, scale = (
            modulation(mods_ref, info, pl.program_id(0) * per + u, n) for n in (2, 3, 4)
        )
        middle = x_ref[cut, :].astype(f32) + gate * branch[cut]
        middle_ref[cut, :] = middle
        unit, _ = norm_parts(middle)
        n2_ref[cut, :] = (unit * (1.0 + scale) + shift).astype(bf16)


def middle_norm(info, x, attended, mods, out_t):
    count, width = x.shape
    head_width = attended[0].shape[1]
    tile = 256
    by_row = pl.BlockSpec((tile, width), lambda i, s: (i, 0))
    by_head = pl.BlockSpec((tile, head_width), lambda i, s: (i, 0))
    return pl.pallas_call(
        middle_kernel,
        grid_spec=pltpu.PrefetchScalarGridSpec(
            num_scalar_prefetch=1,
            grid=(count // tile,),
            in_specs=[
                by_row,
                by_head,
                by_head,
                pl.BlockSpec(mods.shape, lambda i, s: (0, 0)),
                pl.BlockSpec((width, head_width), lambda i, s: (0, 0)),
                pl.BlockSpec((width, head_width), lambda i, s: (0, 0)),
            ],
            out_specs=[by_row] * 3,
        ),
        out_shape=[
            jax.ShapeDtypeStruct((count, width), f32),
            jax.ShapeDtypeStruct((count, width), f32),
            jax.ShapeDtypeStruct((count, width), bf16),
        ],
        compiler_params=pltpu.CompilerParams(vmem_limit_bytes=32 * 2**20),
        cost_estimate=LONG,
        name="middle_norm",
    )(info, x, *attended, mods, *out_t)


def mlp_kernel(first, whole_weights, info, n2_ref, *refs):
    if first:
        cot_ref, mods_ref = refs[:2]
        refs = refs[2:]
    else:
        n2_turned, out_grad, out_turned, branch_before, grad_before = refs[:5]
        refs = refs[5:]
    weight_refs, refs = refs[:whole_weights], refs[whole_weights:]
    branch_ref, grad_ref = refs[:2]
    down_keep_ref, down_send_ref, up_keep_ref, up_send_ref = refs[2:6]
    if first:
        n2_turned, out_grad, out_turned = refs[6:9]
    hidden, pre_grad, *joined = refs[-4:] if whole_weights == 4 else refs[-2:]
    count = n2_ref.shape[0]

    @pl.when(pl.program_id(0) == 0)
    def _():
        if first:
            for i in range(count // CONT):
                cut = slice(i * CONT, (i + 1) * CONT)
                gate = modulation(mods_ref, info, i, 5)
                out_grad[cut, :] = (cot_ref[cut, :].astype(f32) * gate).astype(bf16)
            n2_turned[...] = jnp.transpose(n2_ref[...])
            out_turned[...] = jnp.transpose(out_grad[...])
            branch_ref[...] = jnp.zeros_like(branch_ref)
            grad_ref[...] = jnp.zeros_like(grad_ref)
        else:
            branch_ref[...] = branch_before[...]
            grad_ref[...] = grad_before[...]

    if joined:
        for n, out_ref in enumerate(joined):
            own_ref, came_ref = weight_refs[2 * n : 2 * n + 2]
            rows_each = own_ref.shape[1]
            for k in range(own_ref.shape[0]):
                own, came = own_ref[k], came_ref[k]
                start = 2 * k * rows_each
                out_ref[start : start + rows_each, :] = jnp.where(info[10] == 0, own, came)
                start += rows_each
                out_ref[start : start + rows_each, :] = jnp.where(info[10] == 0, came, own)
        up, down = joined[0][...], joined[1][...]
    else:
        up, down = weight_refs[0][...], weight_refs[1][...]
    tile = 256
    for i in range(count // tile):
        cut = slice(i * tile, (i + 1) * tile)
        pre = dot(n2_ref[cut, :], up)
        cdf = 0.5 * (1.0 + lax.erf(pre * (2.0**-0.5)))
        pdf = jnp.exp(-0.5 * pre * pre) * ((2.0 * math.pi) ** -0.5)
        value = (pre * cdf).astype(bf16)
        hidden[cut, :] = value
        grad = (dot(out_grad[cut, :], down) * (cdf + pre * pdf)).astype(bf16)
        pre_grad[cut, :] = grad
        branch_ref[cut, :] += dot(value, down, NT)
        grad_ref[cut, :] += dot(grad, up, NT)
    store_pieces(dot(out_turned[...], hidden[...]), info, down_keep_ref, down_send_ref, ())
    store_pieces(dot(n2_turned[...], pre_grad[...]), info, up_keep_ref, up_send_ref, ())


def feed_forward(info, n2, sources, weights):
    count, width = n2.shape
    hidden_width = weights[0].shape[-1]
    first = len(sources) == 2
    cols = 384
    dp_count = lax.axis_size("dp")
    pieces = (dp_count // 2, width // dp_count, hidden_width)

    def whole(array):
        return pl.BlockSpec(
            array.shape, lambda b, s: (0,) * array.ndim, pipeline_mode=pl.Buffered(1)
        )

    piece_spec = pl.BlockSpec(pieces[:2] + (cols,), lambda b, s: (0, 0, b))
    weight_specs = [
        pl.BlockSpec(w.shape[:-1] + (cols,), lambda b, s, lead=w.ndim - 1: (0,) * lead + (b,))
        for w in weights
    ]
    scratch = [pltpu.VMEM((count, cols), bf16)] * 2
    if len(weights) == 4:
        scratch += [pltpu.VMEM((width, cols), bf16)] * 2
    outs = [jax.ShapeDtypeStruct((count, width), f32)] * 2 + [
        jax.ShapeDtypeStruct(pieces, bf16)
    ] * 4
    out_specs = [whole(n2)] * 2 + [piece_spec] * 4
    if first:
        shapes = [(width, count), (count, width), (width, count)]
        outs += [jax.ShapeDtypeStruct(shape, bf16) for shape in shapes]
        out_specs += [pl.BlockSpec(shape, lambda b, s: (0, 0)) for shape in shapes]
    return pl.pallas_call(
        lambda *refs: mlp_kernel(first, len(weights), *refs),
        grid_spec=pltpu.PrefetchScalarGridSpec(
            num_scalar_prefetch=1,
            grid=(hidden_width // cols,),
            in_specs=[whole(n2)] + [whole(array) for array in sources] + weight_specs,
            out_specs=out_specs,
            scratch_shapes=scratch,
        ),
        out_shape=outs,
        compiler_params=pltpu.CompilerParams(vmem_limit_bytes=52 * 2**20),
        cost_estimate=LONG,
        name="feed_forward",
    )(info, n2, *sources, *weights)


def post_kernel(
    info,
    middle_ref,
    branch_ref,
    mlp_ref,
    n2_grad_ref,
    cot_ref,
    a0_ref,
    a1_ref,
    mods_ref,
    o0_ref,
    o1_ref,
    out_ref,
    middle_grad_ref,
    g0_ref,
    g1_ref,
    sums_ref,
    keep_ref,
    send_ref,
    total,
    attn_grad,
):
    step = pl.program_id(0)
    per = middle_ref.shape[0] // CONT
    for u in range(per):
        cut = slice(u * CONT, (u + 1) * CONT)
        tile = step * per + u
        gate1, scale2, gate2 = (modulation(mods_ref, info, tile, n) for n in (2, 4, 5))
        middle, branch, mlp = middle_ref[cut, :], branch_ref[cut, :], mlp_ref[cut, :]
        n2_grad, upstream = n2_grad_ref[cut, :], cot_ref[cut, :].astype(f32)
        mlp_part, attn_part = gate2 * mlp, gate1 * branch
        result = middle + mlp_part
        out_ref[cut, :] = result.astype(bf16)
        unit, inverse = norm_parts(middle)
        middle_grad = upstream + norm_back(unit, inverse, n2_grad, scale2)
        middle_grad_ref[cut, :] = middle_grad
        attn_grad[cut, :] = (middle_grad * gate1).astype(bf16)
        valid = (rows((CONT, 1)) < info[2 + tile]).astype(f32)
        for n, value in enumerate(
            (
                middle_grad * branch,
                n2_grad,
                n2_grad * unit,
                upstream * mlp,
                valid * result * result,
                valid * attn_part * attn_part,
                valid * mlp_part * mlp_part,
            )
        ):
            sums_ref[u, n : n + 1, :] = jnp.sum(value, 0, keepdims=True)
        sums_ref[u, 7:8, :] = jnp.zeros_like(gate1)
    halves = ((a0_ref, g0_ref, o0_ref), (a1_ref, g1_ref, o1_ref))
    for t, (a_ref, g_ref, o_ref) in enumerate(halves):
        g_ref[...] = dot(attn_grad[...], o_ref[...]).astype(bf16)
        part = dot(attn_grad[...], a_ref[...], TN)
        total[t] = jnp.where(step == 0, part, total[t] + part)

    @pl.when(step == pl.num_programs(0) - 1)
    def _():
        for t in range(2):
            store_pieces(total[t], info, keep_ref, send_ref, (t,))


def post(info, middle, branch, mlp, n2_grad, cotangent, attended, mods, out_t):
    count, width = middle.shape
    head_width = attended[0].shape[1]
    tile = 256
    tiles = count // CONT
    dp_count = lax.axis_size("dp")
    pieces = (2, dp_count // 2, width // dp_count, head_width)
    by_row = pl.BlockSpec((tile, width), lambda i, s: (i, 0))
    by_head = pl.BlockSpec((tile, head_width), lambda i, s: (i, 0))
    return pl.pallas_call(
        post_kernel,
        grid_spec=pltpu.PrefetchScalarGridSpec(
            num_scalar_prefetch=1,
            grid=(count // tile,),
            in_specs=[by_row] * 5
            + [
                by_head,
                by_head,
                pl.BlockSpec(mods.shape, lambda i, s: (0, 0)),
                pl.BlockSpec((width, head_width), lambda i, s: (0, 0)),
                pl.BlockSpec((width, head_width), lambda i, s: (0, 0)),
            ],
            out_specs=[
                by_row,
                by_row,
                by_head,
                by_head,
                pl.BlockSpec((tile // CONT, 8, width), lambda i, s: (i, 0, 0)),
                pl.BlockSpec(pieces, lambda i, s: (0, 0, 0, 0)),
                pl.BlockSpec(pieces, lambda i, s: (0, 0, 0, 0)),
            ],
            scratch_shapes=[
                pltpu.VMEM((2, width, head_width), f32),
                pltpu.VMEM((tile, width), bf16),
            ],
        ),
        out_shape=[
            jax.ShapeDtypeStruct((count, width), bf16),
            jax.ShapeDtypeStruct((count, width), f32),
            jax.ShapeDtypeStruct((count, head_width), bf16),
            jax.ShapeDtypeStruct((count, head_width), bf16),
            jax.ShapeDtypeStruct((tiles, 8, width), f32),
            jax.ShapeDtypeStruct(pieces, bf16),
            jax.ShapeDtypeStruct(pieces, bf16),
        ],
        compiler_params=pltpu.CompilerParams(vmem_limit_bytes=48 * 2**20),
        cost_estimate=LONG,
        name="post",
    )(info, middle, branch, mlp, n2_grad, cotangent, *attended, mods, *out_t)


def last_kernel(
    info, x_ref, own_ref, prompt_ref, came_ref, middle_grad_ref, mods_ref, out_ref, sums_ref
):
    step = pl.program_id(0)
    per = x_ref.shape[0] // CONT
    for u in range(per):
        cut = slice(u * CONT, (u + 1) * CONT)
        scale = modulation(mods_ref, info, step * per + u, 1)
        prompt = prompt_ref[cut, :] + came_ref[cut, :].astype(f32)
        grad = own_ref[cut, :] + jnp.where(info[0] == 0, prompt, 0.0)
        unit, inverse = norm_parts(x_ref[cut, :].astype(f32))
        sums_ref[u, 0:1, :] = jnp.sum(grad, 0, keepdims=True)
        sums_ref[u, 1:2, :] = jnp.sum(grad * unit, 0, keepdims=True)
        sums_ref[u, 2:, :] = jnp.zeros((6, x_ref.shape[1]), f32)
        out_ref[cut, :] = middle_grad_ref[cut, :] + norm_back(unit, inverse, grad, scale)


def last(info, x, own_sum, prompt_sum, came, middle_grad, mods):
    count, width = x.shape
    tile = 256
    by_row = pl.BlockSpec((tile, width), lambda i, s: (i, 0))
    return pl.pallas_call(
        last_kernel,
        grid_spec=pltpu.PrefetchScalarGridSpec(
            num_scalar_prefetch=1,
            grid=(count // tile,),
            in_specs=[by_row] * 5 + [pl.BlockSpec(mods.shape, lambda i, s: (0, 0))],
            out_specs=[by_row, pl.BlockSpec((tile // CONT, 8, width), lambda i, s: (i, 0, 0))],
        ),
        out_shape=[
            jax.ShapeDtypeStruct((count, width), f32),
            jax.ShapeDtypeStruct((count // CONT, 8, width), f32),
        ],
        compiler_params=pltpu.CompilerParams(vmem_limit_bytes=16 * 2**20),
        cost_estimate=LONG,
        name="last",
    )(info, x, own_sum, prompt_sum, came, middle_grad, mods)


def forward_kernel(info, *refs):
    q_ref, kp_ref, vp_ref, ko_ref, vo_ref = (ref.at[0] for ref in refs[:5])
    o_ref, lse_ref = refs[5:]
    role = info[0]
    prompt_count = info[1]
    count = q_ref.shape[0]
    lane = lanes((count, 128))
    row = rows((count, 128))
    tile = 256
    blocks = count // tile

    def prepare(h):
        sel = (lane // 64) == h
        extra = 64 * (1 - h)
        q = jnp.where(sel, q_ref[...], jnp.where(lane == extra, 1.0, 0.0).astype(bf16))
        bias = jnp.where((lane == extra) & (row >= prompt_count), NEG, 0.0).astype(bf16)
        k = jnp.where(sel, kp_ref[...], bias)
        v = jnp.where(sel, vp_ref[...], jnp.ones((), bf16))
        return sel, q, k, v

    def finish(h, i, o, top):
        extra = 64 * (1 - h)
        weight = o[:, extra : extra + 1]
        lse = top * SCALE2 + jnp.log2(weight)
        turned = jnp.transpose(jnp.broadcast_to(lse, (tile, 128)))
        lse_ref[0, h : h + 1, i * tile : (i + 1) * tile] = turned[0:1, :]
        return o * (1.0 / weight)

    def store(outs):
        for i in range(blocks):
            merged = jnp.where(lanes((tile, 128)) < 64, outs[0][i], outs[1][i])
            o_ref[i * tile : (i + 1) * tile, :] = merged.astype(bf16)

    @pl.when(role == 0)
    def _():
        outs = []
        for h in range(2):
            sel, q, k, v = prepare(h)
            heads = []
            for i in range(blocks):
                start, stop = i * tile, (i + 1) * tile
                s = dot(q[start:stop], k[:stop], NT)
                near = jnp.where(lanes((tile, tile)) <= rows((tile, tile)), s[:, start:], NEG)
                top = jnp.max(near, 1, keepdims=True)
                if i:
                    top = jnp.maximum(top, jnp.max(s[:, :start], 1, keepdims=True))
                o = dot(jnp.exp2(near * SCALE2 - top * SCALE2).astype(bf16), v[start:stop])
                if i:
                    o = o + dot(
                        jnp.exp2(s[:, :start] * SCALE2 - top * SCALE2).astype(bf16), v[:start]
                    )
                heads.append(finish(h, i, o, top))
            outs.append(heads)
        store(outs)

    @pl.when(role != 0)
    def _():
        outs = []
        for h in range(2):
            sel, q, k, v = prepare(h)
            own_k = jnp.where(sel, ko_ref[...], jnp.zeros((), bf16))
            own_v = jnp.where(sel, vo_ref[...], jnp.ones((), bf16))
            heads, far, near, tops = [], [], [], []
            col, line = lanes((CONT, CONT)), rows((CONT, CONT))
            cuts = [slice(r, r + CONT) for r in range(0, count, CONT)]
            for n, cut in enumerate(cuts):
                fine = (col <= line) & (col < info[2 + n])
                near.append(jnp.where(fine, dot(q[cut], own_k[cut], NT), NEG))
            near = jnp.concatenate(near, 0)
            near_tops = jnp.max(near, 1, keepdims=True)
            for i in range(blocks):
                cut = slice(i * tile, (i + 1) * tile)
                s = dot(q[cut], k, NT)
                tops.append(jnp.maximum(jnp.max(s, 1, keepdims=True), near_tops[cut]))
                far.append(dot(jnp.exp2(s * SCALE2 - tops[i] * SCALE2).astype(bf16), v))
            weight = jnp.exp2(near * SCALE2 - jnp.concatenate(tops, 0) * SCALE2).astype(bf16)
            own = jnp.concatenate([dot(weight[cut], own_v[cut]) for cut in cuts], 0)
            for i in range(blocks):
                heads.append(finish(h, i, far[i] + own[i * tile : (i + 1) * tile], tops[i]))
            outs.append(heads)
        store(outs)


def attend(info, joined, prompts, t):
    count = joined.shape[1]
    head_width = joined.shape[2] // 3
    pairs = head_width // 128

    def spec(offset):
        return pl.BlockSpec((1, count, 128), lambda h, s: (t, 0, offset + h))

    return pl.pallas_call(
        forward_kernel,
        grid_spec=pltpu.PrefetchScalarGridSpec(
            num_scalar_prefetch=1,
            grid=(pairs,),
            in_specs=[spec(0), spec(0), spec(pairs), spec(pairs), spec(2 * pairs)],
            out_specs=[
                pl.BlockSpec((count, 128), lambda h, s: (0, h)),
                pl.BlockSpec((1, 2, count), lambda h, s: (h, 0, 0)),
            ],
        ),
        out_shape=[
            jax.ShapeDtypeStruct((count, head_width), bf16),
            jax.ShapeDtypeStruct((pairs, 2, count), f32),
        ],
        compiler_params=pltpu.CompilerParams(vmem_limit_bytes=20 * 2**20),
        cost_estimate=LONG,
        name="attend",
    )(info, joined, prompts, prompts, joined, joined)


def backward_kernel(first, last, tiles, own, info, *refs):
    refs = list(refs)
    q_ref, do_ref, o_ref, lse_ref = refs[0].at[0], *refs[1:4]
    del refs[:4]
    if tiles:
        kp_ref, vp_ref, cp_ref, sp_ref = refs[0].at[0], refs[1].at[0], *refs[2:4]
        del refs[:4]
    if own:
        ko_ref, vo_ref = refs[0].at[0], refs[1].at[0]
        del refs[:2]
    if own or last:
        co_ref, so_ref = refs[:2]
        del refs[:2]
    before_ref = None if first else refs.pop(0)
    dq_ref = refs.pop(0)
    if tiles:
        dkp_ref, dvp_ref = refs[:2]
        del refs[:2]
    if own:
        dko_ref, dvo_ref = refs[:2]
        del refs[:2]
    (dq_acc,) = refs
    role = info[0]
    prompt_count = info[1]
    count = q_ref.shape[0]
    tile = 256
    lane = lanes((count, 128))
    none = jnp.zeros((), bf16)
    products = jnp.transpose(do_ref[...].astype(f32) * o_ref[...].astype(f32))
    deltas = [jnp.sum(products[64 * h : 64 * h + 64], 0, keepdims=True) for h in range(2)]
    dq_acc[...] = jnp.zeros_like(dq_acc) if first else before_ref[...]

    def far_block(j, prompt):
        start, stop = j * tile, (j + 1) * tile
        cut = slice(start - tiles[0] * tile, stop - tiles[0] * tile)
        q_from = start if prompt else 0
        lane_k = lanes((tile, 128))
        row_k = rows((tile, 128)) + start
        key_parts, value_parts = [], []
        for h in range(2):
            extra = 64 * (1 - h)
            sel = (lane_k // 64) == h
            bias = jnp.where((lane_k == extra) & (row_k >= prompt_count), NEG, 0.0).astype(bf16)
            k = jnp.where(sel, kp_ref[cut, :], bias)
            k_plain = jnp.where(sel, kp_ref[cut, :], none)
            v = jnp.where(sel, vp_ref[cut, :], none)
            lane_q = lane[q_from:]
            ones = jnp.where(lane_q == extra, 1.0, 0.0).astype(bf16)
            q = jnp.where((lane_q // 64) == h, q_ref[q_from:, :], ones)
            s = dot(k, q, NT)
            if prompt:
                near = jnp.where(rows((tile, tile)) <= lanes((tile, tile)), s[:, :tile], NEG)
                s = jnp.concatenate([near, s[:, tile:]], 1) if stop < count else near
            weight = jnp.exp2(s * SCALE2 - lse_ref[0, h : h + 1, q_from:])
            grad = dot(v, do_ref[q_from:, :], NT)
            score = (weight * (grad - deltas[h][:, q_from:])).astype(bf16)
            value_parts.append(dot(weight.astype(bf16), do_ref[q_from:, :]))
            key_parts.append(dot(score, q_ref[q_from:, :]))
            dq_acc[q_from:, :] += dot(score, k_plain, TN)
        key_grad = jnp.where(lane_k < 64, key_parts[0], key_parts[1]) * SCALE
        value_grad = jnp.where(lane_k < 64, value_parts[0], value_parts[1])
        dkp_ref[cut, :] = turn_back(key_grad, cp_ref[cut, :], sp_ref[cut, :]).astype(bf16)
        dvp_ref[cut, :] = value_grad.astype(bf16)

    @pl.when(role == 0)
    def _():
        for j in tiles:
            far_block(j, True)
        if own:
            dko_ref[...] = jnp.zeros_like(dko_ref)
            dvo_ref[...] = jnp.zeros_like(dvo_ref)

    @pl.when(role != 0)
    def _():
        for j in tiles:
            far_block(j, False)
        lane_k = lanes((CONT, CONT))
        row_k = rows((CONT, CONT))
        every = range(count // CONT if own else 0)
        cuts = [slice(i * CONT, (i + 1) * CONT) for i in every]
        key_parts, value_parts = [], []
        for h in range(2 if own else 0):
            sel = (lane // 64) == h
            k = jnp.where(sel, ko_ref[...], none)
            v = jnp.where(sel, vo_ref[...], none)
            scores, weights = [], []
            for i, cut in enumerate(cuts):
                fine = (row_k <= lane_k) & (row_k < info[2 + i])
                scores.append(jnp.where(fine, dot(k[cut], q_ref[cut, :], NT), NEG) * SCALE2 - lse_ref[0, h : h + 1, cut])
            weight = jnp.exp2(jnp.concatenate(scores, 0))
            grad = jnp.concatenate([dot(v[cut], do_ref[cut, :], NT) - deltas[h][:, cut] for cut in cuts], 0)
            score = (weight * grad).astype(bf16)
            weight = weight.astype(bf16)
            value_parts.append([dot(weight[cut], do_ref[cut, :]) for cut in cuts])
            key_parts.append([dot(score[cut], q_ref[cut, :]) for cut in cuts])
            for cut in cuts:
                dq_acc[cut, :] += dot(score[cut], k[cut], TN)
        for i, cut in enumerate(cuts):
            key_grad = jnp.where(lane_k < 64, key_parts[0][i], key_parts[1][i]) * SCALE
            value_grad = jnp.where(lane_k < 64, value_parts[0][i], value_parts[1][i])
            dko_ref[cut, :] = turn_back(key_grad, co_ref[cut, :], so_ref[cut, :]).astype(bf16)
            dvo_ref[cut, :] = value_grad.astype(bf16)

    if last:
        dq_ref[...] = turn_back(dq_acc[...] * SCALE, co_ref[...], so_ref[...]).astype(bf16)
    else:
        dq_ref[...] = dq_acc[...]


def attend_back(info, joined, prompts, t, grad, out, lse, tables, tiles, own, before=None, last=True):
    count = joined.shape[1]
    head_width = joined.shape[2] // 3
    pairs = head_width // 128
    first = before is None
    part = 256 * len(tiles)

    def half_spec(offset):
        return pl.BlockSpec((1, count, 128), lambda h, s: (t, 0, offset + h))

    def part_spec(offset):
        return pl.BlockSpec((1, part, 128), lambda h, s: (t, tiles[0] * 256 // part, offset + h))

    rows_spec = pl.BlockSpec((count, 128), lambda h, s: (0, h))
    whole = pl.BlockSpec((count, 128), lambda h, s: (0, 0))
    args = [joined, grad, out, lse]
    specs = [
        half_spec(0),
        rows_spec,
        rows_spec,
        pl.BlockSpec((1, 2, count), lambda h, s: (h, 0, 0)),
    ]
    outs = [jax.ShapeDtypeStruct((count, head_width), bf16 if last else f32)]
    out_specs = [rows_spec]
    if tiles:
        args += [prompts, prompts, tables[2], tables[3]]
        part_table = pl.BlockSpec((part, 128), lambda h, s: (tiles[0] * 256 // part, 0))
        specs += [part_spec(0), part_spec(pairs), part_table, part_table]
        outs += [jax.ShapeDtypeStruct((part, head_width), bf16)] * 2
        out_specs += [pl.BlockSpec((part, 128), lambda h, s: (0, h))] * 2
    if own:
        args += [joined, joined]
        specs += [half_spec(pairs), half_spec(2 * pairs)]
        outs += [jax.ShapeDtypeStruct((count, head_width), bf16)] * 2
        out_specs += [rows_spec] * 2
    if own or last:
        args += [tables[0], tables[1]]
        specs += [whole, whole]
    if not first:
        args += [before]
        specs += [rows_spec]
    return pl.pallas_call(
        lambda *refs: backward_kernel(first, last, tiles, own, *refs),
        grid_spec=pltpu.PrefetchScalarGridSpec(
            num_scalar_prefetch=1,
            grid=(pairs,),
            in_specs=specs,
            out_specs=out_specs,
            scratch_shapes=[pltpu.VMEM((count, 128), f32)],
        ),
        out_shape=outs,
        compiler_params=pltpu.CompilerParams(vmem_limit_bytes=20 * 2**20),
        cost_estimate=LONG,
        name="attend_back",
    )(info, *args)


def split_three(values):
    high = lax.reduce_precision(values, 8, 7)
    rest = values - high
    mid = lax.reduce_precision(rest, 8, 7)
    return high, mid, rest - mid


def pick(x, index, axis):
    return lax.dynamic_index_in_dim(x, index, axis, keepdims=False)


def body(
    block_input,
    cotangent,
    w_qkv,
    w_out,
    w_up,
    w_down,
    w_mod,
    time_table,
    prompt_len,
    cont_len,
    timestep,
):
    count, width = block_input.shape
    tiles = count // CONT
    dp_count = lax.axis_size("dp")
    tensor_count = lax.axis_size("tensor")
    devices = dp_count * tensor_count
    role = lax.axis_index("tensor")
    is_prompt = role == 0
    me = lax.axis_index("dp")
    core, near, far = me % 2, (me // 2) % 2, me // 4
    fars = far_count()
    low_bits = far_bits()
    high_bits = list(reversed(low_bits))
    head_width = w_qkv.shape[2]
    half = count // 2

    def far_bit(bit):
        return (far // bit) % 2

    far_top, far_rest = high_bits[0], high_bits[1:]
    cuts = (head_width, w_up.shape[1], w_down.shape[0])
    table_rows, rows_each = time_table.shape[0], w_qkv.shape[0]
    steps = jnp.pad(timestep.reshape(1, -1), ((0, rows_each - 1), (0, 128 - SEGS))).astype(bf16)
    table_width = table_rows * width // rows_each
    table_width += -table_width % 128
    table_part = time_table.reshape(-1)
    table_part = jnp.pad(table_part, (0, rows_each * table_width - table_part.shape[0]))
    table_part = table_part.reshape(rows_each, table_width)
    first = [w_qkv.reshape(rows_each, -1), table_part, steps]
    first_cuts = (first[0].shape[1], table_width + 128)
    first = jnp.concatenate(first, 1)[None]
    bounds = [0, count // 4, count * 5 // 8, count]
    x_parts = [block_input[bounds[n] : bounds[n + 1]] for n in range(3)]
    rest = jnp.concatenate([w_out.T, w_up, w_down.T], 1)[None]
    came_first = swap(first, 8 * far_top)
    first, came_first, x_parts, rest = tie(first, came_first, x_parts, rest)
    came = [swap(x_parts[0], TENSOR)]
    for bit in far_rest:
        first = join(first, came_first, far_bit(2 * bit))
        came_first = swap(first, 8 * bit)
    came_first, first, came, rest = tie(came_first, first, came, rest)
    qkv_far, table_far = join(first, came_first, far_bit(1), first_cuts)

    table_near = [swap(table_far, bits) for bits in (NEAR, TENSOR, NEAR + TENSOR)]
    qkv_near = [swap(qkv_far, bits) for bits in (NEAR, TENSOR)]
    table_own = join(table_far, table_near[0], near)
    table_other = join(table_near[1], table_near[2], near)
    table_came = [swap(table_own, CORE), swap(table_other, CORE)]
    table_cuts = (table_width, 128)
    packets = [
        join(table_own, table_came[0], core, table_cuts),
        join(table_other, table_came[1], core, table_cuts),
    ]
    rest_came = swap(rest, 8 * far_top)

    turns = HEAD_DIM // 2
    freqs = 10000.0 ** (-(jnp.arange(128, dtype=jnp.int32) % turns).astype(f32) / turns)
    inside = jnp.arange(count, dtype=jnp.int32)
    prompt_count = prompt_len[0]
    own_places = jnp.where(is_prompt, inside, prompt_count + inside % CONT).astype(f32)
    own_angles = own_places[:, None] * freqs[None, :]
    prompt_angles = inside.astype(f32)[:, None] * freqs[None, :]
    tables = (jnp.cos(own_angles), jnp.sin(own_angles), jnp.cos(prompt_angles), jnp.sin(prompt_angles))
    own_len = jnp.where(
        is_prompt,
        jnp.clip(prompt_count - CONT * jnp.arange(NCONT, dtype=jnp.int32), 0, CONT),
        cont_len[0],
    )
    info = jnp.concatenate(
        [jnp.stack([role, prompt_count]), own_len, jnp.stack([core, near, far])]
    ).astype(jnp.int32)

    table_full = jnp.concatenate([packets[0][0], packets[1][0]], 0)
    table_full = table_full.reshape(2 * dp_count, -1)[:, : table_rows * width]
    table_full = table_full.reshape(STEPS, width)
    step_rows = packets[0][1][:, 0, :SEGS].astype(jnp.int32)
    row_ids = (jnp.arange(2)[:, None, None] + role) % 2 * table_rows + (
        jnp.arange(dp_count)[None, :, None] * 2 * table_rows + jnp.arange(table_rows)
    )
    row_ids = row_ids.reshape(-1).astype(jnp.int32)
    step_pad = jnp.pad(step_rows, ((0, 0), (0, 16 - SEGS))).reshape(-1)
    chosen = (step_pad[:, None] == row_ids[None, :]).astype(bf16)
    cond = dot(chosen, table_full).astype(bf16)
    col_width = w_mod.shape[1]
    col_part = dot(cond, w_mod).reshape(dp_count, 1, 16, col_width)
    col_part = jnp.broadcast_to(col_part, (dp_count, tensor_count, 16, col_width))
    col_part = col_part.reshape(devices, 16, col_width).astype(f32)
    arrived = lax.all_to_all(col_part, BOTH, 0, 0, tiled=True)
    qkv_far, qkv_near, rest, rest_came, tables, info, _ = tie(
        qkv_far, qkv_near, rest, rest_came, tables, info, col_part
    )
    qkv_near.append(swap(qkv_far, NEAR + TENSOR))
    rest = join(rest, rest_came, far_bit(far_top), None if far_rest else cuts)
    if far_rest:
        rest_came = swap(rest, 8 * far_rest[0])

    qkv_far, qkv_near, arrived, came, x_parts = tie(qkv_far, qkv_near, arrived, came, x_parts)
    mods = jnp.transpose(arrived, (1, 0, 2)).reshape(16, 6 * width)
    came.append(swap(x_parts[1], TENSOR))
    qkv_own = join(qkv_far, qkv_near[0], near)
    qkv_other = join(qkv_near[1], qkv_near[2], near)
    qkv_came = [swap(qkv_own, CORE), swap(qkv_other, CORE)]
    for bit in far_rest[1:]:
        rest = join(rest, rest_came, far_bit(bit * 2))
        rest_came = swap(rest, 8 * bit)
    qkv = [
        join(own, other, core).reshape(width, -1)
        for own, other in zip((qkv_own, qkv_other), qkv_came)
    ]
    rest, rest_came, mods, qkv, came, x_parts = tie(rest, rest_came, mods, qkv, came, x_parts)

    def both_cores(own, came):
        return [own, came] if rows_each % 16 == 0 else [join(own, came, core).reshape(width, -1)]

    came.append(swap(x_parts[2], TENSOR))
    o_own, u_own, d_own = join(rest, rest_came, far_bit(1), cuts) if far_rest else rest
    u_near, o_near, o_other = swap(u_own, NEAR), swap(o_own, NEAR), swap(o_own, TENSOR)
    joined, normed = project(
        project_own_kernel, 3, LONG, info, [block_input], mods, qkv, tables[:2]
    )
    came, joined, u_near = tie(came, joined, u_near)
    prompts, prompt_normed = project(
        project_prompt_kernel, 2, LONG, info, [block_input, *came], mods, qkv, tables[2:]
    )
    u_near, o_near, o_other, u_own, o_own, d_own, prompts = tie(
        u_near, o_near, o_other, u_own, o_own, d_own, prompts
    )
    d_near, u_other, oo_near = swap(d_own, NEAR), swap(u_own, TENSOR), swap(o_other, NEAR)
    u_own, o_own = join(u_own, u_near, near), join(o_own, o_near, near)
    u_core = swap(u_own, CORE)
    out_0, lse_0 = attend(info, *tie(joined, prompts, u_own, o_own)[:2], 0)
    d_near, u_other, oo_near, u_core, d_own, u_own, o_own, o_other, out_0, joined = tie(
        d_near, u_other, oo_near, u_core, d_own, u_own, o_own, o_other, out_0, joined
    )
    d_other, uu_near = swap(d_own, TENSOR), swap(u_other, NEAR)
    d_own, o_other = join(d_own, d_near, near), join(o_other, oo_near, near)
    d_core, o_core, oo_core = swap(d_own, CORE), swap(o_own, CORE), swap(o_other, CORE)
    up_0 = both_cores(u_own, u_core)
    out_1, lse_1 = attend(info, *tie(joined, prompts, d_own, o_other, up_0)[:2], 1)
    d_other, uu_near, d_core, o_core, oo_core, d_own, o_own, o_other, u_other, out_1 = tie(
        d_other, uu_near, d_core, o_core, oo_core, d_own, o_own, o_other, u_other, out_1
    )
    attended, lses = [out_0, out_1], [lse_0, lse_1]
    out_t = [
        join(o_own, o_core, core).reshape(width, -1),
        join(o_other, oo_core, core).reshape(width, -1),
    ]
    branch, middle, normed_two = middle_norm(info, block_input, attended, mods, out_t)

    dd_near = swap(d_other, NEAR)
    u_other = join(u_other, uu_near, near)
    uu_core = swap(u_other, CORE)
    down_0 = both_cores(d_own, d_core)
    d_other, u_other, normed_two, down_0 = tie(d_other, u_other, normed_two, down_0)
    mlp, n2_grad, d_keep_0, d_send_0, u_keep_0, u_send_0, *shared = feed_forward(
        info, normed_two, (cotangent, mods), up_0 + down_0
    )
    dd_near, uu_core, d_other, u_other, mlp, d_send_0, u_send_0 = tie(
        dd_near, uu_core, d_other, u_other, mlp, d_send_0, u_send_0
    )
    d_other = join(d_other, dd_near, near)
    dd_core = swap(d_other, CORE)
    up_1 = both_cores(u_other, uu_core)
    down_1 = both_cores(d_other, dd_core)
    up_1, down_1, mlp, d_send_0, u_send_0 = tie(up_1, down_1, mlp, d_send_0, u_send_0)
    d_came_0, u_came_0 = swap(d_send_0, CORE), swap(u_send_0, CORE)
    mlp, n2_grad, d_keep_1, d_send_1, u_keep_1, u_send_1 = feed_forward(
        info, normed_two, (*shared, mlp, n2_grad), up_1 + down_1
    )
    d_came_0, u_came_0, mlp, d_send_1, u_send_1 = tie(d_came_0, u_came_0, mlp, d_send_1, u_send_1)
    d_came_1, u_came_1 = swap(d_send_1, CORE), swap(u_send_1, CORE)
    block_output, middle_grad, grad_0, grad_1, post_sums, o_keep, o_send = post(
        info, middle, branch, mlp, n2_grad, cotangent, attended, mods, out_t
    )
    d_came_1, u_came_1, o_keep, o_send, grad_0, grad_1 = tie(
        d_came_1, u_came_1, o_keep, o_send, grad_0, grad_1
    )

    def by_near(x):
        return x.reshape((2, 2, fars) + x.shape[2:])

    def near_part(keep, came, part):
        half_of = slice(part * fars, (part + 1) * fars)
        return plus(keep[half_of], came[half_of])

    o_came = swap(o_send, CORE)
    d_send = [near_part(d_keep_0, d_came_0, 1), near_part(d_keep_1, d_came_1, 1)]
    d_keep = [near_part(d_keep_0, d_came_0, 0), near_part(d_keep_1, d_came_1, 0)]
    u_send, u_keep = plus(u_keep_1, u_came_1), plus(u_keep_0, u_came_0)
    d_came, u_came = swap(jnp.stack(d_send), NEAR), swap(u_send, TENSOR)
    d_keep, u_keep, grad_1 = tie(d_keep, u_keep, grad_1)

    def back(t, grad, blocks, own, before=None, last=True):
        return attend_back(
            info, joined, prompts, t, grad, attended[t], lses[t], tables, blocks, own, before, last
        )

    def prompt_part(t, dkv):
        return dot(dkv, qkv[t][:, head_width:], NT)

    def weight_part(dqkv, dkv_prompt):
        whole = dot(normed, dqkv, TN)
        parts = [whole[:, :head_width], whole[:, head_width:] + dot(prompt_normed, dkv_prompt, TN)]
        whole = jnp.concatenate([part.astype(bf16) for part in parts], 1)
        return whole.reshape(fars, 2, 2, -1, whole.shape[1])

    dq_1, dkp_1, dvp_1, dk_1, dv_1 = back(1, grad_1, (0, 1, 2, 3), True)
    d_came, u_came, o_came, d_keep, u_keep, o_keep, grad_0, dq_1, dkp_1, dvp_1, dk_1, dv_1 = tie(
        d_came, u_came, o_came, d_keep, u_keep, o_keep, grad_0, dq_1, dkp_1, dvp_1, dk_1, dv_1
    )
    o_cur = by_near(plus(o_keep, o_came))
    d_keep, d_send = plus(d_keep[0], d_came[0]), plus(d_keep[1], d_came[1])
    u_keep, u_send = near_part(u_keep, u_came, 0), near_part(u_keep, u_came, 1)
    d_came, u_came = swap(d_send, TENSOR), swap(u_send, NEAR)
    o_came = swap(o_cur[:, 1], NEAR)
    o_keep = o_cur[:, 0]
    dqkv_1 = jnp.concatenate([dq_1, dk_1, dv_1], 1)
    dkvp_1 = jnp.concatenate([dkp_1, dvp_1], 1)
    q_cur = weight_part(dqkv_1, dkvp_1)
    q_came = swap(pick(q_cur, 1 - core, 2), CORE)
    q_keep = pick(q_cur, core, 2)
    own_sum = dot(dqkv_1, qkv[1], NT)
    prompt_sum = prompt_part(1, dkvp_1)
    q_keep, own_sum, prompt_sum, grad_0, d_keep, u_keep, o_keep = tie(
        q_keep, own_sum, prompt_sum, grad_0, d_keep, u_keep, o_keep
    )

    dq_0, dkp_a, dvp_a = back(0, grad_0, (0, 1), False, None, False)
    q_came, d_came, u_came, o_came, q_keep, d_keep, u_keep, o_keep, dq_0, dkp_a, dvp_a = tie(
        q_came, d_came, u_came, o_came, q_keep, d_keep, u_keep, o_keep, dq_0, dkp_a, dvp_a
    )
    dkvp_a = jnp.concatenate([dkp_a, dvp_a], 1)
    sum_a = prompt_sum[:half] + prompt_part(0, dkvp_a)
    came_a = swap(sum_a.astype(bf16), TENSOR)
    d_keep, d_send = send_far(plus(d_keep, d_came))
    u_keep, u_send = send_far(plus(u_keep, u_came))
    o_cur = plus(o_keep, o_came)
    q_cur = plus(q_keep, q_came)
    d_came, u_came = swap(d_send, 8), swap(u_send, 8)
    o_came, o_keep = swap(o_cur[1], TENSOR), o_cur[0]
    q_came, q_keep = swap(pick(q_cur, 1 - near, 1), NEAR), pick(q_cur, near, 1)
    sum_a, d_keep, u_keep, o_keep, q_keep, dq_0 = tie(sum_a, d_keep, u_keep, o_keep, q_keep, dq_0)

    dq_0, dkp_b, dvp_b = back(0, grad_0, (2, 3), False, dq_0, False)
    came, keep, grads = tie(
        (came_a, d_came, u_came, o_came, q_came),
        (d_keep, u_keep, o_keep, q_keep),
        (dkp_b, dvp_b, dq_0),
    )
    came_a, d_came, u_came, o_came, q_came = came
    d_keep, u_keep, o_keep, q_keep = keep
    dkp_b, dvp_b, dq_0 = grads
    dkvp_b = jnp.concatenate([dkp_b, dvp_b], 1)
    sum_b = prompt_sum[half:] + prompt_part(0, dkvp_b)
    came_b = swap(sum_b.astype(bf16), TENSOR)

    def far_end(keep, came):
        for bit in low_bits[1:]:
            keep, send = send_far(plus(keep, came))
            came = swap(send, 8 * bit)
        return keep, came

    d_keep, d_came = far_end(d_keep, d_came)
    u_keep, u_came = far_end(u_keep, u_came)
    o_keep, o_send = send_far(plus(o_keep, o_came))
    o_came = swap(o_send, 8)
    q_send = plus(q_keep, q_came)
    q_send, sum_b, dq_0 = tie(q_send, sum_b, dq_0)
    dq_0, dk_0, dv_0 = back(0, grad_0, (), True, dq_0, True)
    came, keep, grads = tie(
        (d_came, u_came, o_came), (d_keep, u_keep, o_keep), (dq_0, dk_0, dv_0, q_send)
    )
    d_came, u_came, o_came = came
    d_keep, u_keep, o_keep = keep
    dq_0, dk_0, dv_0, q_send = grads
    dqkv_0 = jnp.concatenate([dq_0, dk_0, dv_0], 1)
    q_cur = weight_part(dqkv_0, jnp.concatenate([dkvp_a, dkvp_b], 0))
    q_came, q_keep = swap(pick(q_cur, 1 - core, 2), CORE), pick(q_cur, core, 2)
    own_sum = own_sum + dot(dqkv_0, qkv[0], NT)
    q_came, q_keep, own_sum, q_send = tie(q_came, q_keep, own_sum, q_send)
    q_cur = plus(q_keep, q_came)
    q_came, q_keep = swap(pick(q_cur, 1 - near, 1), NEAR), pick(q_cur, near, 1)
    q_keep, own_sum, came_b, q_send = tie(q_keep, own_sum, came_b, q_send)
    q_other = swap(q_send, TENSOR)
    input_grad, last_sums = last(
        info,
        block_input,
        own_sum,
        jnp.concatenate([sum_a, sum_b], 0),
        jnp.concatenate([came_a, came_b], 0),
        middle_grad,
        mods,
    )
    last_sums, d_keep, u_keep, q_came, q_other, q_keep = tie(
        last_sums, d_keep, u_keep, q_came, q_other, q_keep
    )
    q_cur = q_keep.astype(f32) + q_came.astype(f32) + q_other.astype(f32)
    q_cur = q_cur.reshape((2,) * len(low_bits) + q_cur.shape[1:])

    def q_step(cur, bit):
        mine = (far // bit) % 2
        cur = cur.astype(bf16)
        return pick(cur, mine, cur.ndim - 3), swap(pick(cur, 1 - mine, cur.ndim - 3), 8 * bit)

    q_keep, q_came = q_step(q_cur, low_bits[0])
    down_grad = (d_keep.astype(f32) + d_came.astype(f32))[0]
    up_grad = (u_keep.astype(f32) + u_came.astype(f32))[0]
    o_keep, o_came = far_end(o_keep, o_came)
    out_grad = (o_keep.astype(f32) + o_came.astype(f32))[0]
    order = [last_sums[:, 0], last_sums[:, 1]] + [post_sums[:, n] for n in range(4)]
    sums = jnp.stack(order, 1).reshape(tiles, 6 * width)
    first_row = (jnp.arange(tiles) == 0)[:, None]
    prompt_sums = jnp.where(first_row, jnp.sum(sums, 0, keepdims=True), 0.0)
    segment_sums = jnp.where(is_prompt, prompt_sums, sums).astype(bf16)

    local = jnp.concatenate(
        [
            jnp.sum(post_sums[:, 4:7], (0, 2)),
            (jnp.sum(own_len) * width).astype(f32).reshape(1),
        ]
    )
    local = jnp.concatenate(split_three(local))
    local = jnp.pad(local, (0, col_width - 12)).astype(bf16)
    packet = segment_sums.reshape(tiles, devices, col_width).transpose(1, 0, 2)
    packet = jnp.concatenate(
        [packet, jnp.broadcast_to(local[None, None], (devices, 1, col_width))], 1
    )
    packet = jnp.pad(packet, ((0, 0), (0, 16 - packet.shape[1]), (0, 0)))
    packets = lax.all_to_all(packet, BOTH, 0, 0, tiled=True)
    packets, q_keep, q_came = tie(packets, q_keep, q_came)
    q_cur = q_keep.astype(f32) + q_came.astype(f32)
    for bit in low_bits[1:]:
        q_keep, q_came = q_step(q_cur, bit)
        q_cur = q_keep.astype(f32) + q_came.astype(f32)
    totals = jnp.sum(packets[:, tiles, :12].astype(f32), 0)
    totals = totals[:4] + totals[4:8] + totals[8:12]
    stats = jnp.sqrt(totals[:3] / totals[3])

    grads = packets[:, :tiles].reshape(devices * tiles, col_width)
    cond_groups = cond.reshape(dp_count, 16, width)
    own_steps = step_pad.reshape(dp_count, 16)
    cond_rows = jnp.stack([cond_groups[:, :tiles], cond_groups[:, 1 : 1 + tiles]], 1)
    step_slots = jnp.stack([own_steps[:, :tiles], own_steps[:, 1 : 1 + tiles]], 1).reshape(-1)
    mod_grad = dot(cond_rows.reshape(devices * tiles, width), grads, TN)
    condition_grad = dot(grads, w_mod, NT)
    slot_pick = (step_slots[:, None] == jnp.arange(STEPS, dtype=jnp.int32)[None, :]).astype(f32)
    table_part = lax.dot_general(
        slot_pick,
        condition_grad,
        TN,
        precision=lax.Precision.HIGHEST,
        preferred_element_type=f32,
    )
    table_pieces = lax.all_to_all(
        table_part.astype(bf16).reshape(devices, table_rows, width), BOTH, 0, 0, tiled=True
    )
    table_grad = jnp.sum(table_pieces.astype(f32), 0)
    return (
        block_output,
        input_grad,
        q_cur.reshape(w_qkv.shape),
        out_grad.T,
        up_grad,
        down_grad.T,
        mod_grad,
        table_grad,
        stats,
    )


def solution(mesh):
    return jax.shard_map(
        body,
        mesh=mesh,
        in_specs=(
            P(("dp", "tensor"), None),
            P(("dp", "tensor"), None),
            P("dp", None, "tensor"),
            P("tensor", "dp"),
            P("dp", "tensor"),
            P("tensor", "dp"),
            P(None, ("dp", "tensor")),
            P(("dp", "tensor"), None),
            P("dp"),
            P("dp", None),
            P("dp", None),
        ),
        out_specs=(
            P(("dp", "tensor"), None),
            P(("dp", "tensor"), None),
            P("dp", None, "tensor"),
            P("tensor", "dp"),
            P("dp", "tensor"),
            P("tensor", "dp"),
            P(None, ("dp", "tensor")),
            P(("dp", "tensor"), None),
            P(),
        ),
        check_vma=False,
    )
```

```python
import math

import jax
import jax.numpy as jnp
from jax import lax
from jax.experimental import pallas as pl
from jax.experimental.pallas import tpu as pltpu
from jax.sharding import PartitionSpec as P

HEAD_DIM = 64
PROMPT = 1024
CONT = 128
NCONT = 8
STEPS = 256
SEGS = 1 + NCONT

bf16 = jnp.bfloat16
f32 = jnp.float32
NN = (((1,), (0,)), ((), ()))
NT = (((1,), (1,)), ((), ()))
TN = (((0,), (0,)), ((), ()))
SCALE = HEAD_DIM ** (-0.5)
SCALE2 = SCALE * math.log2(math.e)
NEG = -1e30


def dot(left, right, dims=NN):
    return lax.dot_general(left, right, dims, preferred_element_type=f32)


def lanes(shape):
    return lax.broadcasted_iota(jnp.int32, shape, 1)


def rows(shape):
    return lax.broadcasted_iota(jnp.int32, shape, 0)


BOTH = ("dp", "tensor")
TENSOR, CORE, NEAR = 1, 2, 4
LONG = pl.CostEstimate(flops=10**11, bytes_accessed=1, transcendentals=0)


def swap(x, bits):
    count = lax.axis_size(BOTH)
    return lax.ppermute(x, BOTH, [(i, i ^ bits) for i in range(count)])


def tie(*arrays):
    return lax.optimization_barrier(arrays)


def after(array, *others):
    return lax.optimization_barrier((array,) + others)[0]


def far_count():
    return lax.axis_size("dp") // 4


def far_bits():
    return [1 << k for k in range(far_count().bit_length() - 1)]


def plus(left, right):
    return (left.astype(f32) + right.astype(f32)).astype(bf16)


def send_far(cur):
    cur = cur.reshape((-1, 2) + cur.shape[1:])
    return cur[:, 0], cur[:, 1]


def join_kernel(cuts, bit_ref, own_ref, came_ref, *out_refs):
    bit = bit_ref[0]
    start = 0
    for out_ref, cut in zip(out_refs, cuts):
        for n in range(own_ref.shape[0]):
            out_ref[n, bit] = own_ref[n, :, start : start + cut]
            out_ref[n, 1 - bit] = came_ref[n, :, start : start + cut]
        start += cut


def join(own, came, bit, cuts=None):
    count, rows_each, columns = own.shape
    sizes = cuts or (columns,)
    group = min(count, 2)
    spec = pl.BlockSpec((group, rows_each, columns), lambda n, s: (n, 0, 0))
    outs = pl.pallas_call(
        lambda *refs: join_kernel(sizes, *refs),
        grid_spec=pltpu.PrefetchScalarGridSpec(
            num_scalar_prefetch=1,
            grid=(count // group,),
            in_specs=[spec, spec],
            out_specs=[
                pl.BlockSpec((group, 2, rows_each, cut), lambda n, s: (n, 0, 0, 0)) for cut in sizes
            ],
        ),
        out_shape=[jax.ShapeDtypeStruct((count, 2, rows_each, cut), bf16) for cut in sizes],
        cost_estimate=pl.CostEstimate(flops=1, bytes_accessed=10**6, transcendentals=0),
        compiler_params=pltpu.CompilerParams(vmem_limit_bytes=16 * 2**20),
        name="join",
    )(bit.astype(jnp.int32).reshape(1), own, came)
    outs = [out.reshape(2 * count, rows_each, -1) for out in outs]
    return outs if cuts else outs[0]


def turn(x, cosine, sine):
    lane = lanes(x.shape) % 64
    swapped = jnp.where(lane < 32, -pltpu.roll(x, 96, 1), pltpu.roll(x, 32, 1))
    return x * cosine + swapped * sine


def turn_back(x, cosine, sine):
    lane = lanes(x.shape) % 64
    swapped = jnp.where(lane < 32, pltpu.roll(x, 96, 1), -pltpu.roll(x, 32, 1))
    return x * cosine + swapped * sine


def norm_parts(inputs):
    average = jnp.mean(inputs, -1, keepdims=True)
    centred = inputs - average
    spread = jnp.mean(centred * centred, -1, keepdims=True)
    inverse = lax.rsqrt(spread + 1e-05)
    return centred * inverse, inverse


def norm_back(unit, inverse, grad, scales):
    inner = grad * (1.0 + scales)
    first = jnp.mean(inner, -1, keepdims=True)
    second = jnp.mean(inner * unit, -1, keepdims=True)
    return inverse * (inner - first - unit * second)


def modulation(mods_ref, info, tile, part):
    segment = jnp.where(info[0] == 0, 0, 1 + tile)
    width = mods_ref.shape[1] // 6
    return mods_ref[pl.ds(segment, 1), part * width : (part + 1) * width]


def store_pieces(total, info, keep_ref, send_ref, lead):
    half, rows_each = keep_ref.shape[-3], keep_ref.shape[-2]
    fars = half // 2
    for k in range(half):
        low = total[2 * k * rows_each : (2 * k + 1) * rows_each]
        high = total[(2 * k + 1) * rows_each : (2 * k + 2) * rows_each]
        place = ((k % 2) ^ info[11]) * fars + ((k // 2) ^ info[12])
        keep_ref[lead + (place,)] = jnp.where(info[10] == 0, low, high).astype(bf16)
        send_ref[lead + (place,)] = jnp.where(info[10] == 0, high, low).astype(bf16)


def fill(source_ref, w_refs, out_ref, tables):
    for half, w_ref in enumerate(w_refs):
        pl.when(pl.program_id(0) == half)(lambda w_ref=w_ref: fill_half(source_ref, w_ref, out_ref, tables))


def fill_half(source_ref, w_ref, out_ref, tables):
    joined = dot(source_ref[...], w_ref[...])
    for c in range(joined.shape[1] // 128):
        cut = slice(c * 128, (c + 1) * 128)
        piece = joined[:, cut]
        if tables:
            piece = turn(piece, tables[0][...], tables[1][...])
        out_ref[0, :, cut] = piece.astype(bf16)


def project_own_kernel(info, x_ref, mods_ref, *refs):
    w_ref, (cos_ref, sin_ref, joined_ref, normed_ref) = refs[:2], refs[2:]
    half, part = pl.program_id(0), pl.program_id(1)

    @pl.when((half == 0) & (part == 0))
    def _():
        for i in range(x_ref.shape[0] // CONT):
            cut = slice(i * CONT, (i + 1) * CONT)
            unit, _ = norm_parts(x_ref[cut, :].astype(f32))
            shift, scale = (modulation(mods_ref, info, i, n) for n in range(2))
            normed_ref[cut, :] = (unit * (1.0 + scale) + shift).astype(bf16)

    pl.when(part < 2)(lambda: fill(normed_ref, w_ref, joined_ref, (cos_ref, sin_ref)))
    pl.when(part == 2)(lambda: fill(normed_ref, w_ref, joined_ref, None))


def project_prompt_kernel(info, x_ref, *refs):
    came_refs, (mods_ref, *w_ref, cos_ref, sin_ref, joined_ref, normed_ref) = refs[:-7], refs[-7:]
    half, part = pl.program_id(0), pl.program_id(1)
    width = x_ref.shape[1]

    @pl.when((half == 0) & (part == 0))
    def _():
        shift, scale = mods_ref[0:1, :width], mods_ref[0:1, width : 2 * width]
        for i in range(x_ref.shape[0] // CONT):
            cut = slice(i * CONT, (i + 1) * CONT)
            place = i * CONT
            for came_ref in came_refs:
                if 0 <= place < came_ref.shape[0]:
                    came = came_ref[place : place + CONT, :].astype(f32)
                place -= came_ref.shape[0]
            x = jnp.where(info[0] == 0, x_ref[cut, :].astype(f32), came)
            unit, _ = norm_parts(x)
            normed_ref[cut, :] = (unit * (1.0 + scale) + shift).astype(bf16)

    pl.when(part == 0)(lambda: fill(normed_ref, w_ref, joined_ref, (cos_ref, sin_ref)))
    pl.when(part == 1)(lambda: fill(normed_ref, w_ref, joined_ref, None))


def project(kernel, parts, estimate, info, inputs, mods, qkv, tables):
    count, width = inputs[0].shape
    head_width = qkv[0].shape[1] // 3

    def whole(array):
        return pl.BlockSpec(array.shape, lambda t, p, s: (0,) * array.ndim)

    def weight(half):
        def place(t, p, s):
            now = p + 3 - parts
            return (0, jnp.where(t == half, now, 2 if half == 0 else 3 - parts))

        return pl.BlockSpec((width, head_width), place)

    return pl.pallas_call(
        kernel,
        grid_spec=pltpu.PrefetchScalarGridSpec(
            num_scalar_prefetch=1,
            grid=(2, parts),
            in_specs=[whole(array) for array in inputs]
            + [whole(mods), weight(0), weight(1)]
            + [whole(table) for table in tables],
            out_specs=[
                pl.BlockSpec((1, count, head_width), lambda t, p, s: (t, 0, p)),
                whole(inputs[0]),
            ],
        ),
        out_shape=[
            jax.ShapeDtypeStruct((2, count, parts * head_width), bf16),
            jax.ShapeDtypeStruct((count, width), bf16),
        ],
        compiler_params=pltpu.CompilerParams(vmem_limit_bytes=20 * 2**20),
        cost_estimate=estimate,
        name="project",
    )(info, *inputs, mods, *qkv, *tables)


def middle_kernel(
    info, x_ref, a0_ref, a1_ref, mods_ref, o0_ref, o1_ref, branch_ref, middle_ref, n2_ref
):
    branch = dot(a0_ref[...], o0_ref[...], NT) + dot(a1_ref[...], o1_ref[...], NT)
    branch_ref[...] = branch
    per = x_ref.shape[0] // CONT
    for u in range(per):
        cut = slice(u * CONT, (u + 1) * CONT)
        gate, shift, scale = (
            modulation(mods_ref, info, pl.program_id(0) * per + u, n) for n in (2, 3, 4)
        )
        middle = x_ref[cut, :].astype(f32) + gate * branch[cut]
        middle_ref[cut, :] = middle
        unit, _ = norm_parts(middle)
        n2_ref[cut, :] = (unit * (1.0 + scale) + shift).astype(bf16)


def middle_norm(info, x, attended, mods, out_t):
    count, width = x.shape
    head_width = attended[0].shape[1]
    tile = 256
    by_row = pl.BlockSpec((tile, width), lambda i, s: (i, 0))
    by_head = pl.BlockSpec((tile, head_width), lambda i, s: (i, 0))
    return pl.pallas_call(
        middle_kernel,
        grid_spec=pltpu.PrefetchScalarGridSpec(
            num_scalar_prefetch=1,
            grid=(count // tile,),
            in_specs=[
                by_row,
                by_head,
                by_head,
                pl.BlockSpec(mods.shape, lambda i, s: (0, 0)),
                pl.BlockSpec((width, head_width), lambda i, s: (0, 0)),
                pl.BlockSpec((width, head_width), lambda i, s: (0, 0)),
            ],
            out_specs=[by_row] * 3,
        ),
        out_shape=[
            jax.ShapeDtypeStruct((count, width), f32),
            jax.ShapeDtypeStruct((count, width), f32),
            jax.ShapeDtypeStruct((count, width), bf16),
        ],
        compiler_params=pltpu.CompilerParams(vmem_limit_bytes=32 * 2**20),
        cost_estimate=LONG,
        name="middle_norm",
    )(info, x, *attended, mods, *out_t)


def mlp_kernel(first, whole_weights, info, n2_ref, *refs):
    if first:
        cot_ref, mods_ref = refs[:2]
        refs = refs[2:]
    else:
        n2_turned, out_grad, out_turned, branch_before, grad_before = refs[:5]
        refs = refs[5:]
    weight_refs, refs = refs[:whole_weights], refs[whole_weights:]
    branch_ref, grad_ref = refs[:2]
    down_keep_ref, down_send_ref, up_keep_ref, up_send_ref = refs[2:6]
    if first:
        n2_turned, out_grad, out_turned = refs[6:9]
    hidden, pre_grad, *joined = refs[-4:] if whole_weights == 4 else refs[-2:]
    count = n2_ref.shape[0]

    @pl.when(pl.program_id(0) == 0)
    def _():
        if first:
            for i in range(count // CONT):
                cut = slice(i * CONT, (i + 1) * CONT)
                gate = modulation(mods_ref, info, i, 5)
                out_grad[cut, :] = (cot_ref[cut, :].astype(f32) * gate).astype(bf16)
            n2_turned[...] = jnp.transpose(n2_ref[...])
            out_turned[...] = jnp.transpose(out_grad[...])
            branch_ref[...] = jnp.zeros_like(branch_ref)
            grad_ref[...] = jnp.zeros_like(grad_ref)
        else:
            branch_ref[...] = branch_before[...]
            grad_ref[...] = grad_before[...]

    if joined:
        for n, out_ref in enumerate(joined):
            own_ref, came_ref = weight_refs[2 * n : 2 * n + 2]
            rows_each = own_ref.shape[1]
            for k in range(own_ref.shape[0]):
                own, came = own_ref[k], came_ref[k]
                start = 2 * k * rows_each
                out_ref[start : start + rows_each, :] = jnp.where(info[10] == 0, own, came)
                start += rows_each
                out_ref[start : start + rows_each, :] = jnp.where(info[10] == 0, came, own)
        up, down = joined[0][...], joined[1][...]
    else:
        up, down = weight_refs[0][...], weight_refs[1][...]
    tile = 256
    for i in range(count // tile):
        cut = slice(i * tile, (i + 1) * tile)
        pre = dot(n2_ref[cut, :], up)
        cdf = 0.5 * (1.0 + lax.erf(pre * (2.0**-0.5)))
        pdf = jnp.exp(-0.5 * pre * pre) * ((2.0 * math.pi) ** -0.5)
        value = (pre * cdf).astype(bf16)
        hidden[cut, :] = value
        grad = (dot(out_grad[cut, :], down) * (cdf + pre * pdf)).astype(bf16)
        pre_grad[cut, :] = grad
        branch_ref[cut, :] += dot(value, down, NT)
        grad_ref[cut, :] += dot(grad, up, NT)
    store_pieces(dot(out_turned[...], hidden[...]), info, down_keep_ref, down_send_ref, ())
    store_pieces(dot(n2_turned[...], pre_grad[...]), info, up_keep_ref, up_send_ref, ())


def feed_forward(info, n2, sources, weights):
    count, width = n2.shape
    hidden_width = weights[0].shape[-1]
    first = len(sources) == 2
    cols = 384
    dp_count = lax.axis_size("dp")
    pieces = (dp_count // 2, width // dp_count, hidden_width)

    def whole(array):
        return pl.BlockSpec(
            array.shape, lambda b, s: (0,) * array.ndim, pipeline_mode=pl.Buffered(1)
        )

    piece_spec = pl.BlockSpec(pieces[:2] + (cols,), lambda b, s: (0, 0, b))
    weight_specs = [
        pl.BlockSpec(w.shape[:-1] + (cols,), lambda b, s, lead=w.ndim - 1: (0,) * lead + (b,))
        for w in weights
    ]
    scratch = [pltpu.VMEM((count, cols), bf16)] * 2
    if len(weights) == 4:
        scratch += [pltpu.VMEM((width, cols), bf16)] * 2
    outs = [jax.ShapeDtypeStruct((count, width), f32)] * 2 + [
        jax.ShapeDtypeStruct(pieces, bf16)
    ] * 4
    out_specs = [whole(n2)] * 2 + [piece_spec] * 4
    if first:
        shapes = [(width, count), (count, width), (width, count)]
        outs += [jax.ShapeDtypeStruct(shape, bf16) for shape in shapes]
        out_specs += [pl.BlockSpec(shape, lambda b, s: (0, 0)) for shape in shapes]
    return pl.pallas_call(
        lambda *refs: mlp_kernel(first, len(weights), *refs),
        grid_spec=pltpu.PrefetchScalarGridSpec(
            num_scalar_prefetch=1,
            grid=(hidden_width // cols,),
            in_specs=[whole(n2)] + [whole(array) for array in sources] + weight_specs,
            out_specs=out_specs,
            scratch_shapes=scratch,
        ),
        out_shape=outs,
        compiler_params=pltpu.CompilerParams(vmem_limit_bytes=52 * 2**20),
        cost_estimate=LONG,
        name="feed_forward",
    )(info, n2, *sources, *weights)


def post_kernel(
    info,
    middle_ref,
    branch_ref,
    mlp_ref,
    n2_grad_ref,
    cot_ref,
    a0_ref,
    a1_ref,
    mods_ref,
    o0_ref,
    o1_ref,
    out_ref,
    middle_grad_ref,
    g0_ref,
    g1_ref,
    sums_ref,
    keep_ref,
    send_ref,
    total,
    attn_grad,
):
    step = pl.program_id(0)
    per = middle_ref.shape[0] // CONT
    for u in range(per):
        cut = slice(u * CONT, (u + 1) * CONT)
        tile = step * per + u
        gate1, scale2, gate2 = (modulation(mods_ref, info, tile, n) for n in (2, 4, 5))
        middle, branch, mlp = middle_ref[cut, :], branch_ref[cut, :], mlp_ref[cut, :]
        n2_grad, upstream = n2_grad_ref[cut, :], cot_ref[cut, :].astype(f32)
        mlp_part, attn_part = gate2 * mlp, gate1 * branch
        result = middle + mlp_part
        out_ref[cut, :] = result.astype(bf16)
        unit, inverse = norm_parts(middle)
        middle_grad = upstream + norm_back(unit, inverse, n2_grad, scale2)
        middle_grad_ref[cut, :] = middle_grad
        attn_grad[cut, :] = (middle_grad * gate1).astype(bf16)
        valid = (rows((CONT, 1)) < info[2 + tile]).astype(f32)
        for n, value in enumerate(
            (
                middle_grad * branch,
                n2_grad,
                n2_grad * unit,
                upstream * mlp,
                valid * result * result,
                valid * attn_part * attn_part,
                valid * mlp_part * mlp_part,
            )
        ):
            sums_ref[u, n : n + 1, :] = jnp.sum(value, 0, keepdims=True)
        sums_ref[u, 7:8, :] = jnp.zeros_like(gate1)
    halves = ((a0_ref, g0_ref, o0_ref), (a1_ref, g1_ref, o1_ref))
    for t, (a_ref, g_ref, o_ref) in enumerate(halves):
        g_ref[...] = dot(attn_grad[...], o_ref[...]).astype(bf16)
        part = dot(attn_grad[...], a_ref[...], TN)
        total[t] = jnp.where(step == 0, part, total[t] + part)

    @pl.when(step == pl.num_programs(0) - 1)
    def _():
        for t in range(2):
            store_pieces(total[t], info, keep_ref, send_ref, (t,))


def post(info, middle, branch, mlp, n2_grad, cotangent, attended, mods, out_t):
    count, width = middle.shape
    head_width = attended[0].shape[1]
    tile = 256
    tiles = count // CONT
    dp_count = lax.axis_size("dp")
    pieces = (2, dp_count // 2, width // dp_count, head_width)
    by_row = pl.BlockSpec((tile, width), lambda i, s: (i, 0))
    by_head = pl.BlockSpec((tile, head_width), lambda i, s: (i, 0))
    return pl.pallas_call(
        post_kernel,
        grid_spec=pltpu.PrefetchScalarGridSpec(
            num_scalar_prefetch=1,
            grid=(count // tile,),
            in_specs=[by_row] * 5
            + [
                by_head,
                by_head,
                pl.BlockSpec(mods.shape, lambda i, s: (0, 0)),
                pl.BlockSpec((width, head_width), lambda i, s: (0, 0)),
                pl.BlockSpec((width, head_width), lambda i, s: (0, 0)),
            ],
            out_specs=[
                by_row,
                by_row,
                by_head,
                by_head,
                pl.BlockSpec((tile // CONT, 8, width), lambda i, s: (i, 0, 0)),
                pl.BlockSpec(pieces, lambda i, s: (0, 0, 0, 0)),
                pl.BlockSpec(pieces, lambda i, s: (0, 0, 0, 0)),
            ],
            scratch_shapes=[
                pltpu.VMEM((2, width, head_width), f32),
                pltpu.VMEM((tile, width), bf16),
            ],
        ),
        out_shape=[
            jax.ShapeDtypeStruct((count, width), bf16),
            jax.ShapeDtypeStruct((count, width), f32),
            jax.ShapeDtypeStruct((count, head_width), bf16),
            jax.ShapeDtypeStruct((count, head_width), bf16),
            jax.ShapeDtypeStruct((tiles, 8, width), f32),
            jax.ShapeDtypeStruct(pieces, bf16),
            jax.ShapeDtypeStruct(pieces, bf16),
        ],
        compiler_params=pltpu.CompilerParams(vmem_limit_bytes=48 * 2**20),
        cost_estimate=LONG,
        name="post",
    )(info, middle, branch, mlp, n2_grad, cotangent, *attended, mods, *out_t)


def last_kernel(
    info, x_ref, own_ref, prompt_ref, came_ref, middle_grad_ref, mods_ref, out_ref, sums_ref
):
    step = pl.program_id(0)
    per = x_ref.shape[0] // CONT
    for u in range(per):
        cut = slice(u * CONT, (u + 1) * CONT)
        scale = modulation(mods_ref, info, step * per + u, 1)
        prompt = prompt_ref[cut, :] + came_ref[cut, :].astype(f32)
        grad = own_ref[cut, :] + jnp.where(info[0] == 0, prompt, 0.0)
        unit, inverse = norm_parts(x_ref[cut, :].astype(f32))
        sums_ref[u, 0:1, :] = jnp.sum(grad, 0, keepdims=True)
        sums_ref[u, 1:2, :] = jnp.sum(grad * unit, 0, keepdims=True)
        sums_ref[u, 2:, :] = jnp.zeros((6, x_ref.shape[1]), f32)
        out_ref[cut, :] = middle_grad_ref[cut, :] + norm_back(unit, inverse, grad, scale)


def last(info, x, own_sum, prompt_sum, came, middle_grad, mods):
    count, width = x.shape
    tile = 256
    by_row = pl.BlockSpec((tile, width), lambda i, s: (i, 0))
    return pl.pallas_call(
        last_kernel,
        grid_spec=pltpu.PrefetchScalarGridSpec(
            num_scalar_prefetch=1,
            grid=(count // tile,),
            in_specs=[by_row] * 5 + [pl.BlockSpec(mods.shape, lambda i, s: (0, 0))],
            out_specs=[by_row, pl.BlockSpec((tile // CONT, 8, width), lambda i, s: (i, 0, 0))],
        ),
        out_shape=[
            jax.ShapeDtypeStruct((count, width), f32),
            jax.ShapeDtypeStruct((count // CONT, 8, width), f32),
        ],
        compiler_params=pltpu.CompilerParams(vmem_limit_bytes=16 * 2**20),
        cost_estimate=LONG,
        name="last",
    )(info, x, own_sum, prompt_sum, came, middle_grad, mods)


def forward_kernel(info, *refs):
    q_ref, kp_ref, vp_ref, ko_ref, vo_ref = (ref.at[0] for ref in refs[:5])
    o_ref, lse_ref = refs[5:]
    role = info[0]
    prompt_count = info[1]
    count = q_ref.shape[0]
    lane = lanes((count, 128))
    row = rows((count, 128))
    tile = 256
    blocks = count // tile

    def prepare(h):
        sel = (lane // 64) == h
        extra = 64 * (1 - h)
        q = jnp.where(sel, q_ref[...], jnp.where(lane == extra, 1.0, 0.0).astype(bf16))
        bias = jnp.where((lane == extra) & (row >= prompt_count), NEG, 0.0).astype(bf16)
        k = jnp.where(sel, kp_ref[...], bias)
        v = jnp.where(sel, vp_ref[...], jnp.ones((), bf16))
        return sel, q, k, v

    def finish(h, i, o, top):
        extra = 64 * (1 - h)
        weight = o[:, extra : extra + 1]
        lse = top * SCALE2 + jnp.log2(weight)
        turned = jnp.transpose(jnp.broadcast_to(lse, (tile, 128)))
        lse_ref[0, h : h + 1, i * tile : (i + 1) * tile] = turned[0:1, :]
        return o * (1.0 / weight)

    def store(outs):
        for i in range(blocks):
            merged = jnp.where(lanes((tile, 128)) < 64, outs[0][i], outs[1][i])
            o_ref[i * tile : (i + 1) * tile, :] = merged.astype(bf16)

    @pl.when(role == 0)
    def _():
        outs = []
        for h in range(2):
            sel, q, k, v = prepare(h)
            heads = []
            for i in range(blocks):
                start, stop = i * tile, (i + 1) * tile
                s = dot(q[start:stop], k[:stop], NT)
                near = jnp.where(lanes((tile, tile)) <= rows((tile, tile)), s[:, start:], NEG)
                top = jnp.max(near, 1, keepdims=True)
                if i:
                    top = jnp.maximum(top, jnp.max(s[:, :start], 1, keepdims=True))
                o = dot(jnp.exp2(near * SCALE2 - top * SCALE2).astype(bf16), v[start:stop])
                if i:
                    o = o + dot(
                        jnp.exp2(s[:, :start] * SCALE2 - top * SCALE2).astype(bf16), v[:start]
                    )
                heads.append(finish(h, i, o, top))
            outs.append(heads)
        store(outs)

    @pl.when(role != 0)
    def _():
        outs = []
        for h in range(2):
            sel, q, k, v = prepare(h)
            own_k = jnp.where(sel, ko_ref[...], jnp.zeros((), bf16))
            own_v = jnp.where(sel, vo_ref[...], jnp.ones((), bf16))
            heads, far, near, tops = [], [], [], []
            col, line = lanes((CONT, CONT)), rows((CONT, CONT))
            cuts = [slice(r, r + CONT) for r in range(0, count, CONT)]
            for n, cut in enumerate(cuts):
                fine = (col <= line) & (col < info[2 + n])
                near.append(jnp.where(fine, dot(q[cut], own_k[cut], NT), NEG))
            near = jnp.concatenate(near, 0)
            near_tops = jnp.max(near, 1, keepdims=True)
            for i in range(blocks):
                cut = slice(i * tile, (i + 1) * tile)
                s = dot(q[cut], k, NT)
                tops.append(jnp.maximum(jnp.max(s, 1, keepdims=True), near_tops[cut]))
                far.append(dot(jnp.exp2(s * SCALE2 - tops[i] * SCALE2).astype(bf16), v))
            weight = jnp.exp2(near * SCALE2 - jnp.concatenate(tops, 0) * SCALE2).astype(bf16)
            own = jnp.concatenate([dot(weight[cut], own_v[cut]) for cut in cuts], 0)
            for i in range(blocks):
                heads.append(finish(h, i, far[i] + own[i * tile : (i + 1) * tile], tops[i]))
            outs.append(heads)
        store(outs)


def attend(info, joined, prompts, t):
    count = joined.shape[1]
    head_width = joined.shape[2] // 3
    pairs = head_width // 128

    def spec(offset):
        return pl.BlockSpec((1, count, 128), lambda h, s: (t, 0, offset + h))

    return pl.pallas_call(
        forward_kernel,
        grid_spec=pltpu.PrefetchScalarGridSpec(
            num_scalar_prefetch=1,
            grid=(pairs,),
            in_specs=[spec(0), spec(0), spec(pairs), spec(pairs), spec(2 * pairs)],
            out_specs=[
                pl.BlockSpec((count, 128), lambda h, s: (0, h)),
                pl.BlockSpec((1, 2, count), lambda h, s: (h, 0, 0)),
            ],
        ),
        out_shape=[
            jax.ShapeDtypeStruct((count, head_width), bf16),
            jax.ShapeDtypeStruct((pairs, 2, count), f32),
        ],
        compiler_params=pltpu.CompilerParams(vmem_limit_bytes=20 * 2**20),
        cost_estimate=LONG,
        name="attend",
    )(info, joined, prompts, prompts, joined, joined)


def backward_kernel(first, last, tiles, own, info, *refs):
    refs = list(refs)
    q_ref, do_ref, o_ref, lse_ref = refs[0].at[0], *refs[1:4]
    del refs[:4]
    if tiles:
        kp_ref, vp_ref, cp_ref, sp_ref = refs[0].at[0], refs[1].at[0], *refs[2:4]
        del refs[:4]
    if own:
        ko_ref, vo_ref = refs[0].at[0], refs[1].at[0]
        del refs[:2]
    if own or last:
        co_ref, so_ref = refs[:2]
        del refs[:2]
    before_ref = None if first else refs.pop(0)
    dq_ref = refs.pop(0)
    if tiles:
        dkp_ref, dvp_ref = refs[:2]
        del refs[:2]
    if own:
        dko_ref, dvo_ref = refs[:2]
        del refs[:2]
    (dq_acc,) = refs
    role = info[0]
    prompt_count = info[1]
    count = q_ref.shape[0]
    tile = 256
    lane = lanes((count, 128))
    none = jnp.zeros((), bf16)
    products = jnp.transpose(do_ref[...].astype(f32) * o_ref[...].astype(f32))
    deltas = [jnp.sum(products[64 * h : 64 * h + 64], 0, keepdims=True) for h in range(2)]
    dq_acc[...] = jnp.zeros_like(dq_acc) if first else before_ref[...]

    def far_block(j, prompt):
        start, stop = j * tile, (j + 1) * tile
        cut = slice(start - tiles[0] * tile, stop - tiles[0] * tile)
        q_from = start if prompt else 0
        lane_k = lanes((tile, 128))
        row_k = rows((tile, 128)) + start
        key_parts, value_parts = [], []
        for h in range(2):
            extra = 64 * (1 - h)
            sel = (lane_k // 64) == h
            bias = jnp.where((lane_k == extra) & (row_k >= prompt_count), NEG, 0.0).astype(bf16)
            k = jnp.where(sel, kp_ref[cut, :], bias)
            k_plain = jnp.where(sel, kp_ref[cut, :], none)
            v = jnp.where(sel, vp_ref[cut, :], none)
            lane_q = lane[q_from:]
            ones = jnp.where(lane_q == extra, 1.0, 0.0).astype(bf16)
            q = jnp.where((lane_q // 64) == h, q_ref[q_from:, :], ones)
            s = dot(k, q, NT)
            if prompt:
                near = jnp.where(rows((tile, tile)) <= lanes((tile, tile)), s[:, :tile], NEG)
                s = jnp.concatenate([near, s[:, tile:]], 1) if stop < count else near
            weight = jnp.exp2(s * SCALE2 - lse_ref[0, h : h + 1, q_from:])
            grad = dot(v, do_ref[q_from:, :], NT)
            score = (weight * (grad - deltas[h][:, q_from:])).astype(bf16)
            value_parts.append(dot(weight.astype(bf16), do_ref[q_from:, :]))
            key_parts.append(dot(score, q_ref[q_from:, :]))
            dq_acc[q_from:, :] += dot(score, k_plain, TN)
        key_grad = jnp.where(lane_k < 64, key_parts[0], key_parts[1]) * SCALE
        value_grad = jnp.where(lane_k < 64, value_parts[0], value_parts[1])
        dkp_ref[cut, :] = turn_back(key_grad, cp_ref[cut, :], sp_ref[cut, :]).astype(bf16)
        dvp_ref[cut, :] = value_grad.astype(bf16)

    @pl.when(role == 0)
    def _():
        for j in tiles:
            far_block(j, True)
        if own:
            dko_ref[...] = jnp.zeros_like(dko_ref)
            dvo_ref[...] = jnp.zeros_like(dvo_ref)

    @pl.when(role != 0)
    def _():
        for j in tiles:
            far_block(j, False)
        lane_k = lanes((CONT, CONT))
        row_k = rows((CONT, CONT))
        every = range(count // CONT if own else 0)
        cuts = [slice(i * CONT, (i + 1) * CONT) for i in every]
        key_parts, value_parts = [], []
        for h in range(2 if own else 0):
            sel = (lane // 64) == h
            k = jnp.where(sel, ko_ref[...], none)
            v = jnp.where(sel, vo_ref[...], none)
            scores, weights = [], []
            for i, cut in enumerate(cuts):
                fine = (row_k <= lane_k) & (row_k < info[2 + i])
                scores.append(jnp.where(fine, dot(k[cut], q_ref[cut, :], NT), NEG) * SCALE2 - lse_ref[0, h : h + 1, cut])
            weight = jnp.exp2(jnp.concatenate(scores, 0))
            grad = jnp.concatenate([dot(v[cut], do_ref[cut, :], NT) - deltas[h][:, cut] for cut in cuts], 0)
            score = (weight * grad).astype(bf16)
            weight = weight.astype(bf16)
            value_parts.append([dot(weight[cut], do_ref[cut, :]) for cut in cuts])
            key_parts.append([dot(score[cut], q_ref[cut, :]) for cut in cuts])
            for cut in cuts:
                dq_acc[cut, :] += dot(score[cut], k[cut], TN)
        for i, cut in enumerate(cuts):
            key_grad = jnp.where(lane_k < 64, key_parts[0][i], key_parts[1][i]) * SCALE
            value_grad = jnp.where(lane_k < 64, value_parts[0][i], value_parts[1][i])
            dko_ref[cut, :] = turn_back(key_grad, co_ref[cut, :], so_ref[cut, :]).astype(bf16)
            dvo_ref[cut, :] = value_grad.astype(bf16)

    if last:
        dq_ref[...] = turn_back(dq_acc[...] * SCALE, co_ref[...], so_ref[...]).astype(bf16)
    else:
        dq_ref[...] = dq_acc[...]


def attend_back(info, joined, prompts, t, grad, out, lse, tables, tiles, own, before=None, last=True):
    count = joined.shape[1]
    head_width = joined.shape[2] // 3
    pairs = head_width // 128
    first = before is None
    part = 256 * len(tiles)

    def half_spec(offset):
        return pl.BlockSpec((1, count, 128), lambda h, s: (t, 0, offset + h))

    def part_spec(offset):
        return pl.BlockSpec((1, part, 128), lambda h, s: (t, tiles[0] * 256 // part, offset + h))

    rows_spec = pl.BlockSpec((count, 128), lambda h, s: (0, h))
    whole = pl.BlockSpec((count, 128), lambda h, s: (0, 0))
    args = [joined, grad, out, lse]
    specs = [
        half_spec(0),
        rows_spec,
        rows_spec,
        pl.BlockSpec((1, 2, count), lambda h, s: (h, 0, 0)),
    ]
    outs = [jax.ShapeDtypeStruct((count, head_width), bf16 if last else f32)]
    out_specs = [rows_spec]
    if tiles:
        args += [prompts, prompts, tables[2], tables[3]]
        part_table = pl.BlockSpec((part, 128), lambda h, s: (tiles[0] * 256 // part, 0))
        specs += [part_spec(0), part_spec(pairs), part_table, part_table]
        outs += [jax.ShapeDtypeStruct((part, head_width), bf16)] * 2
        out_specs += [pl.BlockSpec((part, 128), lambda h, s: (0, h))] * 2
    if own:
        args += [joined, joined]
        specs += [half_spec(pairs), half_spec(2 * pairs)]
        outs += [jax.ShapeDtypeStruct((count, head_width), bf16)] * 2
        out_specs += [rows_spec] * 2
    if own or last:
        args += [tables[0], tables[1]]
        specs += [whole, whole]
    if not first:
        args += [before]
        specs += [rows_spec]
    return pl.pallas_call(
        lambda *refs: backward_kernel(first, last, tiles, own, *refs),
        grid_spec=pltpu.PrefetchScalarGridSpec(
            num_scalar_prefetch=1,
            grid=(pairs,),
            in_specs=specs,
            out_specs=out_specs,
            scratch_shapes=[pltpu.VMEM((count, 128), f32)],
        ),
        out_shape=outs,
        compiler_params=pltpu.CompilerParams(vmem_limit_bytes=20 * 2**20),
        cost_estimate=LONG,
        name="attend_back",
    )(info, *args)


def split_three(values):
    high = lax.reduce_precision(values, 8, 7)
    rest = values - high
    mid = lax.reduce_precision(rest, 8, 7)
    return high, mid, rest - mid


def pick(x, index, axis):
    return lax.dynamic_index_in_dim(x, index, axis, keepdims=False)


def body(
    block_input,
    cotangent,
    w_qkv,
    w_out,
    w_up,
    w_down,
    w_mod,
    time_table,
    prompt_len,
    cont_len,
    timestep,
):
    count, width = block_input.shape
    tiles = count // CONT
    dp_count = lax.axis_size("dp")
    tensor_count = lax.axis_size("tensor")
    devices = dp_count * tensor_count
    role = lax.axis_index("tensor")
    is_prompt = role == 0
    me = lax.axis_index("dp")
    core, near, far = me % 2, (me // 2) % 2, me // 4
    fars = far_count()
    low_bits = far_bits()
    high_bits = list(reversed(low_bits))
    head_width = w_qkv.shape[2]
    half = count // 2

    def far_bit(bit):
        return (far // bit) % 2

    far_top, far_rest = high_bits[0], high_bits[1:]
    cuts = (head_width, w_up.shape[1], w_down.shape[0])
    table_rows, rows_each = time_table.shape[0], w_qkv.shape[0]
    steps = jnp.pad(timestep.reshape(1, -1), ((0, rows_each - 1), (0, 128 - SEGS))).astype(bf16)
    table_width = table_rows * width // rows_each
    table_width += -table_width % 128
    table_part = time_table.reshape(-1)
    table_part = jnp.pad(table_part, (0, rows_each * table_width - table_part.shape[0]))
    table_part = table_part.reshape(rows_each, table_width)
    first = [w_qkv.reshape(rows_each, -1), table_part, steps]
    first_cuts = (first[0].shape[1], table_width + 128)
    first = jnp.concatenate(first, 1)[None]
    bounds = [0, count // 4, count * 5 // 8, count]
    x_parts = [block_input[bounds[n] : bounds[n + 1]] for n in range(3)]
    rest = jnp.concatenate([w_out.T, w_up, w_down.T], 1)[None]
    came_first = swap(first, 8 * far_top)
    first, came_first, x_parts, rest = tie(first, came_first, x_parts, rest)
    came = [swap(x_parts[0], TENSOR)]
    for bit in far_rest:
        first = join(first, came_first, far_bit(2 * bit))
        came_first = swap(first, 8 * bit)
    came_first, first, came, rest = tie(came_first, first, came, rest)
    qkv_far, table_far = join(first, came_first, far_bit(1), first_cuts)

    table_near = [swap(table_far, bits) for bits in (NEAR, TENSOR, NEAR + TENSOR)]
    qkv_near = [swap(qkv_far, bits) for bits in (NEAR, TENSOR)]
    table_own = join(table_far, table_near[0], near)
    table_other = join(table_near[1], table_near[2], near)
    table_came = [swap(table_own, CORE), swap(table_other, CORE)]
    table_cuts = (table_width, 128)
    packets = [
        join(table_own, table_came[0], core, table_cuts),
        join(table_other, table_came[1], core, table_cuts),
    ]
    rest_came = swap(rest, 8 * far_top)

    turns = HEAD_DIM // 2
    freqs = 10000.0 ** (-(jnp.arange(128, dtype=jnp.int32) % turns).astype(f32) / turns)
    inside = jnp.arange(count, dtype=jnp.int32)
    prompt_count = prompt_len[0]
    own_places = jnp.where(is_prompt, inside, prompt_count + inside % CONT).astype(f32)
    own_angles = own_places[:, None] * freqs[None, :]
    prompt_angles = inside.astype(f32)[:, None] * freqs[None, :]
    tables = (jnp.cos(own_angles), jnp.sin(own_angles), jnp.cos(prompt_angles), jnp.sin(prompt_angles))
    own_len = jnp.where(
        is_prompt,
        jnp.clip(prompt_count - CONT * jnp.arange(NCONT, dtype=jnp.int32), 0, CONT),
        cont_len[0],
    )
    info = jnp.concatenate(
        [jnp.stack([role, prompt_count]), own_len, jnp.stack([core, near, far])]
    ).astype(jnp.int32)

    table_full = jnp.concatenate([packets[0][0], packets[1][0]], 0)
    table_full = table_full.reshape(2 * dp_count, -1)[:, : table_rows * width]
    table_full = table_full.reshape(STEPS, width)
    step_rows = packets[0][1][:, 0, :SEGS].astype(jnp.int32)
    row_ids = (jnp.arange(2)[:, None, None] + role) % 2 * table_rows + (
        jnp.arange(dp_count)[None, :, None] * 2 * table_rows + jnp.arange(table_rows)
    )
    row_ids = row_ids.reshape(-1).astype(jnp.int32)
    step_pad = jnp.pad(step_rows, ((0, 0), (0, 16 - SEGS))).reshape(-1)
    chosen = (step_pad[:, None] == row_ids[None, :]).astype(bf16)
    cond = dot(chosen, table_full).astype(bf16)
    col_width = w_mod.shape[1]
    col_part = dot(cond, w_mod).reshape(dp_count, 1, 16, col_width)
    col_part = jnp.broadcast_to(col_part, (dp_count, tensor_count, 16, col_width))
    col_part = col_part.reshape(devices, 16, col_width).astype(f32)
    arrived = lax.all_to_all(col_part, BOTH, 0, 0, tiled=True)
    qkv_far, qkv_near, rest, rest_came, tables, info, _ = tie(
        qkv_far, qkv_near, rest, rest_came, tables, info, col_part
    )
    qkv_near.append(swap(qkv_far, NEAR + TENSOR))
    rest = join(rest, rest_came, far_bit(far_top), None if far_rest else cuts)
    if far_rest:
        rest_came = swap(rest, 8 * far_rest[0])

    qkv_far, qkv_near, arrived, came, x_parts = tie(qkv_far, qkv_near, arrived, came, x_parts)
    mods = jnp.transpose(arrived, (1, 0, 2)).reshape(16, 6 * width)
    came.append(swap(x_parts[1], TENSOR))
    qkv_own = join(qkv_far, qkv_near[0], near)
    qkv_other = join(qkv_near[1], qkv_near[2], near)
    qkv_came = [swap(qkv_own, CORE), swap(qkv_other, CORE)]
    for bit in far_rest[1:]:
        rest = join(rest, rest_came, far_bit(bit * 2))
        rest_came = swap(rest, 8 * bit)
    qkv = [
        join(own, other, core).reshape(width, -1)
        for own, other in zip((qkv_own, qkv_other), qkv_came)
    ]
    rest, rest_came, mods, qkv, came, x_parts = tie(rest, rest_came, mods, qkv, came, x_parts)

    def both_cores(own, came):
        return [own, came] if rows_each % 16 == 0 else [join(own, came, core).reshape(width, -1)]

    came.append(swap(x_parts[2], TENSOR))
    o_own, u_own, d_own = join(rest, rest_came, far_bit(1), cuts) if far_rest else rest
    u_near, o_near, o_other = swap(u_own, NEAR), swap(o_own, NEAR), swap(o_own, TENSOR)
    joined, normed = project(
        project_own_kernel, 3, LONG, info, [block_input], mods, qkv, tables[:2]
    )
    came, joined, u_near = tie(came, joined, u_near)
    prompts, prompt_normed = project(
        project_prompt_kernel, 2, LONG, info, [block_input, *came], mods, qkv, tables[2:]
    )
    u_near, o_near, o_other, u_own, o_own, d_own, prompts = tie(
        u_near, o_near, o_other, u_own, o_own, d_own, prompts
    )
    d_near, u_other, oo_near = swap(d_own, NEAR), swap(u_own, TENSOR), swap(o_other, NEAR)
    u_own, o_own = join(u_own, u_near, near), join(o_own, o_near, near)
    u_core = swap(u_own, CORE)
    out_0, lse_0 = attend(info, *tie(joined, prompts, u_own, o_own)[:2], 0)
    d_near, u_other, oo_near, u_core, d_own, u_own, o_own, o_other, out_0, joined = tie(
        d_near, u_other, oo_near, u_core, d_own, u_own, o_own, o_other, out_0, joined
    )
    d_other, uu_near = swap(d_own, TENSOR), swap(u_other, NEAR)
    d_own, o_other = join(d_own, d_near, near), join(o_other, oo_near, near)
    d_core, o_core, oo_core = swap(d_own, CORE), swap(o_own, CORE), swap(o_other, CORE)
    up_0 = both_cores(u_own, u_core)
    out_1, lse_1 = attend(info, *tie(joined, prompts, d_own, o_other, up_0)[:2], 1)
    d_other, uu_near, d_core, o_core, oo_core, d_own, o_own, o_other, u_other, out_1 = tie(
        d_other, uu_near, d_core, o_core, oo_core, d_own, o_own, o_other, u_other, out_1
    )
    attended, lses = [out_0, out_1], [lse_0, lse_1]
    out_t = [
        join(o_own, o_core, core).reshape(width, -1),
        join(o_other, oo_core, core).reshape(width, -1),
    ]
    branch, middle, normed_two = middle_norm(info, block_input, attended, mods, out_t)

    dd_near = swap(d_other, NEAR)
    u_other = join(u_other, uu_near, near)
    uu_core = swap(u_other, CORE)
    down_0 = both_cores(d_own, d_core)
    d_other, u_other, normed_two, down_0 = tie(d_other, u_other, normed_two, down_0)
    mlp, n2_grad, d_keep_0, d_send_0, u_keep_0, u_send_0, *shared = feed_forward(
        info, normed_two, (cotangent, mods), up_0 + down_0
    )
    dd_near, uu_core, d_other, u_other, mlp, d_send_0, u_send_0 = tie(
        dd_near, uu_core, d_other, u_other, mlp, d_send_0, u_send_0
    )
    d_other = join(d_other, dd_near, near)
    dd_core = swap(d_other, CORE)
    up_1 = both_cores(u_other, uu_core)
    down_1 = both_cores(d_other, dd_core)
    up_1, down_1, mlp, d_send_0, u_send_0 = tie(up_1, down_1, mlp, d_send_0, u_send_0)
    d_came_0, u_came_0 = swap(d_send_0, CORE), swap(u_send_0, CORE)
    mlp, n2_grad, d_keep_1, d_send_1, u_keep_1, u_send_1 = feed_forward(
        info, normed_two, (*shared, mlp, n2_grad), up_1 + down_1
    )
    d_came_0, u_came_0, mlp, d_send_1, u_send_1 = tie(d_came_0, u_came_0, mlp, d_send_1, u_send_1)
    d_came_1, u_came_1 = swap(d_send_1, CORE), swap(u_send_1, CORE)
    block_output, middle_grad, grad_0, grad_1, post_sums, o_keep, o_send = post(
        info, middle, branch, mlp, n2_grad, cotangent, attended, mods, out_t
    )
    d_came_1, u_came_1, o_keep, o_send, grad_0, grad_1 = tie(
        d_came_1, u_came_1, o_keep, o_send, grad_0, grad_1
    )

    def by_near(x):
        return x.reshape((2, 2, fars) + x.shape[2:])

    def near_part(keep, came, part):
        half_of = slice(part * fars, (part + 1) * fars)
        return plus(keep[half_of], came[half_of])

    o_came = swap(o_send, CORE)
    d_send = [near_part(d_keep_0, d_came_0, 1), near_part(d_keep_1, d_came_1, 1)]
    d_keep = [near_part(d_keep_0, d_came_0, 0), near_part(d_keep_1, d_came_1, 0)]
    u_send, u_keep = plus(u_keep_1, u_came_1), plus(u_keep_0, u_came_0)
    d_came, u_came = swap(jnp.stack(d_send), NEAR), swap(u_send, TENSOR)
    d_keep, u_keep, grad_1 = tie(d_keep, u_keep, grad_1)

    def back(t, grad, blocks, own, before=None, last=True):
        return attend_back(
            info, joined, prompts, t, grad, attended[t], lses[t], tables, blocks, own, before, last
        )

    def prompt_part(t, dkv):
        return dot(dkv, qkv[t][:, head_width:], NT)

    def weight_part(dqkv, dkv_prompt):
        whole = dot(normed, dqkv, TN)
        parts = [whole[:, :head_width], whole[:, head_width:] + dot(prompt_normed, dkv_prompt, TN)]
        whole = jnp.concatenate([part.astype(bf16) for part in parts], 1)
        return whole.reshape(fars, 2, 2, -1, whole.shape[1])

    dq_1, dkp_1, dvp_1, dk_1, dv_1 = back(1, grad_1, (0, 1, 2, 3), True)
    d_came, u_came, o_came, d_keep, u_keep, o_keep, grad_0, dq_1, dkp_1, dvp_1, dk_1, dv_1 = tie(
        d_came, u_came, o_came, d_keep, u_keep, o_keep, grad_0, dq_1, dkp_1, dvp_1, dk_1, dv_1
    )
    o_cur = by_near(plus(o_keep, o_came))
    d_keep, d_send = plus(d_keep[0], d_came[0]), plus(d_keep[1], d_came[1])
    u_keep, u_send = near_part(u_keep, u_came, 0), near_part(u_keep, u_came, 1)
    d_came, u_came = swap(d_send, TENSOR), swap(u_send, NEAR)
    o_came = swap(o_cur[:, 1], NEAR)
    o_keep = o_cur[:, 0]
    dqkv_1 = jnp.concatenate([dq_1, dk_1, dv_1], 1)
    dkvp_1 = jnp.concatenate([dkp_1, dvp_1], 1)
    q_cur = weight_part(dqkv_1, dkvp_1)
    q_came = swap(pick(q_cur, 1 - core, 2), CORE)
    q_keep = pick(q_cur, core, 2)
    prompt_sum = prompt_part(1, dkvp_1)
    q_keep, prompt_sum, grad_0, d_keep, u_keep, o_keep = tie(
        q_keep, prompt_sum, grad_0, d_keep, u_keep, o_keep
    )

    dq_0, dkp_a, dvp_a = back(0, grad_0, (0, 1), False, None, False)
    q_came, d_came, u_came, o_came, q_keep, d_keep, u_keep, o_keep, dq_0, dkp_a, dvp_a = tie(
        q_came, d_came, u_came, o_came, q_keep, d_keep, u_keep, o_keep, dq_0, dkp_a, dvp_a
    )
    dkvp_a = jnp.concatenate([dkp_a, dvp_a], 1)
    sum_a = prompt_sum[:half] + prompt_part(0, dkvp_a)
    came_a = swap(sum_a.astype(bf16), TENSOR)
    d_keep, d_send = send_far(plus(d_keep, d_came))
    u_keep, u_send = send_far(plus(u_keep, u_came))
    o_cur = plus(o_keep, o_came)
    q_cur = plus(q_keep, q_came)
    d_came, u_came = swap(d_send, 8), swap(u_send, 8)
    o_came, o_keep = swap(o_cur[1], TENSOR), o_cur[0]
    q_came, q_keep = swap(pick(q_cur, 1 - near, 1), NEAR), pick(q_cur, near, 1)
    sum_a, d_keep, u_keep, o_keep, q_keep, dq_0 = tie(sum_a, d_keep, u_keep, o_keep, q_keep, dq_0)

    dq_0, dkp_b, dvp_b = back(0, grad_0, (2, 3), False, dq_0, False)
    came, keep, grads = tie(
        (came_a, d_came, u_came, o_came, q_came),
        (d_keep, u_keep, o_keep, q_keep),
        (dkp_b, dvp_b, dq_0),
    )
    came_a, d_came, u_came, o_came, q_came = came
    d_keep, u_keep, o_keep, q_keep = keep
    dkp_b, dvp_b, dq_0 = grads
    dkvp_b = jnp.concatenate([dkp_b, dvp_b], 1)
    sum_b = prompt_sum[half:] + prompt_part(0, dkvp_b)
    came_b = swap(sum_b.astype(bf16), TENSOR)

    def far_end(keep, came):
        for bit in low_bits[1:]:
            keep, send = send_far(plus(keep, came))
            came = swap(send, 8 * bit)
        return keep, came

    d_keep, d_came = far_end(d_keep, d_came)
    u_keep, u_came = far_end(u_keep, u_came)
    o_keep, o_send = send_far(plus(o_keep, o_came))
    o_came = swap(o_send, 8)
    q_send = plus(q_keep, q_came)
    q_send, sum_b, dq_0 = tie(q_send, sum_b, dq_0)
    dq_0, dk_0, dv_0 = back(0, grad_0, (), True, dq_0, True)
    came, keep, grads = tie(
        (d_came, u_came, o_came), (d_keep, u_keep, o_keep), (dq_0, dk_0, dv_0, q_send)
    )
    d_came, u_came, o_came = came
    d_keep, u_keep, o_keep = keep
    dq_0, dk_0, dv_0, q_send = grads
    dqkv_0 = jnp.concatenate([dq_0, dk_0, dv_0], 1)
    q_cur = weight_part(dqkv_0, jnp.concatenate([dkvp_a, dkvp_b], 0))
    q_came, q_keep = swap(pick(q_cur, 1 - core, 2), CORE), pick(q_cur, core, 2)
    own_sum = dot(after(dqkv_1, dq_0), qkv[1], NT) + dot(dqkv_0, qkv[0], NT)
    q_came, q_keep, own_sum, q_send = tie(q_came, q_keep, own_sum, q_send)
    q_cur = plus(q_keep, q_came)
    q_came, q_keep = swap(pick(q_cur, 1 - near, 1), NEAR), pick(q_cur, near, 1)
    q_keep, own_sum, came_b, q_send = tie(q_keep, own_sum, came_b, q_send)
    q_other = swap(q_send, TENSOR)
    input_grad, last_sums = last(
        info,
        block_input,
        own_sum,
        jnp.concatenate([sum_a, sum_b], 0),
        jnp.concatenate([came_a, came_b], 0),
        middle_grad,
        mods,
    )
    last_sums, d_keep, u_keep, q_came, q_other, q_keep = tie(
        last_sums, d_keep, u_keep, q_came, q_other, q_keep
    )
    q_cur = q_keep.astype(f32) + q_came.astype(f32) + q_other.astype(f32)
    q_cur = q_cur.reshape((2,) * len(low_bits) + q_cur.shape[1:])

    def q_step(cur, bit):
        mine = (far // bit) % 2
        cur = cur.astype(bf16)
        return pick(cur, mine, cur.ndim - 3), swap(pick(cur, 1 - mine, cur.ndim - 3), 8 * bit)

    q_keep, q_came = q_step(q_cur, low_bits[0])
    down_grad = (d_keep.astype(f32) + d_came.astype(f32))[0]
    up_grad = (u_keep.astype(f32) + u_came.astype(f32))[0]
    o_keep, o_came = far_end(o_keep, o_came)
    out_grad = (o_keep.astype(f32) + o_came.astype(f32))[0]
    order = [last_sums[:, 0], last_sums[:, 1]] + [post_sums[:, n] for n in range(4)]
    sums = jnp.stack(order, 1).reshape(tiles, 6 * width)
    first_row = (jnp.arange(tiles) == 0)[:, None]
    prompt_sums = jnp.where(first_row, jnp.sum(sums, 0, keepdims=True), 0.0)
    segment_sums = jnp.where(is_prompt, prompt_sums, sums).astype(bf16)

    local = jnp.concatenate(
        [
            jnp.sum(post_sums[:, 4:7], (0, 2)),
            (jnp.sum(own_len) * width).astype(f32).reshape(1),
        ]
    )
    local = jnp.concatenate(split_three(local))
    local = jnp.pad(local, (0, col_width - 12)).astype(bf16)
    packet = segment_sums.reshape(tiles, devices, col_width).transpose(1, 0, 2)
    packet = jnp.concatenate(
        [packet, jnp.broadcast_to(local[None, None], (devices, 1, col_width))], 1
    )
    packet = jnp.pad(packet, ((0, 0), (0, 16 - packet.shape[1]), (0, 0)))
    packets = lax.all_to_all(packet, BOTH, 0, 0, tiled=True)
    packets, q_keep, q_came = tie(packets, q_keep, q_came)
    q_cur = q_keep.astype(f32) + q_came.astype(f32)
    for bit in low_bits[1:]:
        q_keep, q_came = q_step(q_cur, bit)
        q_cur = q_keep.astype(f32) + q_came.astype(f32)
    totals = jnp.sum(packets[:, tiles, :12].astype(f32), 0)
    totals = totals[:4] + totals[4:8] + totals[8:12]
    stats = jnp.sqrt(totals[:3] / totals[3])

    grads = packets[:, :tiles].reshape(devices * tiles, col_width)
    cond_groups = cond.reshape(dp_count, 16, width)
    own_steps = step_pad.reshape(dp_count, 16)
    cond_rows = jnp.stack([cond_groups[:, :tiles], cond_groups[:, 1 : 1 + tiles]], 1)
    step_slots = jnp.stack([own_steps[:, :tiles], own_steps[:, 1 : 1 + tiles]], 1).reshape(-1)
    mod_grad = dot(cond_rows.reshape(devices * tiles, width), grads, TN)
    condition_grad = dot(grads, w_mod, NT)
    slot_pick = (step_slots[:, None] == jnp.arange(STEPS, dtype=jnp.int32)[None, :]).astype(f32)
    table_part = lax.dot_general(
        slot_pick,
        condition_grad,
        TN,
        precision=lax.Precision.HIGHEST,
        preferred_element_type=f32,
    )
    table_pieces = lax.all_to_all(
        table_part.astype(bf16).reshape(devices, table_rows, width), BOTH, 0, 0, tiled=True
    )
    table_grad = jnp.sum(table_pieces.astype(f32), 0)
    return (
        block_output,
        input_grad,
        q_cur.reshape(w_qkv.shape),
        out_grad.T,
        up_grad,
        down_grad.T,
        mod_grad,
        table_grad,
        stats,
    )


def solution(mesh):
    return jax.shard_map(
        body,
        mesh=mesh,
        in_specs=(
            P(("dp", "tensor"), None),
            P(("dp", "tensor"), None),
            P("dp", None, "tensor"),
            P("tensor", "dp"),
            P("dp", "tensor"),
            P("tensor", "dp"),
            P(None, ("dp", "tensor")),
            P(("dp", "tensor"), None),
            P("dp"),
            P("dp", None),
            P("dp", None),
        ),
        out_specs=(
            P(("dp", "tensor"), None),
            P(("dp", "tensor"), None),
            P("dp", None, "tensor"),
            P("tensor", "dp"),
            P("dp", "tensor"),
            P("tensor", "dp"),
            P(None, ("dp", "tensor")),
            P(("dp", "tensor"), None),
            P(),
        ),
        check_vma=False,
    )
```

```python
import math

import jax
import jax.numpy as jnp
from jax import lax
from jax.experimental import pallas as pl
from jax.experimental.pallas import tpu as pltpu
from jax.sharding import PartitionSpec as P

HEAD_DIM = 64
PROMPT = 1024
CONT = 128
NCONT = 8
STEPS = 256
SEGS = 1 + NCONT

bf16 = jnp.bfloat16
f32 = jnp.float32
NN = (((1,), (0,)), ((), ()))
NT = (((1,), (1,)), ((), ()))
TN = (((0,), (0,)), ((), ()))
SCALE = HEAD_DIM ** (-0.5)
SCALE2 = SCALE * math.log2(math.e)
NEG = -1e30


def dot(left, right, dims=NN):
    return lax.dot_general(left, right, dims, preferred_element_type=f32)


def lanes(shape):
    return lax.broadcasted_iota(jnp.int32, shape, 1)


def rows(shape):
    return lax.broadcasted_iota(jnp.int32, shape, 0)


BOTH = ("dp", "tensor")
TENSOR, CORE, NEAR = 1, 2, 4
LONG = pl.CostEstimate(flops=10**11, bytes_accessed=1, transcendentals=0)


def swap(x, bits):
    count = lax.axis_size(BOTH)
    return lax.ppermute(x, BOTH, [(i, i ^ bits) for i in range(count)])


def tie(*arrays):
    return lax.optimization_barrier(arrays)


def after(array, *others):
    return lax.optimization_barrier((array,) + others)[0]


def far_count():
    return lax.axis_size("dp") // 4


def far_bits():
    return [1 << k for k in range(far_count().bit_length() - 1)]


def plus(left, right):
    return (left.astype(f32) + right.astype(f32)).astype(bf16)


def send_far(cur):
    cur = cur.reshape((-1, 2) + cur.shape[1:])
    return cur[:, 0], cur[:, 1]


def join_kernel(cuts, bit_ref, own_ref, came_ref, *out_refs):
    bit = bit_ref[0]
    start = 0
    for out_ref, cut in zip(out_refs, cuts):
        for n in range(own_ref.shape[0]):
            out_ref[n, bit] = own_ref[n, :, start : start + cut]
            out_ref[n, 1 - bit] = came_ref[n, :, start : start + cut]
        start += cut


def join(own, came, bit, cuts=None):
    count, rows_each, columns = own.shape
    sizes = cuts or (columns,)
    group = min(count, 2)
    spec = pl.BlockSpec((group, rows_each, columns), lambda n, s: (n, 0, 0))
    outs = pl.pallas_call(
        lambda *refs: join_kernel(sizes, *refs),
        grid_spec=pltpu.PrefetchScalarGridSpec(
            num_scalar_prefetch=1,
            grid=(count // group,),
            in_specs=[spec, spec],
            out_specs=[
                pl.BlockSpec((group, 2, rows_each, cut), lambda n, s: (n, 0, 0, 0)) for cut in sizes
            ],
        ),
        out_shape=[jax.ShapeDtypeStruct((count, 2, rows_each, cut), bf16) for cut in sizes],
        cost_estimate=pl.CostEstimate(flops=1, bytes_accessed=10**6, transcendentals=0),
        compiler_params=pltpu.CompilerParams(vmem_limit_bytes=16 * 2**20),
        name="join",
    )(bit.astype(jnp.int32).reshape(1), own, came)
    outs = [out.reshape(2 * count, rows_each, -1) for out in outs]
    return outs if cuts else outs[0]


def turn(x, cosine, sine):
    lane = lanes(x.shape) % 64
    swapped = jnp.where(lane < 32, -pltpu.roll(x, 96, 1), pltpu.roll(x, 32, 1))
    return x * cosine + swapped * sine


def turn_back(x, cosine, sine):
    lane = lanes(x.shape) % 64
    swapped = jnp.where(lane < 32, pltpu.roll(x, 96, 1), -pltpu.roll(x, 32, 1))
    return x * cosine + swapped * sine


def norm_parts(inputs):
    average = jnp.mean(inputs, -1, keepdims=True)
    centred = inputs - average
    spread = jnp.mean(centred * centred, -1, keepdims=True)
    inverse = lax.rsqrt(spread + 1e-05)
    return centred * inverse, inverse


def norm_back(unit, inverse, grad, scales):
    inner = grad * (1.0 + scales)
    first = jnp.mean(inner, -1, keepdims=True)
    second = jnp.mean(inner * unit, -1, keepdims=True)
    return inverse * (inner - first - unit * second)


def modulation(mods_ref, info, tile, part):
    segment = jnp.where(info[0] == 0, 0, 1 + tile)
    width = mods_ref.shape[1] // 6
    return mods_ref[pl.ds(segment, 1), part * width : (part + 1) * width]


def store_pieces(total, info, keep_ref, send_ref, lead):
    half, rows_each = keep_ref.shape[-3], keep_ref.shape[-2]
    fars = half // 2
    for k in range(half):
        low = total[2 * k * rows_each : (2 * k + 1) * rows_each]
        high = total[(2 * k + 1) * rows_each : (2 * k + 2) * rows_each]
        place = ((k % 2) ^ info[11]) * fars + ((k // 2) ^ info[12])
        keep_ref[lead + (place,)] = jnp.where(info[10] == 0, low, high).astype(bf16)
        send_ref[lead + (place,)] = jnp.where(info[10] == 0, high, low).astype(bf16)


def fill(source_ref, w_refs, out_ref, tables):
    for half, w_ref in enumerate(w_refs):
        pl.when(pl.program_id(0) == half)(lambda w_ref=w_ref: fill_half(source_ref, w_ref, out_ref, tables))


def fill_half(source_ref, w_ref, out_ref, tables):
    joined = dot(source_ref[...], w_ref[...])
    for c in range(joined.shape[1] // 128):
        cut = slice(c * 128, (c + 1) * 128)
        piece = joined[:, cut]
        if tables:
            piece = turn(piece, tables[0][...], tables[1][...])
        out_ref[0, :, cut] = piece.astype(bf16)


def project_own_kernel(info, x_ref, mods_ref, *refs):
    w_ref, (cos_ref, sin_ref, joined_ref, normed_ref) = refs[:2], refs[2:]
    half, part = pl.program_id(0), pl.program_id(1)

    @pl.when((half == 0) & (part == 0))
    def _():
        for i in range(x_ref.shape[0] // CONT):
            cut = slice(i * CONT, (i + 1) * CONT)
            unit, _ = norm_parts(x_ref[cut, :].astype(f32))
            shift, scale = (modulation(mods_ref, info, i, n) for n in range(2))
            normed_ref[cut, :] = (unit * (1.0 + scale) + shift).astype(bf16)

    pl.when(part < 2)(lambda: fill(normed_ref, w_ref, joined_ref, (cos_ref, sin_ref)))
    pl.when(part == 2)(lambda: fill(normed_ref, w_ref, joined_ref, None))


def project_prompt_kernel(info, x_ref, *refs):
    came_refs, (mods_ref, *w_ref, cos_ref, sin_ref, joined_ref, normed_ref) = refs[:-7], refs[-7:]
    half, part = pl.program_id(0), pl.program_id(1)
    width = x_ref.shape[1]

    @pl.when((half == 0) & (part == 0))
    def _():
        shift, scale = mods_ref[0:1, :width], mods_ref[0:1, width : 2 * width]
        for i in range(x_ref.shape[0] // CONT):
            cut = slice(i * CONT, (i + 1) * CONT)
            place = i * CONT
            for came_ref in came_refs:
                if 0 <= place < came_ref.shape[0]:
                    came = came_ref[place : place + CONT, :].astype(f32)
                place -= came_ref.shape[0]
            x = jnp.where(info[0] == 0, x_ref[cut, :].astype(f32), came)
            unit, _ = norm_parts(x)
            normed_ref[cut, :] = (unit * (1.0 + scale) + shift).astype(bf16)

    pl.when(part == 0)(lambda: fill(normed_ref, w_ref, joined_ref, (cos_ref, sin_ref)))
    pl.when(part == 1)(lambda: fill(normed_ref, w_ref, joined_ref, None))


def project(kernel, parts, estimate, info, inputs, mods, qkv, tables):
    count, width = inputs[0].shape
    head_width = qkv[0].shape[1] // 3

    def whole(array):
        return pl.BlockSpec(array.shape, lambda t, p, s: (0,) * array.ndim)

    def weight(half):
        def place(t, p, s):
            now = p + 3 - parts
            return (0, jnp.where(t == half, now, 2 if half == 0 else 3 - parts))

        return pl.BlockSpec((width, head_width), place)

    return pl.pallas_call(
        kernel,
        grid_spec=pltpu.PrefetchScalarGridSpec(
            num_scalar_prefetch=1,
            grid=(2, parts),
            in_specs=[whole(array) for array in inputs]
            + [whole(mods), weight(0), weight(1)]
            + [whole(table) for table in tables],
            out_specs=[
                pl.BlockSpec((1, count, head_width), lambda t, p, s: (t, 0, p)),
                whole(inputs[0]),
            ],
        ),
        out_shape=[
            jax.ShapeDtypeStruct((2, count, parts * head_width), bf16),
            jax.ShapeDtypeStruct((count, width), bf16),
        ],
        compiler_params=pltpu.CompilerParams(vmem_limit_bytes=20 * 2**20),
        cost_estimate=estimate,
        name="project",
    )(info, *inputs, mods, *qkv, *tables)


def middle_kernel(
    info, x_ref, a0_ref, a1_ref, mods_ref, o0_ref, o1_ref, branch_ref, middle_ref, n2_ref
):
    branch = dot(a0_ref[...], o0_ref[...], NT) + dot(a1_ref[...], o1_ref[...], NT)
    branch_ref[...] = branch
    per = x_ref.shape[0] // CONT
    for u in range(per):
        cut = slice(u * CONT, (u + 1) * CONT)
        gate, shift, scale = (
            modulation(mods_ref, info, pl.program_id(0) * per + u, n) for n in (2, 3, 4)
        )
        middle = x_ref[cut, :].astype(f32) + gate * branch[cut]
        middle_ref[cut, :] = middle
        unit, _ = norm_parts(middle)
        n2_ref[cut, :] = (unit * (1.0 + scale) + shift).astype(bf16)


def middle_norm(info, x, attended, mods, out_t):
    count, width = x.shape
    head_width = attended[0].shape[1]
    tile = 256
    by_row = pl.BlockSpec((tile, width), lambda i, s: (i, 0))
    by_head = pl.BlockSpec((tile, head_width), lambda i, s: (i, 0))
    return pl.pallas_call(
        middle_kernel,
        grid_spec=pltpu.PrefetchScalarGridSpec(
            num_scalar_prefetch=1,
            grid=(count // tile,),
            in_specs=[
                by_row,
                by_head,
                by_head,
                pl.BlockSpec(mods.shape, lambda i, s: (0, 0)),
                pl.BlockSpec((width, head_width), lambda i, s: (0, 0)),
                pl.BlockSpec((width, head_width), lambda i, s: (0, 0)),
            ],
            out_specs=[by_row] * 3,
        ),
        out_shape=[
            jax.ShapeDtypeStruct((count, width), f32),
            jax.ShapeDtypeStruct((count, width), f32),
            jax.ShapeDtypeStruct((count, width), bf16),
        ],
        compiler_params=pltpu.CompilerParams(vmem_limit_bytes=32 * 2**20),
        cost_estimate=LONG,
        name="middle_norm",
    )(info, x, *attended, mods, *out_t)


def mlp_kernel(first, whole_weights, info, n2_ref, *refs):
    if first:
        cot_ref, mods_ref = refs[:2]
        refs = refs[2:]
    else:
        n2_turned, out_grad, out_turned, branch_before, grad_before = refs[:5]
        refs = refs[5:]
    weight_refs, refs = refs[:whole_weights], refs[whole_weights:]
    branch_ref, grad_ref = refs[:2]
    down_keep_ref, down_send_ref, up_keep_ref, up_send_ref = refs[2:6]
    if first:
        n2_turned, out_grad, out_turned = refs[6:9]
    hidden, pre_grad, *joined = refs[-4:] if whole_weights == 4 else refs[-2:]
    count = n2_ref.shape[0]

    @pl.when(pl.program_id(0) == 0)
    def _():
        if first:
            for i in range(count // CONT):
                cut = slice(i * CONT, (i + 1) * CONT)
                gate = modulation(mods_ref, info, i, 5)
                out_grad[cut, :] = (cot_ref[cut, :].astype(f32) * gate).astype(bf16)
            n2_turned[...] = jnp.transpose(n2_ref[...])
            out_turned[...] = jnp.transpose(out_grad[...])
            branch_ref[...] = jnp.zeros_like(branch_ref)
            grad_ref[...] = jnp.zeros_like(grad_ref)
        else:
            branch_ref[...] = branch_before[...]
            grad_ref[...] = grad_before[...]

    if joined:
        for n, out_ref in enumerate(joined):
            own_ref, came_ref = weight_refs[2 * n : 2 * n + 2]
            rows_each = own_ref.shape[1]
            for k in range(own_ref.shape[0]):
                own, came = own_ref[k], came_ref[k]
                start = 2 * k * rows_each
                out_ref[start : start + rows_each, :] = jnp.where(info[10] == 0, own, came)
                start += rows_each
                out_ref[start : start + rows_each, :] = jnp.where(info[10] == 0, came, own)
        up, down = joined[0][...], joined[1][...]
    else:
        up, down = weight_refs[0][...], weight_refs[1][...]
    tile = 256
    for i in range(count // tile):
        cut = slice(i * tile, (i + 1) * tile)
        pre = dot(n2_ref[cut, :], up)
        cdf = 0.5 * (1.0 + lax.erf(pre * (2.0**-0.5)))
        pdf = jnp.exp(-0.5 * pre * pre) * ((2.0 * math.pi) ** -0.5)
        value = (pre * cdf).astype(bf16)
        hidden[cut, :] = value
        grad = (dot(out_grad[cut, :], down) * (cdf + pre * pdf)).astype(bf16)
        pre_grad[cut, :] = grad
        branch_ref[cut, :] += dot(value, down, NT)
        grad_ref[cut, :] += dot(grad, up, NT)
    store_pieces(dot(out_turned[...], hidden[...]), info, down_keep_ref, down_send_ref, ())
    store_pieces(dot(n2_turned[...], pre_grad[...]), info, up_keep_ref, up_send_ref, ())


def feed_forward(info, n2, sources, weights):
    count, width = n2.shape
    hidden_width = weights[0].shape[-1]
    first = len(sources) == 2
    cols = 384
    dp_count = lax.axis_size("dp")
    pieces = (dp_count // 2, width // dp_count, hidden_width)

    def whole(array):
        return pl.BlockSpec(
            array.shape, lambda b, s: (0,) * array.ndim, pipeline_mode=pl.Buffered(1)
        )

    piece_spec = pl.BlockSpec(pieces[:2] + (cols,), lambda b, s: (0, 0, b))
    weight_specs = [
        pl.BlockSpec(w.shape[:-1] + (cols,), lambda b, s, lead=w.ndim - 1: (0,) * lead + (b,))
        for w in weights
    ]
    scratch = [pltpu.VMEM((count, cols), bf16)] * 2
    if len(weights) == 4:
        scratch += [pltpu.VMEM((width, cols), bf16)] * 2
    outs = [jax.ShapeDtypeStruct((count, width), f32)] * 2 + [
        jax.ShapeDtypeStruct(pieces, bf16)
    ] * 4
    out_specs = [whole(n2)] * 2 + [piece_spec] * 4
    if first:
        shapes = [(width, count), (count, width), (width, count)]
        outs += [jax.ShapeDtypeStruct(shape, bf16) for shape in shapes]
        out_specs += [pl.BlockSpec(shape, lambda b, s: (0, 0)) for shape in shapes]
    return pl.pallas_call(
        lambda *refs: mlp_kernel(first, len(weights), *refs),
        grid_spec=pltpu.PrefetchScalarGridSpec(
            num_scalar_prefetch=1,
            grid=(hidden_width // cols,),
            in_specs=[whole(n2)] + [whole(array) for array in sources] + weight_specs,
            out_specs=out_specs,
            scratch_shapes=scratch,
        ),
        out_shape=outs,
        compiler_params=pltpu.CompilerParams(vmem_limit_bytes=52 * 2**20),
        cost_estimate=LONG,
        name="feed_forward",
    )(info, n2, *sources, *weights)


def post_kernel(
    info,
    middle_ref,
    branch_ref,
    mlp_ref,
    n2_grad_ref,
    cot_ref,
    a0_ref,
    a1_ref,
    mods_ref,
    o0_ref,
    o1_ref,
    out_ref,
    middle_grad_ref,
    g0_ref,
    g1_ref,
    sums_ref,
    keep_ref,
    send_ref,
    total,
    attn_grad,
):
    step = pl.program_id(0)
    per = middle_ref.shape[0] // CONT
    for u in range(per):
        cut = slice(u * CONT, (u + 1) * CONT)
        tile = step * per + u
        gate1, scale2, gate2 = (modulation(mods_ref, info, tile, n) for n in (2, 4, 5))
        middle, branch, mlp = middle_ref[cut, :], branch_ref[cut, :], mlp_ref[cut, :]
        n2_grad, upstream = n2_grad_ref[cut, :], cot_ref[cut, :].astype(f32)
        mlp_part, attn_part = gate2 * mlp, gate1 * branch
        result = middle + mlp_part
        out_ref[cut, :] = result.astype(bf16)
        unit, inverse = norm_parts(middle)
        middle_grad = upstream + norm_back(unit, inverse, n2_grad, scale2)
        middle_grad_ref[cut, :] = middle_grad
        attn_grad[cut, :] = (middle_grad * gate1).astype(bf16)
        valid = (rows((CONT, 1)) < info[2 + tile]).astype(f32)
        for n, value in enumerate(
            (
                middle_grad * branch,
                n2_grad,
                n2_grad * unit,
                upstream * mlp,
                valid * result * result,
                valid * attn_part * attn_part,
                valid * mlp_part * mlp_part,
            )
        ):
            sums_ref[u, n : n + 1, :] = jnp.sum(value, 0, keepdims=True)
        sums_ref[u, 7:8, :] = jnp.zeros_like(gate1)
    halves = ((a0_ref, g0_ref, o0_ref), (a1_ref, g1_ref, o1_ref))
    for t, (a_ref, g_ref, o_ref) in enumerate(halves):
        g_ref[...] = dot(attn_grad[...], o_ref[...]).astype(bf16)
        part = dot(attn_grad[...], a_ref[...], TN)
        total[t] = jnp.where(step == 0, part, total[t] + part)

    @pl.when(step == pl.num_programs(0) - 1)
    def _():
        for t in range(2):
            store_pieces(total[t], info, keep_ref, send_ref, (t,))


def post(info, middle, branch, mlp, n2_grad, cotangent, attended, mods, out_t):
    count, width = middle.shape
    head_width = attended[0].shape[1]
    tile = 256
    tiles = count // CONT
    dp_count = lax.axis_size("dp")
    pieces = (2, dp_count // 2, width // dp_count, head_width)
    by_row = pl.BlockSpec((tile, width), lambda i, s: (i, 0))
    by_head = pl.BlockSpec((tile, head_width), lambda i, s: (i, 0))
    return pl.pallas_call(
        post_kernel,
        grid_spec=pltpu.PrefetchScalarGridSpec(
            num_scalar_prefetch=1,
            grid=(count // tile,),
            in_specs=[by_row] * 5
            + [
                by_head,
                by_head,
                pl.BlockSpec(mods.shape, lambda i, s: (0, 0)),
                pl.BlockSpec((width, head_width), lambda i, s: (0, 0)),
                pl.BlockSpec((width, head_width), lambda i, s: (0, 0)),
            ],
            out_specs=[
                by_row,
                by_row,
                by_head,
                by_head,
                pl.BlockSpec((tile // CONT, 8, width), lambda i, s: (i, 0, 0)),
                pl.BlockSpec(pieces, lambda i, s: (0, 0, 0, 0)),
                pl.BlockSpec(pieces, lambda i, s: (0, 0, 0, 0)),
            ],
            scratch_shapes=[
                pltpu.VMEM((2, width, head_width), f32),
                pltpu.VMEM((tile, width), bf16),
            ],
        ),
        out_shape=[
            jax.ShapeDtypeStruct((count, width), bf16),
            jax.ShapeDtypeStruct((count, width), f32),
            jax.ShapeDtypeStruct((count, head_width), bf16),
            jax.ShapeDtypeStruct((count, head_width), bf16),
            jax.ShapeDtypeStruct((tiles, 8, width), f32),
            jax.ShapeDtypeStruct(pieces, bf16),
            jax.ShapeDtypeStruct(pieces, bf16),
        ],
        compiler_params=pltpu.CompilerParams(vmem_limit_bytes=48 * 2**20),
        cost_estimate=LONG,
        name="post",
    )(info, middle, branch, mlp, n2_grad, cotangent, *attended, mods, *out_t)


def last_kernel(
    info, x_ref, own_ref, prompt_ref, came_ref, middle_grad_ref, mods_ref, out_ref, sums_ref
):
    step = pl.program_id(0)
    per = x_ref.shape[0] // CONT
    for u in range(per):
        cut = slice(u * CONT, (u + 1) * CONT)
        scale = modulation(mods_ref, info, step * per + u, 1)
        prompt = prompt_ref[cut, :] + came_ref[cut, :].astype(f32)
        grad = own_ref[cut, :] + jnp.where(info[0] == 0, prompt, 0.0)
        unit, inverse = norm_parts(x_ref[cut, :].astype(f32))
        sums_ref[u, 0:1, :] = jnp.sum(grad, 0, keepdims=True)
        sums_ref[u, 1:2, :] = jnp.sum(grad * unit, 0, keepdims=True)
        sums_ref[u, 2:, :] = jnp.zeros((6, x_ref.shape[1]), f32)
        out_ref[cut, :] = middle_grad_ref[cut, :] + norm_back(unit, inverse, grad, scale)


def last(info, x, own_sum, prompt_sum, came, middle_grad, mods):
    count, width = x.shape
    tile = 256
    by_row = pl.BlockSpec((tile, width), lambda i, s: (i, 0))
    return pl.pallas_call(
        last_kernel,
        grid_spec=pltpu.PrefetchScalarGridSpec(
            num_scalar_prefetch=1,
            grid=(count // tile,),
            in_specs=[by_row] * 5 + [pl.BlockSpec(mods.shape, lambda i, s: (0, 0))],
            out_specs=[by_row, pl.BlockSpec((tile // CONT, 8, width), lambda i, s: (i, 0, 0))],
        ),
        out_shape=[
            jax.ShapeDtypeStruct((count, width), f32),
            jax.ShapeDtypeStruct((count // CONT, 8, width), f32),
        ],
        compiler_params=pltpu.CompilerParams(vmem_limit_bytes=16 * 2**20),
        cost_estimate=LONG,
        name="last",
    )(info, x, own_sum, prompt_sum, came, middle_grad, mods)


def forward_kernel(info, *refs):
    q_ref, kp_ref, vp_ref, ko_ref, vo_ref = (ref.at[0] for ref in refs[:5])
    o_ref, lse_ref = refs[5:]
    role = info[0]
    prompt_count = info[1]
    count = q_ref.shape[0]
    lane = lanes((count, 128))
    row = rows((count, 128))
    tile = 256
    blocks = count // tile

    def prepare(h):
        sel = (lane // 64) == h
        extra = 64 * (1 - h)
        q = jnp.where(sel, q_ref[...], jnp.where(lane == extra, 1.0, 0.0).astype(bf16))
        bias = jnp.where((lane == extra) & (row >= prompt_count), NEG, 0.0).astype(bf16)
        k = jnp.where(sel, kp_ref[...], bias)
        v = jnp.where(sel, vp_ref[...], jnp.ones((), bf16))
        return sel, q, k, v

    def finish(h, i, o, top):
        extra = 64 * (1 - h)
        weight = o[:, extra : extra + 1]
        lse = top * SCALE2 + jnp.log2(weight)
        turned = jnp.transpose(jnp.broadcast_to(lse, (tile, 128)))
        lse_ref[0, h : h + 1, i * tile : (i + 1) * tile] = turned[0:1, :]
        return o * (1.0 / weight)

    def store(outs):
        for i in range(blocks):
            merged = jnp.where(lanes((tile, 128)) < 64, outs[0][i], outs[1][i])
            o_ref[i * tile : (i + 1) * tile, :] = merged.astype(bf16)

    @pl.when(role == 0)
    def _():
        outs = []
        for h in range(2):
            sel, q, k, v = prepare(h)
            heads = []
            for i in range(blocks):
                start, stop = i * tile, (i + 1) * tile
                s = dot(q[start:stop], k[:stop], NT)
                near = jnp.where(lanes((tile, tile)) <= rows((tile, tile)), s[:, start:], NEG)
                top = jnp.max(near, 1, keepdims=True)
                if i:
                    top = jnp.maximum(top, jnp.max(s[:, :start], 1, keepdims=True))
                o = dot(jnp.exp2(near * SCALE2 - top * SCALE2).astype(bf16), v[start:stop])
                if i:
                    o = o + dot(
                        jnp.exp2(s[:, :start] * SCALE2 - top * SCALE2).astype(bf16), v[:start]
                    )
                heads.append(finish(h, i, o, top))
            outs.append(heads)
        store(outs)

    @pl.when(role != 0)
    def _():
        outs = []
        for h in range(2):
            sel, q, k, v = prepare(h)
            own_k = jnp.where(sel, ko_ref[...], jnp.zeros((), bf16))
            own_v = jnp.where(sel, vo_ref[...], jnp.ones((), bf16))
            heads, far, near, tops = [], [], [], []
            col, line = lanes((CONT, CONT)), rows((CONT, CONT))
            cuts = [slice(r, r + CONT) for r in range(0, count, CONT)]
            for n, cut in enumerate(cuts):
                fine = (col <= line) & (col < info[2 + n])
                near.append(jnp.where(fine, dot(q[cut], own_k[cut], NT), NEG))
            near = jnp.concatenate(near, 0)
            near_tops = jnp.max(near, 1, keepdims=True)
            for i in range(blocks):
                cut = slice(i * tile, (i + 1) * tile)
                s = dot(q[cut], k, NT)
                tops.append(jnp.maximum(jnp.max(s, 1, keepdims=True), near_tops[cut]))
                far.append(dot(jnp.exp2(s * SCALE2 - tops[i] * SCALE2).astype(bf16), v))
            weight = jnp.exp2(near * SCALE2 - jnp.concatenate(tops, 0) * SCALE2).astype(bf16)
            own = jnp.concatenate([dot(weight[cut], own_v[cut]) for cut in cuts], 0)
            for i in range(blocks):
                heads.append(finish(h, i, far[i] + own[i * tile : (i + 1) * tile], tops[i]))
            outs.append(heads)
        store(outs)


def attend(info, joined, prompts, t):
    count = joined.shape[1]
    head_width = joined.shape[2] // 3
    pairs = head_width // 128

    def spec(offset):
        return pl.BlockSpec((1, count, 128), lambda h, s: (t, 0, offset + h))

    return pl.pallas_call(
        forward_kernel,
        grid_spec=pltpu.PrefetchScalarGridSpec(
            num_scalar_prefetch=1,
            grid=(pairs,),
            in_specs=[spec(0), spec(0), spec(pairs), spec(pairs), spec(2 * pairs)],
            out_specs=[
                pl.BlockSpec((count, 128), lambda h, s: (0, h)),
                pl.BlockSpec((1, 2, count), lambda h, s: (h, 0, 0)),
            ],
        ),
        out_shape=[
            jax.ShapeDtypeStruct((count, head_width), bf16),
            jax.ShapeDtypeStruct((pairs, 2, count), f32),
        ],
        compiler_params=pltpu.CompilerParams(vmem_limit_bytes=20 * 2**20),
        cost_estimate=LONG,
        name="attend",
    )(info, joined, prompts, prompts, joined, joined)


def backward_kernel(first, last, tiles, own, info, *refs):
    refs = list(refs)
    q_ref, do_ref, o_ref, lse_ref = refs[0].at[0], *refs[1:4]
    del refs[:4]
    if tiles:
        kp_ref, vp_ref, cp_ref, sp_ref = refs[0].at[0], refs[1].at[0], *refs[2:4]
        del refs[:4]
    if own:
        ko_ref, vo_ref = refs[0].at[0], refs[1].at[0]
        del refs[:2]
    if own or last:
        co_ref, so_ref = refs[:2]
        del refs[:2]
    before_ref = None if first else refs.pop(0)
    dq_ref = refs.pop(0)
    if tiles:
        dkp_ref, dvp_ref = refs[:2]
        del refs[:2]
    if own:
        dko_ref, dvo_ref = refs[:2]
        del refs[:2]
    (dq_acc,) = refs
    role = info[0]
    prompt_count = info[1]
    count = q_ref.shape[0]
    tile = 256
    lane = lanes((count, 128))
    none = jnp.zeros((), bf16)
    products = jnp.transpose(do_ref[...].astype(f32) * o_ref[...].astype(f32))
    deltas = [jnp.sum(products[64 * h : 64 * h + 64], 0, keepdims=True) for h in range(2)]
    dq_acc[...] = jnp.zeros_like(dq_acc) if first else before_ref[...]

    def far_block(j, prompt):
        start, stop = j * tile, (j + 1) * tile
        cut = slice(start - tiles[0] * tile, stop - tiles[0] * tile)
        q_from = start if prompt else 0
        lane_k = lanes((tile, 128))
        row_k = rows((tile, 128)) + start
        key_parts, value_parts = [], []
        for h in range(2):
            extra = 64 * (1 - h)
            sel = (lane_k // 64) == h
            bias = jnp.where((lane_k == extra) & (row_k >= prompt_count), NEG, 0.0).astype(bf16)
            k = jnp.where(sel, kp_ref[cut, :], bias)
            k_plain = jnp.where(sel, kp_ref[cut, :], none)
            v = jnp.where(sel, vp_ref[cut, :], none)
            lane_q = lane[q_from:]
            ones = jnp.where(lane_q == extra, 1.0, 0.0).astype(bf16)
            q = jnp.where((lane_q // 64) == h, q_ref[q_from:, :], ones)
            s = dot(k, q, NT)
            if prompt:
                near = jnp.where(rows((tile, tile)) <= lanes((tile, tile)), s[:, :tile], NEG)
                s = jnp.concatenate([near, s[:, tile:]], 1) if stop < count else near
            weight = jnp.exp2(s * SCALE2 - lse_ref[0, h : h + 1, q_from:])
            grad = dot(v, do_ref[q_from:, :], NT)
            score = (weight * (grad - deltas[h][:, q_from:])).astype(bf16)
            value_parts.append(dot(weight.astype(bf16), do_ref[q_from:, :]))
            key_parts.append(dot(score, q_ref[q_from:, :]))
            dq_acc[q_from:, :] += dot(score, k_plain, TN)
        key_grad = jnp.where(lane_k < 64, key_parts[0], key_parts[1]) * SCALE
        value_grad = jnp.where(lane_k < 64, value_parts[0], value_parts[1])
        dkp_ref[cut, :] = turn_back(key_grad, cp_ref[cut, :], sp_ref[cut, :]).astype(bf16)
        dvp_ref[cut, :] = value_grad.astype(bf16)

    @pl.when(role == 0)
    def _():
        for j in tiles:
            far_block(j, True)
        if own:
            dko_ref[...] = jnp.zeros_like(dko_ref)
            dvo_ref[...] = jnp.zeros_like(dvo_ref)

    @pl.when(role != 0)
    def _():
        for j in tiles:
            far_block(j, False)
        lane_k = lanes((CONT, CONT))
        row_k = rows((CONT, CONT))
        every = range(count // CONT if own else 0)
        cuts = [slice(i * CONT, (i + 1) * CONT) for i in every]
        key_parts, value_parts = [], []
        for h in range(2 if own else 0):
            sel = (lane // 64) == h
            k = jnp.where(sel, ko_ref[...], none)
            v = jnp.where(sel, vo_ref[...], none)
            scores, weights = [], []
            for i, cut in enumerate(cuts):
                fine = (row_k <= lane_k) & (row_k < info[2 + i])
                scores.append(jnp.where(fine, dot(k[cut], q_ref[cut, :], NT), NEG) * SCALE2 - lse_ref[0, h : h + 1, cut])
            weight = jnp.exp2(jnp.concatenate(scores, 0))
            grad = jnp.concatenate([dot(v[cut], do_ref[cut, :], NT) - deltas[h][:, cut] for cut in cuts], 0)
            score = (weight * grad).astype(bf16)
            weight = weight.astype(bf16)
            value_parts.append([dot(weight[cut], do_ref[cut, :]) for cut in cuts])
            key_parts.append([dot(score[cut], q_ref[cut, :]) for cut in cuts])
            for cut in cuts:
                dq_acc[cut, :] += dot(score[cut], k[cut], TN)
        for i, cut in enumerate(cuts):
            key_grad = jnp.where(lane_k < 64, key_parts[0][i], key_parts[1][i]) * SCALE
            value_grad = jnp.where(lane_k < 64, value_parts[0][i], value_parts[1][i])
            dko_ref[cut, :] = turn_back(key_grad, co_ref[cut, :], so_ref[cut, :]).astype(bf16)
            dvo_ref[cut, :] = value_grad.astype(bf16)

    if last:
        dq_ref[...] = turn_back(dq_acc[...] * SCALE, co_ref[...], so_ref[...]).astype(bf16)
    else:
        dq_ref[...] = dq_acc[...]


def attend_back(info, joined, prompts, t, grad, out, lse, tables, tiles, own, before=None, last=True):
    count = joined.shape[1]
    head_width = joined.shape[2] // 3
    pairs = head_width // 128
    first = before is None
    part = 256 * len(tiles)

    def half_spec(offset):
        return pl.BlockSpec((1, count, 128), lambda h, s: (t, 0, offset + h))

    def part_spec(offset):
        return pl.BlockSpec((1, part, 128), lambda h, s: (t, tiles[0] * 256 // part, offset + h))

    rows_spec = pl.BlockSpec((count, 128), lambda h, s: (0, h))
    whole = pl.BlockSpec((count, 128), lambda h, s: (0, 0))
    args = [joined, grad, out, lse]
    specs = [
        half_spec(0),
        rows_spec,
        rows_spec,
        pl.BlockSpec((1, 2, count), lambda h, s: (h, 0, 0)),
    ]
    outs = [jax.ShapeDtypeStruct((count, head_width), bf16 if last else f32)]
    out_specs = [rows_spec]
    if tiles:
        args += [prompts, prompts, tables[2], tables[3]]
        part_table = pl.BlockSpec((part, 128), lambda h, s: (tiles[0] * 256 // part, 0))
        specs += [part_spec(0), part_spec(pairs), part_table, part_table]
        outs += [jax.ShapeDtypeStruct((part, head_width), bf16)] * 2
        out_specs += [pl.BlockSpec((part, 128), lambda h, s: (0, h))] * 2
    if own:
        args += [joined, joined]
        specs += [half_spec(pairs), half_spec(2 * pairs)]
        outs += [jax.ShapeDtypeStruct((count, head_width), bf16)] * 2
        out_specs += [rows_spec] * 2
    if own or last:
        args += [tables[0], tables[1]]
        specs += [whole, whole]
    if not first:
        args += [before]
        specs += [rows_spec]
    return pl.pallas_call(
        lambda *refs: backward_kernel(first, last, tiles, own, *refs),
        grid_spec=pltpu.PrefetchScalarGridSpec(
            num_scalar_prefetch=1,
            grid=(pairs,),
            in_specs=specs,
            out_specs=out_specs,
            scratch_shapes=[pltpu.VMEM((count, 128), f32)],
        ),
        out_shape=outs,
        compiler_params=pltpu.CompilerParams(vmem_limit_bytes=20 * 2**20),
        cost_estimate=LONG,
        name="attend_back",
    )(info, *args)


def split_three(values):
    high = lax.reduce_precision(values, 8, 7)
    rest = values - high
    mid = lax.reduce_precision(rest, 8, 7)
    return high, mid, rest - mid


def pick(x, index, axis):
    return lax.dynamic_index_in_dim(x, index, axis, keepdims=False)


def body(
    block_input,
    cotangent,
    w_qkv,
    w_out,
    w_up,
    w_down,
    w_mod,
    time_table,
    prompt_len,
    cont_len,
    timestep,
):
    count, width = block_input.shape
    tiles = count // CONT
    dp_count = lax.axis_size("dp")
    tensor_count = lax.axis_size("tensor")
    devices = dp_count * tensor_count
    role = lax.axis_index("tensor")
    is_prompt = role == 0
    me = lax.axis_index("dp")
    core, near, far = me % 2, (me // 2) % 2, me // 4
    fars = far_count()
    low_bits = far_bits()
    high_bits = list(reversed(low_bits))
    head_width = w_qkv.shape[2]
    half = count // 2

    def far_bit(bit):
        return (far // bit) % 2

    far_top, far_rest = high_bits[0], high_bits[1:]
    cuts = (head_width, w_up.shape[1], w_down.shape[0])
    table_rows, rows_each = time_table.shape[0], w_qkv.shape[0]
    steps = jnp.pad(timestep.reshape(1, -1), ((0, rows_each - 1), (0, 128 - SEGS))).astype(bf16)
    table_width = table_rows * width // rows_each
    table_width += -table_width % 128
    table_part = time_table.reshape(-1)
    table_part = jnp.pad(table_part, (0, rows_each * table_width - table_part.shape[0]))
    table_part = table_part.reshape(rows_each, table_width)
    first = [w_qkv.reshape(rows_each, -1), table_part, steps]
    first_cuts = (first[0].shape[1], table_width + 128)
    first = jnp.concatenate(first, 1)[None]
    bounds = [0, count // 4, count * 5 // 8, count]
    x_parts = [block_input[bounds[n] : bounds[n + 1]] for n in range(3)]
    rest = jnp.concatenate([w_out.T, w_up, w_down.T], 1)[None]
    came_first = swap(first, 8 * far_top)
    first, came_first, x_parts, rest = tie(first, came_first, x_parts, rest)
    came = [swap(x_parts[0], TENSOR)]
    for bit in far_rest:
        first = join(first, came_first, far_bit(2 * bit))
        came_first = swap(first, 8 * bit)
    came_first, first, came, rest = tie(came_first, first, came, rest)
    qkv_far, table_far = join(first, came_first, far_bit(1), first_cuts)

    table_near = [swap(table_far, bits) for bits in (NEAR, TENSOR, NEAR + TENSOR)]
    qkv_near = [swap(qkv_far, bits) for bits in (NEAR, TENSOR)]
    table_own = join(table_far, table_near[0], near)
    table_other = join(table_near[1], table_near[2], near)
    table_came = [swap(table_own, CORE), swap(table_other, CORE)]
    table_cuts = (table_width, 128)
    packets = [
        join(table_own, table_came[0], core, table_cuts),
        join(table_other, table_came[1], core, table_cuts),
    ]
    rest_came = swap(rest, 8 * far_top)

    turns = HEAD_DIM // 2
    freqs = 10000.0 ** (-(jnp.arange(128, dtype=jnp.int32) % turns).astype(f32) / turns)
    inside = jnp.arange(count, dtype=jnp.int32)
    prompt_count = prompt_len[0]
    own_places = jnp.where(is_prompt, inside, prompt_count + inside % CONT).astype(f32)
    own_angles = own_places[:, None] * freqs[None, :]
    prompt_angles = inside.astype(f32)[:, None] * freqs[None, :]
    tables = (jnp.cos(own_angles), jnp.sin(own_angles), jnp.cos(prompt_angles), jnp.sin(prompt_angles))
    own_len = jnp.where(
        is_prompt,
        jnp.clip(prompt_count - CONT * jnp.arange(NCONT, dtype=jnp.int32), 0, CONT),
        cont_len[0],
    )
    info = jnp.concatenate(
        [jnp.stack([role, prompt_count]), own_len, jnp.stack([core, near, far])]
    ).astype(jnp.int32)

    table_full = jnp.concatenate([packets[0][0], packets[1][0]], 0)
    table_full = table_full.reshape(2 * dp_count, -1)[:, : table_rows * width]
    table_full = table_full.reshape(STEPS, width)
    step_rows = packets[0][1][:, 0, :SEGS].astype(jnp.int32)
    row_ids = (jnp.arange(2)[:, None, None] + role) % 2 * table_rows + (
        jnp.arange(dp_count)[None, :, None] * 2 * table_rows + jnp.arange(table_rows)
    )
    row_ids = row_ids.reshape(-1).astype(jnp.int32)
    step_pad = jnp.pad(step_rows, ((0, 0), (0, 16 - SEGS))).reshape(-1)
    chosen = (step_pad[:, None] == row_ids[None, :]).astype(bf16)
    cond = dot(chosen, table_full).astype(bf16)
    col_width = w_mod.shape[1]
    col_part = dot(cond, w_mod).reshape(dp_count, 16, col_width)
    prompt_cols = jnp.pad(col_part[:, 0], ((0, 0), (0, -col_width % NCONT)))
    prompt_cols = prompt_cols.reshape(dp_count, NCONT, -1)
    col_part = jnp.concatenate([col_part[:, 1:SEGS], prompt_cols], 2)[:, None]
    col_part = jnp.broadcast_to(col_part, (dp_count, tensor_count) + col_part.shape[2:])
    col_part = col_part.reshape((devices,) + col_part.shape[2:])
    arrived = lax.all_to_all(col_part, BOTH, 0, 0, tiled=True)
    qkv_far, qkv_near, rest, rest_came, tables, info, _ = tie(
        qkv_far, qkv_near, rest, rest_came, tables, info, col_part
    )
    qkv_near.append(swap(qkv_far, NEAR + TENSOR))
    rest = join(rest, rest_came, far_bit(far_top), None if far_rest else cuts)
    if far_rest:
        rest_came = swap(rest, 8 * far_rest[0])

    qkv_far, qkv_near, arrived, came, x_parts = tie(qkv_far, qkv_near, arrived, came, x_parts)
    mods = jnp.transpose(arrived[..., :col_width], (1, 0, 2)).reshape(NCONT, 6 * width)
    prompt_cols = arrived[..., col_width:].reshape(devices, -1)[:, :col_width]
    mods = jnp.concatenate([prompt_cols.reshape(1, 6 * width), mods], 0)
    mods = jnp.pad(mods, ((0, 16 - SEGS), (0, 0)))
    came.append(swap(x_parts[1], TENSOR))
    qkv_own = join(qkv_far, qkv_near[0], near)
    qkv_other = join(qkv_near[1], qkv_near[2], near)
    qkv_came = [swap(qkv_own, CORE), swap(qkv_other, CORE)]
    for bit in far_rest[1:]:
        rest = join(rest, rest_came, far_bit(bit * 2))
        rest_came = swap(rest, 8 * bit)
    qkv = [
        join(own, other, core).reshape(width, -1)
        for own, other in zip((qkv_own, qkv_other), qkv_came)
    ]
    rest, rest_came, mods, qkv, came, x_parts = tie(rest, rest_came, mods, qkv, came, x_parts)

    def both_cores(own, came):
        return [own, came] if rows_each % 16 == 0 else [join(own, came, core).reshape(width, -1)]

    came.append(swap(x_parts[2], TENSOR))
    o_own, u_own, d_own = join(rest, rest_came, far_bit(1), cuts) if far_rest else rest
    u_near, o_near, o_other = swap(u_own, NEAR), swap(o_own, NEAR), swap(o_own, TENSOR)
    joined, normed = project(
        project_own_kernel, 3, LONG, info, [block_input], mods, qkv, tables[:2]
    )
    came, joined, u_near = tie(came, joined, u_near)
    prompts, prompt_normed = project(
        project_prompt_kernel, 2, LONG, info, [block_input, *came], mods, qkv, tables[2:]
    )
    u_near, o_near, o_other, u_own, o_own, d_own, prompts = tie(
        u_near, o_near, o_other, u_own, o_own, d_own, prompts
    )
    d_near, u_other, oo_near = swap(d_own, NEAR), swap(u_own, TENSOR), swap(o_other, NEAR)
    u_own, o_own = join(u_own, u_near, near), join(o_own, o_near, near)
    u_core = swap(u_own, CORE)
    out_0, lse_0 = attend(info, *tie(joined, prompts, u_own, o_own)[:2], 0)
    d_near, u_other, oo_near, u_core, d_own, u_own, o_own, o_other, out_0, joined = tie(
        d_near, u_other, oo_near, u_core, d_own, u_own, o_own, o_other, out_0, joined
    )
    d_other, uu_near = swap(d_own, TENSOR), swap(u_other, NEAR)
    d_own, o_other = join(d_own, d_near, near), join(o_other, oo_near, near)
    d_core, o_core, oo_core = swap(d_own, CORE), swap(o_own, CORE), swap(o_other, CORE)
    up_0 = both_cores(u_own, u_core)
    out_1, lse_1 = attend(info, *tie(joined, prompts, d_own, o_other, up_0)[:2], 1)
    d_other, uu_near, d_core, o_core, oo_core, d_own, o_own, o_other, u_other, out_1 = tie(
        d_other, uu_near, d_core, o_core, oo_core, d_own, o_own, o_other, u_other, out_1
    )
    attended, lses = [out_0, out_1], [lse_0, lse_1]
    out_t = [
        join(o_own, o_core, core).reshape(width, -1),
        join(o_other, oo_core, core).reshape(width, -1),
    ]
    branch, middle, normed_two = middle_norm(info, block_input, attended, mods, out_t)

    dd_near = swap(d_other, NEAR)
    u_other = join(u_other, uu_near, near)
    uu_core = swap(u_other, CORE)
    down_0 = both_cores(d_own, d_core)
    d_other, u_other, normed_two, down_0 = tie(d_other, u_other, normed_two, down_0)
    mlp, n2_grad, d_keep_0, d_send_0, u_keep_0, u_send_0, *shared = feed_forward(
        info, normed_two, (cotangent, mods), up_0 + down_0
    )
    dd_near, uu_core, d_other, u_other, mlp, d_send_0, u_send_0 = tie(
        dd_near, uu_core, d_other, u_other, mlp, d_send_0, u_send_0
    )
    d_other = join(d_other, dd_near, near)
    dd_core = swap(d_other, CORE)
    up_1 = both_cores(u_other, uu_core)
    down_1 = both_cores(d_other, dd_core)
    up_1, down_1, mlp, d_send_0, u_send_0 = tie(up_1, down_1, mlp, d_send_0, u_send_0)
    d_came_0, u_came_0 = swap(d_send_0, CORE), swap(u_send_0, CORE)
    mlp, n2_grad, d_keep_1, d_send_1, u_keep_1, u_send_1 = feed_forward(
        info, normed_two, (*shared, mlp, n2_grad), up_1 + down_1
    )
    d_came_0, u_came_0, mlp, d_send_1, u_send_1 = tie(d_came_0, u_came_0, mlp, d_send_1, u_send_1)
    d_came_1, u_came_1 = swap(d_send_1, CORE), swap(u_send_1, CORE)
    block_output, middle_grad, grad_0, grad_1, post_sums, o_keep, o_send = post(
        info, middle, branch, mlp, n2_grad, cotangent, attended, mods, out_t
    )
    d_came_1, u_came_1, o_keep, o_send, grad_0, grad_1 = tie(
        d_came_1, u_came_1, o_keep, o_send, grad_0, grad_1
    )

    def by_near(x):
        return x.reshape((2, 2, fars) + x.shape[2:])

    def near_part(keep, came, part):
        half_of = slice(part * fars, (part + 1) * fars)
        return plus(keep[half_of], came[half_of])

    o_came = swap(o_send, CORE)
    d_send = [near_part(d_keep_0, d_came_0, 1), near_part(d_keep_1, d_came_1, 1)]
    d_keep = [near_part(d_keep_0, d_came_0, 0), near_part(d_keep_1, d_came_1, 0)]
    u_send, u_keep = plus(u_keep_1, u_came_1), plus(u_keep_0, u_came_0)
    d_came, u_came = swap(jnp.stack(d_send), NEAR), swap(u_send, TENSOR)
    d_keep, u_keep, grad_1 = tie(d_keep, u_keep, grad_1)

    def back(t, grad, blocks, own, before=None, last=True):
        return attend_back(
            info, joined, prompts, t, grad, attended[t], lses[t], tables, blocks, own, before, last
        )

    def prompt_part(t, dkv):
        return dot(dkv, qkv[t][:, head_width:], NT)

    def weight_part(dqkv, dkv_prompt):
        whole = dot(normed, dqkv, TN)
        parts = [whole[:, :head_width], whole[:, head_width:] + dot(prompt_normed, dkv_prompt, TN)]
        whole = jnp.concatenate([part.astype(bf16) for part in parts], 1)
        return whole.reshape(fars, 2, 2, -1, whole.shape[1])

    dq_1, dkp_1, dvp_1, dk_1, dv_1 = back(1, grad_1, (0, 1, 2, 3), True)
    d_came, u_came, o_came, d_keep, u_keep, o_keep, grad_0, dq_1, dkp_1, dvp_1, dk_1, dv_1 = tie(
        d_came, u_came, o_came, d_keep, u_keep, o_keep, grad_0, dq_1, dkp_1, dvp_1, dk_1, dv_1
    )
    o_cur = by_near(plus(o_keep, o_came))
    d_keep, d_send = plus(d_keep[0], d_came[0]), plus(d_keep[1], d_came[1])
    u_keep, u_send = near_part(u_keep, u_came, 0), near_part(u_keep, u_came, 1)
    d_came, u_came = swap(d_send, TENSOR), swap(u_send, NEAR)
    o_came = swap(o_cur[:, 1], NEAR)
    o_keep = o_cur[:, 0]
    dqkv_1 = jnp.concatenate([dq_1, dk_1, dv_1], 1)
    dkvp_1 = jnp.concatenate([dkp_1, dvp_1], 1)
    q_cur = weight_part(dqkv_1, dkvp_1)
    q_came = swap(pick(q_cur, 1 - core, 2), CORE)
    q_keep = pick(q_cur, core, 2)
    prompt_sum = prompt_part(1, dkvp_1)
    q_keep, prompt_sum, grad_0, d_keep, u_keep, o_keep = tie(
        q_keep, prompt_sum, grad_0, d_keep, u_keep, o_keep
    )

    dq_0, dkp_a, dvp_a = back(0, grad_0, (0, 1), False, None, False)
    q_came, d_came, u_came, o_came, q_keep, d_keep, u_keep, o_keep, dq_0, dkp_a, dvp_a = tie(
        q_came, d_came, u_came, o_came, q_keep, d_keep, u_keep, o_keep, dq_0, dkp_a, dvp_a
    )
    dkvp_a = jnp.concatenate([dkp_a, dvp_a], 1)
    sum_a = prompt_sum[:half] + prompt_part(0, dkvp_a)
    came_a = swap(sum_a.astype(bf16), TENSOR)
    d_keep, d_send = send_far(plus(d_keep, d_came))
    u_keep, u_send = send_far(plus(u_keep, u_came))
    o_cur = plus(o_keep, o_came)
    q_cur = plus(q_keep, q_came)
    d_came, u_came = swap(d_send, 8), swap(u_send, 8)
    o_came, o_keep = swap(o_cur[1], TENSOR), o_cur[0]
    q_came, q_keep = swap(pick(q_cur, 1 - near, 1), NEAR), pick(q_cur, near, 1)
    sum_a, d_keep, u_keep, o_keep, q_keep, dq_0 = tie(sum_a, d_keep, u_keep, o_keep, q_keep, dq_0)

    dq_0, dkp_b, dvp_b = back(0, grad_0, (2, 3), False, dq_0, False)
    came, keep, grads = tie(
        (came_a, d_came, u_came, o_came, q_came),
        (d_keep, u_keep, o_keep, q_keep),
        (dkp_b, dvp_b, dq_0),
    )
    came_a, d_came, u_came, o_came, q_came = came
    d_keep, u_keep, o_keep, q_keep = keep
    dkp_b, dvp_b, dq_0 = grads
    dkvp_b = jnp.concatenate([dkp_b, dvp_b], 1)
    sum_b = prompt_sum[half:] + prompt_part(0, dkvp_b)
    came_b = swap(sum_b.astype(bf16), TENSOR)

    def far_end(keep, came):
        for bit in low_bits[1:]:
            keep, send = send_far(plus(keep, came))
            came = swap(send, 8 * bit)
        return keep, came

    d_keep, d_came = far_end(d_keep, d_came)
    u_keep, u_came = far_end(u_keep, u_came)
    o_keep, o_send = send_far(plus(o_keep, o_came))
    o_came = swap(o_send, 8)
    q_send = plus(q_keep, q_came)
    q_send, sum_b, dq_0 = tie(q_send, sum_b, dq_0)
    dq_0, dk_0, dv_0 = back(0, grad_0, (), True, dq_0, True)
    came, keep, grads = tie(
        (d_came, u_came, o_came), (d_keep, u_keep, o_keep), (dq_0, dk_0, dv_0, q_send)
    )
    d_came, u_came, o_came = came
    d_keep, u_keep, o_keep = keep
    dq_0, dk_0, dv_0, q_send = grads
    dqkv_0 = jnp.concatenate([dq_0, dk_0, dv_0], 1)
    q_cur = weight_part(dqkv_0, jnp.concatenate([dkvp_a, dkvp_b], 0))
    q_came, q_keep = swap(pick(q_cur, 1 - core, 2), CORE), pick(q_cur, core, 2)
    own_sum = dot(after(dqkv_1, dq_0), qkv[1], NT) + dot(dqkv_0, qkv[0], NT)
    q_came, q_keep, own_sum, q_send = tie(q_came, q_keep, own_sum, q_send)
    q_cur = plus(q_keep, q_came)
    q_came, q_keep = swap(pick(q_cur, 1 - near, 1), NEAR), pick(q_cur, near, 1)
    q_keep, own_sum, came_b, q_send = tie(q_keep, own_sum, came_b, q_send)
    q_other = swap(q_send, TENSOR)
    input_grad, last_sums = last(
        info,
        block_input,
        own_sum,
        jnp.concatenate([sum_a, sum_b], 0),
        jnp.concatenate([came_a, came_b], 0),
        middle_grad,
        mods,
    )
    last_sums, d_keep, u_keep, q_came, q_other, q_keep = tie(
        last_sums, d_keep, u_keep, q_came, q_other, q_keep
    )
    q_cur = q_keep.astype(f32) + q_came.astype(f32) + q_other.astype(f32)
    q_cur = q_cur.reshape((2,) * len(low_bits) + q_cur.shape[1:])

    def q_step(cur, bit):
        mine = (far // bit) % 2
        cur = cur.astype(bf16)
        return pick(cur, mine, cur.ndim - 3), swap(pick(cur, 1 - mine, cur.ndim - 3), 8 * bit)

    q_keep, q_came = q_step(q_cur, low_bits[0])
    down_grad = (d_keep.astype(f32) + d_came.astype(f32))[0]
    up_grad = (u_keep.astype(f32) + u_came.astype(f32))[0]
    o_keep, o_came = far_end(o_keep, o_came)
    out_grad = (o_keep.astype(f32) + o_came.astype(f32))[0]
    order = [last_sums[:, 0], last_sums[:, 1]] + [post_sums[:, n] for n in range(4)]
    sums = jnp.stack(order, 1).reshape(tiles, 6 * width)
    first_row = (jnp.arange(tiles) == 0)[:, None]
    prompt_sums = jnp.where(first_row, jnp.sum(sums, 0, keepdims=True), 0.0)
    segment_sums = jnp.where(is_prompt, prompt_sums, sums).astype(bf16)

    local = jnp.concatenate(
        [
            jnp.sum(post_sums[:, 4:7], (0, 2)),
            (jnp.sum(own_len) * width).astype(f32).reshape(1),
        ]
    )
    local = jnp.concatenate(split_three(local))
    local = jnp.pad(local, (0, col_width - 12)).astype(bf16)
    packet = segment_sums.reshape(tiles, devices, col_width).transpose(1, 0, 2)
    packet = jnp.concatenate(
        [packet, jnp.broadcast_to(local[None, None], (devices, 1, col_width))], 1
    )
    packet = jnp.pad(packet, ((0, 0), (0, 16 - packet.shape[1]), (0, 0)))
    packets = lax.all_to_all(packet, BOTH, 0, 0, tiled=True)
    packets, q_keep, q_came = tie(packets, q_keep, q_came)
    q_cur = q_keep.astype(f32) + q_came.astype(f32)
    for bit in low_bits[1:]:
        q_keep, q_came = q_step(q_cur, bit)
        q_cur = q_keep.astype(f32) + q_came.astype(f32)
    totals = jnp.sum(packets[:, tiles, :12].astype(f32), 0)
    totals = totals[:4] + totals[4:8] + totals[8:12]
    stats = jnp.sqrt(totals[:3] / totals[3])

    grads = packets[:, :tiles].reshape(devices * tiles, col_width)
    cond_groups = cond.reshape(dp_count, 16, width)
    own_steps = step_pad.reshape(dp_count, 16)
    cond_rows = jnp.stack([cond_groups[:, :tiles], cond_groups[:, 1 : 1 + tiles]], 1)
    step_slots = jnp.stack([own_steps[:, :tiles], own_steps[:, 1 : 1 + tiles]], 1).reshape(-1)
    mod_grad = dot(cond_rows.reshape(devices * tiles, width), grads, TN)
    condition_grad = dot(grads, w_mod, NT)
    slot_pick = (step_slots[:, None] == jnp.arange(STEPS, dtype=jnp.int32)[None, :]).astype(f32)
    table_part = lax.dot_general(
        slot_pick,
        condition_grad,
        TN,
        precision=lax.Precision.HIGHEST,
        preferred_element_type=f32,
    )
    table_pieces = lax.all_to_all(
        table_part.astype(bf16).reshape(devices, table_rows, width), BOTH, 0, 0, tiled=True
    )
    table_grad = jnp.sum(table_pieces.astype(f32), 0)
    return (
        block_output,
        input_grad,
        q_cur.reshape(w_qkv.shape),
        out_grad.T,
        up_grad,
        down_grad.T,
        mod_grad,
        table_grad,
        stats,
    )


def solution(mesh):
    return jax.shard_map(
        body,
        mesh=mesh,
        in_specs=(
            P(("dp", "tensor"), None),
            P(("dp", "tensor"), None),
            P("dp", None, "tensor"),
            P("tensor", "dp"),
            P("dp", "tensor"),
            P("tensor", "dp"),
            P(None, ("dp", "tensor")),
            P(("dp", "tensor"), None),
            P("dp"),
            P("dp", None),
            P("dp", None),
        ),
        out_specs=(
            P(("dp", "tensor"), None),
            P(("dp", "tensor"), None),
            P("dp", None, "tensor"),
            P("tensor", "dp"),
            P("dp", "tensor"),
            P("tensor", "dp"),
            P(None, ("dp", "tensor")),
            P(("dp", "tensor"), None),
            P(),
        ),
        check_vma=False,
    )
```
